256 devices in a mesh: grp: 4 (over y), own: 64 (over x, z, core).
Axes of the slice: x: 4, y: 4, z: 8, core: 2. Of those that a mesh axis runs over, the one named last changes fastest.
Arguments:
- grad_parts: bfloat16 [4, 64, 1024, 1024], P('grp', None, 'own'), may hold values from -6 to 6
- assign: int32 [64], replicated, may hold values from 0 to 63, each once
- block_bounds: int32 [64, 4], replicated, may hold values from 0 to 22016, as said below
- left_root: float32 [64, 1024, 1024], P('own', 'grp'), may hold values from -0.1875 to 0.1875
- right_root: float32 [64, 1024, 1024], P('own', 'grp'), may hold values from -0.1875 to 0.1875
- left_stat: float32 [64, 1024, 1024], P('own', 'grp'), may hold values from -6 to 6
- right_stat: float32 [64, 1024, 1024], P('own', 'grp'), may hold values from -6 to 6
- first_moment: float32 [64, 1024, 1024], P(None, 'own', 'grp'), may hold values from -3 to 3
- second_moment: float32 [64, 1024, 1024], P(None, 'own', 'grp'), may hold values from 1 to 8
Outputs:
- update: bfloat16 [64, 1024, 1024], P(None, 'own', 'grp')
- first_next: float32 [64, 1024, 1024], P(None, 'own', 'grp')
- second_next: float32 [64, 1024, 1024], P(None, 'own', 'grp')
- left_next: float32 [64, 1024, 1024], P('own', 'grp')
- right_next: float32 [64, 1024, 1024], P('own', 'grp')
The draws below stay inside these ranges and needn't reach their ends.
Inputs may be any that keep to these rules, and one draw needn't show every extreme that they name: `assign`: a permutation of 0 to 63. `block_bounds`: offsets are multiples of 1024 inside the matrix; the matrix is 8192 x 22016 or 22016 x 8192; block 0 sits at offsets 0, block 1 at the last column block of a 8192 x 22016 matrix.
All inputs are finite; a program needn't handle non-finite values.
Results may differ from the reference program's by a relative error of at most 0.015.
Values may be sent and summed in bfloat16 or wider, within the bound.
No kernel may reach another device: no remote copies, remote signals or barrier semaphores. Data moves between devices by JAX's collectives and lax.ppermute only.
A program may use at most 128 MiB of HBM per device.

```python
import math
import jax
import jax.numpy as jnp
from jax import lax

D = 8192
FF = 22016
BS = 1024
BLK_DEV = 1
NBLK = 64
N_GRP = 4
N_OWN = 64


def draw_block_bounds(key, part):
    key = jax.random.fold_in(key, 5)
    kind_key, short_key, long_key = jax.random.split(key, 3)
    short_count = (D + BS - 1) // BS
    long_count = (FF + BS - 1) // BS
    kinds = jax.random.randint(kind_key, (NBLK,), 0, 3)
    short_pick = jax.random.randint(short_key, (NBLK,), 0, short_count)
    long_pick = jax.random.randint(long_key, (NBLK,), 0, long_count)
    index = jnp.arange(NBLK)
    kinds = jnp.where(index < 2, 0, kinds)
    short_pick = jnp.where(index == 0, 0, short_pick)
    long_pick = jnp.where(index == 0, 0, jnp.where(index == 1, long_count - 1, long_pick))
    tall = kinds == 2
    row_off = BS * jnp.where(tall, long_pick, short_pick)
    col_off = BS * jnp.where(tall, short_pick, long_pick)
    n_rows = jnp.where(tall, FF, D)
    n_cols = jnp.where(tall, D, FF)
    return jnp.stack([row_off, col_off, n_rows, n_cols], axis=1).astype(jnp.int32)


def steps_of(rng, shape, pieces, low, high):
    gain, own = 1.0, jax.random.fold_in(rng, 6)
    for dim, shards_of in pieces:
        draws = jnp.exp(jax.random.uniform(jax.random.fold_in(own, dim), (shards_of,), jnp.float32, low / len(pieces), high / len(pieces)))
        gain = gain * jnp.repeat(draws, shape[dim] // shards_of).reshape([-1 if axis == dim else 1 for axis in range(len(shape))])
    return gain


def bell_draw(own_key, dims, spread, reach, shards=(), kind=jnp.bfloat16):
    loudness = steps_of(own_key, dims, shards, -0.22, 0.18) if shards else 1.0
    values = jax.random.normal(own_key, dims, jnp.float32) * spread * loudness
    return jnp.minimum(jnp.maximum(values, -reach), reach).astype(kind)


def setup_inputs(seed: int = 0) -> dict:
    key_of = jax.random.split(jax.random.key(seed), 10)
    return {
        "grad_parts": bell_draw(key_of[0], (N_GRP, NBLK, BS, BS), 1.0, 6.0, ((0, 4), (2, 64))),
        "assign": jax.random.permutation(key_of[1], NBLK).astype(jnp.int32),
        "block_bounds": draw_block_bounds(jax.random.fold_in(key_of[9], 71), 0),
        "left_root": bell_draw(key_of[3], (NBLK, BS, BS), BS ** -0.5, 0.1875, ((0, 64), (1, 4)), jnp.float32),
        "right_root": bell_draw(key_of[4], (NBLK, BS, BS), BS ** -0.5, 0.1875, ((0, 64), (1, 4)), jnp.float32),
        "left_stat": bell_draw(key_of[5], (NBLK, BS, BS), 1.0, 6.0, ((0, 64), (1, 4)), jnp.float32),
        "right_stat": bell_draw(key_of[6], (NBLK, BS, BS), 1.0, 6.0, ((0, 64), (1, 4)), jnp.float32),
        "first_moment": bell_draw(key_of[7], (NBLK, BS, BS), 0.5, 3.0, ((1, 64), (2, 4)), jnp.float32),
        "second_moment": jnp.clip(jnp.exp(math.log(8.0) - 2.0794415 * jax.random.uniform(key_of[8], (NBLK, BS, BS), jnp.float32) ** steps_of(key_of[8], (NBLK, BS, BS), ((1, 64), (2, 4)), -0.2, 0.2)), 1.0, 8.0),
    }


BETA_FIRST = 0.9
BETA_SECOND = 0.95
BIAS_FIRST = 1.0 - 0.9 ** 10
BIAS_SECOND = 1.0 - 0.95 ** 10
ADAM_EPS = 1e-08
STAT_DECAY = 0.95
NORM_EPS = 1e-06
HIGH = lax.Precision.HIGHEST

def block_mask(bounds, row_ids, col_ids):
    row_ok = bounds[:, 0:1] + row_ids[None, :] < bounds[:, 2:3]
    col_ok = bounds[:, 1:2] + col_ids[None, :] < bounds[:, 3:4]
    return (row_ok[:, :, None] & col_ok[:, None, :]).astype(jnp.float32)

def reference(grad_parts, assign, block_bounds, left_root, right_root, left_stat, right_stat, first_moment, second_moment):
    lines = jnp.arange(BS, dtype=jnp.int32)
    mask = block_mask(block_bounds, lines, lines)
    gradient = lax.optimization_barrier(jnp.sum(grad_parts.astype(jnp.float32), axis=0)) * mask
    first_next = BETA_FIRST * first_moment + (1.0 - BETA_FIRST) * gradient
    second_next = BETA_SECOND * second_moment + (1.0 - BETA_SECOND) * gradient * gradient
    adam = mask * (first_next / BIAS_FIRST) / (jnp.sqrt(second_next / BIAS_SECOND) + ADAM_EPS)
    adam_sq = lax.optimization_barrier(jnp.sum(adam * adam, axis=(1, 2)))
    key = (assign % N_OWN * BLK_DEV + assign // N_OWN).astype(jnp.int32)
    order = jnp.argsort(key).astype(jnp.int32)
    sorted_grad = gradient[order]

    def one_slot(slot):
        block = sorted_grad[slot]
        mixed = jnp.dot(left_root[slot], block, precision=HIGH, preferred_element_type=jnp.float32)
        precond = jnp.dot(mixed, right_root[slot], precision=HIGH, preferred_element_type=jnp.float32)
        left_new = STAT_DECAY * left_stat[slot] + jnp.dot(block, block.T, precision=HIGH, preferred_element_type=jnp.float32)
        right_new = STAT_DECAY * right_stat[slot] + jnp.dot(block.T, block, precision=HIGH, preferred_element_type=jnp.float32)
        return (precond, left_new, right_new)
    precond, left_next, right_next = lax.map(one_slot, jnp.arange(NBLK, dtype=jnp.int32))
    pre_sq = lax.optimization_barrier(jnp.sum(precond * precond, axis=(1, 2)))
    cells = float(BS * BS)
    scale = jnp.sqrt(adam_sq[order] / cells) / jnp.sqrt(pre_sq / cells + NORM_EPS)
    sorted_update = -scale[:, None, None] * precond * mask[order]
    update = sorted_update[key].astype(jnp.bfloat16)
    return (update, first_next, second_next, left_next, right_next)
```

```python
import jax
import jax.numpy as jnp
from jax import lax
from jax.sharding import PartitionSpec as P

BETA_FIRST = 0.9
BETA_SECOND = 0.95
BIAS_FIRST = 1.0 - 0.9**10
BIAS_SECOND = 1.0 - 0.95**10
ADAM_EPS = 1e-08
STAT_DECAY = 0.95
NORM_EPS = 1e-06
F32 = jnp.float32
BF16 = jnp.bfloat16


def block_mask(bounds, row_ids, col_ids):
    row_ok = bounds[:, 0:1] + row_ids[None, :] < bounds[:, 2:3]
    col_ok = bounds[:, 1:2] + col_ids[None, :] < bounds[:, 3:4]
    return (row_ok[:, :, None] & col_ok[:, None, :]).astype(F32)


def shift(array, step):
    n = lax.axis_size("grp")
    return lax.ppermute(array, "grp", [(i, (i + step) % n) for i in range(n)])


def grp_sum(array):
    return array + shift(array, 1) + shift(array, 2) + shift(array, 3)


def dot(a, b, dims):
    return lax.dot_general(a, b, (dims, ((), ())), preferred_element_type=F32)


def on_device(
    grad_parts,
    assign,
    block_bounds,
    left_root,
    right_root,
    left_stat,
    right_stat,
    first_moment,
    second_moment,
):
    n_own = lax.axis_size("own")
    n_grp = lax.axis_size("grp")
    own_index = lax.axis_index("own")
    grp_index = lax.axis_index("grp")
    total_blocks = assign.shape[0]
    per_owner = total_blocks // n_own
    shard_rows = grad_parts.shape[2]
    width = grad_parts.shape[3]
    quarter = width // n_grp
    half = total_blocks // 2
    part = grad_parts[0]

    def columns(array, step):
        start = (grp_index + step) % n_grp * quarter
        return lax.dynamic_slice_in_dim(array, start, quarter, array.ndim - 1)

    far = columns(part, 2)
    far_up = shift(far[:half], 1)
    far_down = shift(far[half:], -1)
    up = columns(part, 1)
    down = columns(part, 3)
    up_direct = shift(up[half:], 1)
    down_direct = shift(down[:half], -1)
    up_sum = shift((up[:half].astype(F32) + far_up.astype(F32)).astype(BF16), 1)
    down_sum = shift((down[half:].astype(F32) + far_down.astype(F32)).astype(BF16), -1)
    parts = (columns(part, 0), up_sum, up_direct, down_direct, down_sum)

    def total(parts):
        own, up_sum, up_direct, down_direct, down_sum = parts
        from_up = jnp.concatenate([up_sum, up_direct]).astype(F32)
        from_down = jnp.concatenate([down_direct, down_sum]).astype(F32)
        return own.astype(F32) + from_up + from_down

    row_ids = own_index * shard_rows + jnp.arange(shard_rows, dtype=jnp.int32)
    col_ids = grp_index * quarter + jnp.arange(quarter, dtype=jnp.int32)
    mask = block_mask(block_bounds, row_ids, col_ids)
    key = assign % n_own * per_owner + assign // n_own
    slots = jnp.arange(total_blocks, dtype=jnp.int32)
    order = jnp.sum(jnp.where(key[None, :] == slots[:, None], slots[None, :], 0), axis=1)
    sorted_grad = (total(parts) * mask).astype(BF16)[order]

    left_bf, right_bf = lax.optimization_barrier(
        (left_root[0].astype(BF16), right_root[0].astype(BF16))
    )
    left_bf, right_bf, _, _ = lax.optimization_barrier((left_bf, right_bf, up_sum, down_sum))
    sorted_grad, left_bf, right_bf = lax.optimization_barrier((sorted_grad, left_bf, right_bf))
    left_full = lax.all_gather(left_bf, "grp", axis=0, tiled=True)
    roots = [columns(right_bf, 0)] + [
        shift(columns(right_bf, step), step) for step in (3, 2, 1)
    ]
    right_cols = jnp.concatenate(roots, axis=0)

    own_cols = lax.all_to_all(sorted_grad, "own", split_axis=0, concat_axis=0, tiled=True)

    parts, _ = lax.optimization_barrier((parts, sorted_grad))
    gradient = total(parts) * mask
    first_next = BETA_FIRST * first_moment + (1.0 - BETA_FIRST) * gradient
    second_next = BETA_SECOND * second_moment + (1.0 - BETA_SECOND) * gradient * gradient
    adam = mask * (first_next / BIAS_FIRST) / (jnp.sqrt(second_next / BIAS_SECOND) + ADAM_EPS)
    adam_sq = jnp.sum(adam * adam, axis=(1, 2))
    adam_total = lax.psum(adam_sq, ("grp", "own"))

    low, high = own_cols[:half], own_cols[half:]
    prev_low = shift(low, 1)
    next_high = shift(high, -1)
    prev_high = shift(high, 1)
    next_low = shift(low, -1)
    far_low = shift(prev_low, 1)
    far_high = shift(next_high, -1)
    piece = jnp.concatenate(
        [
            own_cols,
            jnp.concatenate([next_low, next_high]),
            jnp.concatenate([far_low, far_high]),
            jnp.concatenate([prev_low, prev_high]),
        ],
        axis=2,
    ).reshape(width, width)

    mixed = dot(piece, right_cols, ((1,), (0,))).astype(BF16)
    precond = dot(left_full, mixed, ((1,), (0,)))
    pre_sq = jnp.sum(precond * precond).reshape(1)
    pre_total = grp_sum(pre_sq)
    adam_owned = lax.dynamic_slice_in_dim(adam_total[order], own_index * per_owner, per_owner, 0)
    cells = float(width * width)
    scale = jnp.sqrt(adam_owned / cells) / jnp.sqrt(pre_total / cells + NORM_EPS)
    grafted = (-scale * precond).astype(BF16).reshape(n_own, shard_rows, quarter)
    piece, own_cols, grafted = lax.optimization_barrier((piece, own_cols, grafted))
    back = lax.all_to_all(grafted, "own", split_axis=0, concat_axis=0, tiled=True)

    rows = lax.dynamic_slice_in_dim(piece, grp_index * quarter, quarter, 0)
    left_acc = STAT_DECAY * left_stat + dot(rows, piece, ((1,), (1,)))[None]
    cross = dot(own_cols.reshape(width, quarter), piece, ((0,), (0,)))
    cross = jnp.concatenate([cross, cross], axis=1)
    cross = lax.dynamic_slice_in_dim(cross, (n_grp - grp_index) % n_grp * quarter, width, 1)
    right_acc = STAT_DECAY * right_stat + cross[None]

    update = back[key] * mask.astype(BF16)
    return (update, first_next, second_next, left_acc, right_acc)


def solution(mesh):
    placed = (
        P("grp", None, "own", None),
        P(),
        P(),
        P("own", "grp", None),
        P("own", "grp", None),
        P("own", "grp", None),
        P("own", "grp", None),
        P(None, "own", "grp"),
        P(None, "own", "grp"),
    )
    return jax.shard_map(
        on_device,
        mesh=mesh,
        in_specs=placed,
        out_specs=(
            P(None, "own", "grp"),
            P(None, "own", "grp"),
            P(None, "own", "grp"),
            P("own", "grp", None),
            P("own", "grp", None),
        ),
        check_vma=False,
    )
```

```python
import functools

import jax
import jax.numpy as jnp
from jax import lax
from jax.experimental import pallas as pl
from jax.experimental.pallas import tpu as pltpu
from jax.sharding import PartitionSpec as P

BETA_FIRST = 0.9
BETA_SECOND = 0.95
BIAS_FIRST = 1.0 - 0.9**10
BIAS_SECOND = 1.0 - 0.95**10
ADAM_EPS = 1e-08
STAT_DECAY = 0.95
NORM_EPS = 1e-06
F32 = jnp.float32
BF16 = jnp.bfloat16
VMEM_LIMIT = 40 * 1024 * 1024
SMEM = pltpu.SMEM
VMEM = pltpu.VMEM


def block_mask(bounds, row_ids, col_ids):
    row_ok = bounds[:, 0:1] + row_ids[None, :] < bounds[:, 2:3]
    col_ok = bounds[:, 1:2] + col_ids[None, :] < bounds[:, 3:4]
    return (row_ok[:, :, None] & col_ok[:, None, :]).astype(F32)


def shift(array, step):
    n = lax.axis_size("grp")
    return lax.ppermute(array, "grp", [(i, (i + step) % n) for i in range(n)])


def dot(a, b, dims):
    return lax.dot_general(a, b, (dims, ((), ())), preferred_element_type=F32)


def pack_kernel(
    place, key, bounds, own, up_sum, up_direct, down_direct, down_sum, out
):
    blocks, rows, cols = out.shape
    half = blocks // 2
    row = lax.broadcasted_iota(jnp.int32, (rows, cols), 0) + place[1] * rows
    col = lax.broadcasted_iota(jnp.int32, (rows, cols), 1) + place[0] * cols

    def one(block, value):
        ok = (row < bounds[block, 2] - bounds[block, 0]) & (
            col < bounds[block, 3] - bounds[block, 1]
        )
        out[key[block]] = jnp.where(ok, value, 0.0).astype(BF16)

    def step(i, carry):
        low = own[0, i].astype(F32) + up_sum[i].astype(F32) + down_direct[i].astype(F32)
        one(i, low)
        j = i + half
        high = own[0, j].astype(F32) + up_direct[i].astype(F32) + down_sum[i].astype(F32)
        one(j, high)
        return carry

    lax.fori_loop(0, half, step, 0, unroll=4)


def pack(place, key, bounds, part, up_sum, up_direct, down_direct, down_sum):
    _, blocks, rows, width = part.shape
    cols = up_sum.shape[2]

    def whole(array):
        return pl.BlockSpec(array.shape, lambda i, *_: (0,) * array.ndim)

    return pl.pallas_call(
        pack_kernel,
        out_shape=jax.ShapeDtypeStruct((blocks, rows, cols), BF16),
        grid_spec=pltpu.PrefetchScalarGridSpec(
            num_scalar_prefetch=3,
            grid=(1,),
            in_specs=[
                pl.BlockSpec((1, blocks, rows, cols), lambda i, place, *_: (0, 0, 0, place[0])),
                whole(up_sum),
                whole(up_direct),
                whole(down_direct),
                whole(down_sum),
            ],
            out_specs=pl.BlockSpec((blocks, rows, cols), lambda i, *_: (0, 0, 0)),
        ),
        compiler_params=pltpu.CompilerParams(vmem_limit_bytes=VMEM_LIMIT),
    )(place, key, bounds, part, up_sum, up_direct, down_direct, down_sum)


def precond_kernel(
    place,
    own,
    next_low,
    next_high,
    far_low,
    far_high,
    prev_low,
    prev_high,
    root_own,
    root_next,
    root_far,
    root_prev,
    left_own,
    left_next,
    left_far_low,
    left_far_high,
    left_prev,
    adam,
    out,
    norms,
    mixed,
):
    width, quarter = out.shape
    half = width // 2
    me = place[0]
    n = width // quarter
    for top, parts in (
        (0, (own.at[pl.ds(0, half)], next_low, far_low, prev_low)),
        (half, (own.at[pl.ds(half, half)], next_high, far_high, prev_high)),
    ):
        for row in range(0, half, quarter):
            total = jnp.zeros((quarter, quarter), F32)
            for piece, root in zip(parts, (root_own, root_next, root_far, root_prev)):
                total += dot(piece[pl.ds(row, quarter), :], root[...], ((1,), (0,)))
            mixed[pl.ds(top + row, quarter), :] = total.astype(BF16)
    square = jnp.zeros((8, quarter), F32)
    eighth = quarter // 2
    for step, left, extra in (
        (0, left_own, 0),
        (1, left_next, 0),
        (2, left_far_low, 0),
        (2, left_far_high, eighth),
        (3, left_prev, 0),
    ):
        base = lax.rem(me + step, n) * quarter + extra
        rows = left.shape[0]
        value = dot(left[...], mixed[...], ((1,), (0,)))
        out[pl.ds(pl.multiple_of(base, eighth), rows), :] = value
        square += jnp.sum((value * value).reshape(rows // 8, 8, quarter), axis=0)
    norms[...] = jnp.zeros_like(norms)
    norms[0:1, :] = jnp.broadcast_to(jnp.sum(square), (1, 128))
    norms[1:2, :] = jnp.sum(adam[...], axis=0, keepdims=True)


def precondition(place, own, pieces, roots, lefts, adam):
    width, quarter = own.shape
    operands = (own, *pieces, *roots, *lefts, adam)
    return pl.pallas_call(
        precond_kernel,
        out_shape=(
            jax.ShapeDtypeStruct((width, quarter), F32),
            jax.ShapeDtypeStruct((8, 128), F32),
        ),
        in_specs=[pl.BlockSpec(memory_space=SMEM)]
        + [pl.BlockSpec(memory_space=VMEM)] * len(operands),
        out_specs=(pl.BlockSpec(memory_space=VMEM),) * 2,
        scratch_shapes=[VMEM((width, quarter), BF16)],
        compiler_params=pltpu.CompilerParams(vmem_limit_bytes=VMEM_LIMIT),
    )(place, *operands)


def graft_kernel(cells, precond, first, second, third, fourth, out):
    sums = first[...] + second[...] + third[...] + fourth[...]
    pre, adam = sums[0:1, :], sums[1:2, :]
    scale = -jnp.sqrt(adam / cells) / jnp.sqrt(pre / cells + NORM_EPS)
    width, quarter = out.shape
    scale = jnp.concatenate([scale] * (quarter // 128), axis=1)
    out[...] = (scale * precond[...]).astype(BF16)


def graft(precond, norms):
    width, quarter = precond.shape
    tiles = 4
    rows = width // tiles
    small = pl.BlockSpec((8, 128), lambda i: (0, 0))
    return pl.pallas_call(
        functools.partial(graft_kernel, float(width * width)),
        out_shape=jax.ShapeDtypeStruct((width, quarter), BF16),
        grid=(tiles,),
        in_specs=[pl.BlockSpec((rows, quarter), lambda i: (i, 0))] + [small] * 4,
        out_specs=pl.BlockSpec((rows, quarter), lambda i: (i, 0)),
        compiler_params=pltpu.CompilerParams(vmem_limit_bytes=VMEM_LIMIT),
    )(precond, *norms)


def on_device(
    grad_parts,
    assign,
    block_bounds,
    left_root,
    right_root,
    left_stat,
    right_stat,
    first_moment,
    second_moment,
):
    n_own = lax.axis_size("own")
    n_grp = lax.axis_size("grp")
    own_index = lax.axis_index("own")
    grp_index = lax.axis_index("grp")
    total_blocks = assign.shape[0]
    per_owner = total_blocks // n_own
    shard_rows = grad_parts.shape[2]
    width = grad_parts.shape[3]
    quarter = width // n_grp
    half = total_blocks // 2
    part = grad_parts[0]
    place = jnp.stack([grp_index, own_index]).astype(jnp.int32)

    def columns(array, step):
        start = (grp_index + step) % n_grp * quarter
        return lax.dynamic_slice_in_dim(array, start, quarter, array.ndim - 1)

    far = columns(part, 2)
    far_up = shift(far[:half], 1)
    far_down = shift(far[half:], -1)
    later, far_up, far_down = lax.optimization_barrier((part, far_up, far_down))
    up = columns(later, 1)
    down = columns(later, 3)
    up_direct = shift(up[half:], 1)
    down_direct = shift(down[:half], -1)
    up_sum = shift((up[:half].astype(F32) + far_up.astype(F32)).astype(BF16), 1)
    down_sum = shift((down[half:].astype(F32) + far_down.astype(F32)).astype(BF16), -1)

    key = (assign % n_own * per_owner + assign // n_own).astype(jnp.int32)
    slots = jnp.arange(total_blocks, dtype=jnp.int32)
    order = jnp.sum(jnp.where(key[None, :] == slots[:, None], slots[None, :], 0), axis=1)
    left_bf, right_bf = left_root[0].astype(BF16), right_root[0].astype(BF16)
    right_parts = [columns(right_bf, step) for step in range(4)]
    up_sum, up_direct, down_direct, down_sum, left_bf, right_parts = lax.optimization_barrier(
        (up_sum, up_direct, down_direct, down_sum, left_bf, right_parts)
    )

    sorted_grad = pack(
        place, key, block_bounds, grad_parts, up_sum, up_direct, down_direct, down_sum
    )
    own_cols = lax.all_to_all(sorted_grad, "own", split_axis=0, concat_axis=0, tiled=True)
    left_half = quarter // 2
    left_prev = shift(left_bf, 1)
    left_next = shift(left_bf, -1)
    left_far_low = shift(left_prev[:left_half], 1)
    left_far_high = shift(left_next[left_half:], -1)
    roots = [right_parts[0]] + [shift(right_parts[step], step) for step in (3, 2, 1)]
    lefts = [left_bf, left_next, left_far_low, left_far_high, left_prev]

    row_ids = own_index * shard_rows + jnp.arange(shard_rows, dtype=jnp.int32)
    col_ids = grp_index * quarter + jnp.arange(quarter, dtype=jnp.int32)
    mask = block_mask(block_bounds, row_ids, col_ids)
    up_sum, up_direct, down_direct, down_sum, later, _ = lax.optimization_barrier(
        (up_sum, up_direct, down_direct, down_sum, part, sorted_grad)
    )
    from_up = jnp.concatenate([up_sum, up_direct]).astype(F32)
    from_down = jnp.concatenate([down_direct, down_sum]).astype(F32)
    gradient = (columns(later, 0).astype(F32) + from_up + from_down) * mask
    first_next = BETA_FIRST * first_moment + (1.0 - BETA_FIRST) * gradient
    second_next = BETA_SECOND * second_moment + (1.0 - BETA_SECOND) * gradient * gradient
    adam = mask * (first_next / BIAS_FIRST) / (jnp.sqrt(second_next / BIAS_SECOND) + ADAM_EPS)
    adam_sq = jnp.sum(adam * adam, axis=(1, 2))

    own_cols, adam_sq, lefts, roots = lax.optimization_barrier((own_cols, adam_sq, lefts, roots))
    low, high = own_cols[:half], own_cols[half:]
    prev_low = shift(low, 1)
    next_high = shift(high, -1)
    prev_high = shift(high, 1)
    next_low = shift(low, -1)
    far_low = shift(prev_low, 1)
    far_high = shift(next_high, -1)
    pieces = [next_low, next_high, far_low, far_high, prev_low, prev_high]

    shares = jnp.broadcast_to(adam_sq[order][:, None, None], (n_own, 1, 128))
    shares = lax.all_to_all(shares, "own", split_axis=0, concat_axis=0, tiled=True)

    flat = [piece.reshape(width // 2, quarter) for piece in pieces]
    precond, norms = precondition(
        place, own_cols.reshape(width, quarter), flat, roots, lefts, shares.reshape(n_own, 128)
    )
    norms = [norms] + [shift(norms, step) for step in (1, 2, 3)]
    grafted = graft(precond, norms).reshape(n_own, shard_rows, quarter)
    pieces, own_cols, grafted = lax.optimization_barrier((pieces, own_cols, grafted))
    back = lax.all_to_all(grafted, "own", split_axis=0, concat_axis=0, tiled=True)

    whole = jnp.concatenate(
        [own_cols] + [jnp.concatenate(pieces[i : i + 2]) for i in (0, 2, 4)], axis=2
    ).reshape(width, width)
    rows = lax.dynamic_slice_in_dim(whole, grp_index * quarter, quarter, 0)
    left_acc = STAT_DECAY * left_stat + dot(rows, whole, ((1,), (1,)))[None]
    cross = dot(own_cols.reshape(width, quarter), whole, ((0,), (0,)))
    cross = jnp.concatenate([cross, cross], axis=1)
    cross = lax.dynamic_slice_in_dim(cross, (n_grp - grp_index) % n_grp * quarter, width, 1)
    right_acc = STAT_DECAY * right_stat + cross[None]

    update = back[key] * mask.astype(BF16)
    return (update, first_next, second_next, left_acc, right_acc)


def solution(mesh):
    placed = (
        P("grp", None, "own", None),
        P(),
        P(),
        P("own", "grp", None),
        P("own", "grp", None),
        P("own", "grp", None),
        P("own", "grp", None),
        P(None, "own", "grp"),
        P(None, "own", "grp"),
    )
    return jax.shard_map(
        on_device,
        mesh=mesh,
        in_specs=placed,
        out_specs=(
            P(None, "own", "grp"),
            P(None, "own", "grp"),
            P(None, "own", "grp"),
            P("own", "grp", None),
            P("own", "grp", None),
        ),
        check_vma=False,
    )
```

```python
import functools

import jax
import jax.numpy as jnp
from jax import lax
from jax.experimental import pallas as pl
from jax.experimental.pallas import tpu as pltpu
from jax.sharding import PartitionSpec as P

BETA_FIRST = 0.9
BETA_SECOND = 0.95
BIAS_FIRST = 1.0 - 0.9**10
BIAS_SECOND = 1.0 - 0.95**10
ADAM_EPS = 1e-08
STAT_DECAY = 0.95
NORM_EPS = 1e-06
F32 = jnp.float32
BF16 = jnp.bfloat16
MIB = 1024 * 1024
SMEM = pltpu.SMEM
VMEM = pltpu.VMEM


def shift(array, step):
    n = lax.axis_size("grp")
    return lax.ppermute(array, "grp", [(i, (i + step) % n) for i in range(n)])


def in_hbm(array):
    return pltpu.with_memory_space_constraint(array, pltpu.HBM)


def slice_at(array, start, size, axis):
    starts = [start if i == axis else 0 for i in range(array.ndim)]
    sizes = [size if i == axis else n for i, n in enumerate(array.shape)]
    return lax.dynamic_slice(array, starts, sizes, allow_negative_indices=False)


def dot(a, b, dims):
    return lax.dot_general(a, b, (dims, ((), ())), preferred_element_type=F32)


def inside(place, bounds, block, rows, cols):
    row = lax.broadcasted_iota(jnp.int32, (rows, cols), 0) + place[1] * rows
    col = lax.broadcasted_iota(jnp.int32, (rows, cols), 1) + place[0] * cols
    return (row < bounds[block, 2] - bounds[block, 0]) & (
        col < bounds[block, 3] - bounds[block, 1]
    )


def pack_kernel(
    place,
    key,
    bounds,
    own,
    up_sum,
    up_direct,
    down_direct,
    down_sum,
    first,
    second,
    out,
    first_out,
    second_out,
):
    _, count, rows, cols = own.shape
    half = out.shape[0] // 2
    begin = pl.program_id(0) * count
    lanes = 128

    def one(side, i, value):
        block = side * half + begin + i
        ok = inside(place, bounds, block, rows, cols)
        grad = jnp.where(ok, value, 0.0)
        first_next = BETA_FIRST * first[side, i] + (1.0 - BETA_FIRST) * grad
        second_next = BETA_SECOND * second[side, i] + (1.0 - BETA_SECOND) * grad * grad
        first_out[side, i] = first_next
        second_out[side, i] = second_next
        adam = (first_next / BIAS_FIRST) / (jnp.sqrt(second_next / BIAS_SECOND) + ADAM_EPS)
        square = jnp.where(ok, adam * adam, 0.0)
        square = square[:, :lanes] + square[:, lanes:]
        square = square[: rows // 2] + square[rows // 2 :]
        piece = jnp.concatenate([grad[:, :lanes], grad[:, lanes:], square], axis=0)
        out[key[block]] = piece.astype(BF16)

    def step(i, carry):
        low = own[0, i].astype(F32) + up_sum[i].astype(F32) + down_direct[i].astype(F32)
        one(0, i, low)
        high = own[1, i].astype(F32) + up_direct[i].astype(F32) + down_sum[i].astype(F32)
        one(1, i, high)
        return carry

    lax.fori_loop(0, count, step, 0, unroll=4)


def pack(place, key, bounds, part, sums, first, second):
    blocks, rows, width = part.shape
    cols = first.shape[2]
    half, steps = blocks // 2, 4 if blocks >= 32 else 1
    count = half // steps
    piece = 2 * rows + rows // 2
    moment = pl.BlockSpec((2, count, rows, cols), lambda i, *_: (0, i, 0, 0))
    halves = jax.ShapeDtypeStruct((2, half, rows, cols), F32)
    out, first_next, second_next = pl.pallas_call(
        pack_kernel,
        out_shape=(pltpu.HBM((blocks, piece, 128), BF16), halves, halves),
        grid_spec=pltpu.PrefetchScalarGridSpec(
            num_scalar_prefetch=3,
            grid=(steps,),
            in_specs=[
                pl.BlockSpec((2, count, rows, cols), lambda i, place, *_: (0, i, 0, place[0]))
            ]
            + [pl.BlockSpec((count, rows, cols), lambda i, *_: (i, 0, 0))] * 4
            + [moment] * 2,
            out_specs=[
                pl.BlockSpec((blocks, piece, 128), lambda i, *_: (0, 0, 0)),
                moment,
                moment,
            ],
        ),
        compiler_params=pltpu.CompilerParams(vmem_limit_bytes=10 * MIB),
    )(
        place,
        key,
        bounds,
        part.reshape(2, half, rows, width),
        *sums,
        in_hbm(first.reshape(halves.shape)),
        in_hbm(second.reshape(halves.shape)),
    )
    return out, first_next.reshape(first.shape), second_next.reshape(second.shape)


def finish_kernel(place, key, bounds, back, out):
    blocks, rows, cols = out.shape

    def step(block, carry):
        ok = inside(place, bounds, block, rows, cols)
        out[block] = jnp.where(ok, back[key[block]].astype(F32), 0.0).astype(BF16)
        return carry

    lax.fori_loop(0, blocks, step, 0, unroll=4)


def finish(place, key, bounds, back):
    whole = pl.BlockSpec(back.shape, lambda i, *_: (0, 0, 0))
    return pl.pallas_call(
        finish_kernel,
        out_shape=jax.ShapeDtypeStruct(back.shape, BF16),
        grid_spec=pltpu.PrefetchScalarGridSpec(
            num_scalar_prefetch=3, grid=(1,), in_specs=[whole], out_specs=whole
        ),
        compiler_params=pltpu.CompilerParams(vmem_limit_bytes=6 * MIB),
    )(place, key, bounds, back)


def precond_kernel(*refs):
    place, own_low, own_high, next_low, next_high, far_low, far_high, prev_low, prev_high = refs[:9]
    roots, lefts, (adam, out, norms, mixed) = refs[9:13], refs[13:20], refs[20:]
    width, quarter = out.shape
    half = width // 2
    me = place[0]
    n = width // quarter
    for top, parts in (
        (0, (own_low, next_low, far_low, prev_low)),
        (half, (own_high, next_high, far_high, prev_high)),
    ):
        for row in range(0, half, quarter):
            total = jnp.zeros((quarter, quarter), F32)
            for piece, root in zip(parts, roots):
                total += dot(piece[pl.ds(row, quarter), :], root[...], ((1,), (0,)))
            mixed[pl.ds(top + row, quarter), :] = total.astype(BF16)
    square = jnp.zeros((8, quarter), F32)
    eighth = quarter // 2
    places = ((0, 0), (1, 0), (1, eighth), (2, 0), (2, eighth), (3, 0), (3, eighth))
    for (step, extra), left in zip(places, lefts):
        base = lax.rem(me + step, n) * quarter + extra
        rows = left.shape[0]
        value = dot(left[...], mixed[...], ((1,), (0,)))
        out[pl.ds(pl.multiple_of(base, eighth), rows), :] = value
        square += jnp.sum((value * value).reshape(rows // 8, 8, quarter), axis=0)
    norms[...] = jnp.zeros_like(norms)
    norms[0:1, :] = jnp.broadcast_to(jnp.sum(square), (1, 128))
    norms[1:2, :] = jnp.broadcast_to(jnp.sum(adam[...].astype(F32)), (1, 128))


def precondition(place, pieces, roots, lefts, adam):
    rows, quarter = pieces[0].shape
    operands = (*pieces, *map(in_hbm, roots), *map(in_hbm, lefts), adam)
    return pl.pallas_call(
        precond_kernel,
        out_shape=(
            jax.ShapeDtypeStruct((2 * rows, quarter), F32),
            jax.ShapeDtypeStruct((8, 128), F32),
        ),
        in_specs=[pl.BlockSpec(memory_space=SMEM)]
        + [pl.BlockSpec(memory_space=VMEM)] * len(operands),
        out_specs=(pl.BlockSpec(memory_space=VMEM),) * 2,
        scratch_shapes=[VMEM((2 * rows, quarter), BF16)],
        compiler_params=pltpu.CompilerParams(vmem_limit_bytes=12 * MIB),
    )(place, *operands)


def graft_kernel(cells, precond, first, second, third, fourth, out):
    sums = first[...] + second[...] + third[...] + fourth[...]
    pre, adam = sums[0:1, :], sums[1:2, :]
    scale = -jnp.sqrt(adam / cells) / jnp.sqrt(pre / cells + NORM_EPS)
    width, quarter = out.shape
    scale = jnp.concatenate([scale] * (quarter // 128), axis=1)
    out[...] = (scale * precond[...]).astype(BF16)


def graft(precond, norms):
    width, quarter = precond.shape
    tiles = 4
    rows = width // tiles
    small = pl.BlockSpec((8, 128), lambda i: (0, 0))
    return pl.pallas_call(
        functools.partial(graft_kernel, float(width * width)),
        out_shape=jax.ShapeDtypeStruct((width, quarter), BF16),
        grid=(tiles,),
        in_specs=[pl.BlockSpec((rows, quarter), lambda i: (i, 0))] + [small] * 4,
        out_specs=pl.BlockSpec((rows, quarter), lambda i: (i, 0)),
        compiler_params=pltpu.CompilerParams(vmem_limit_bytes=6 * MIB),
    )(precond, *norms)


def on_device(
    grad_parts,
    assign,
    block_bounds,
    left_root,
    right_root,
    left_stat,
    right_stat,
    first_moment,
    second_moment,
):
    n_own = lax.axis_size("own")
    n_grp = lax.axis_size("grp")
    own_index = lax.axis_index("own")
    grp_index = lax.axis_index("grp")
    total_blocks = assign.shape[0]
    per_owner = total_blocks // n_own
    shard_rows = grad_parts.shape[2]
    width = grad_parts.shape[3]
    quarter = width // n_grp
    half = total_blocks // 2
    part = grad_parts[0]
    place = jnp.stack([grp_index, own_index]).astype(jnp.int32)
    starts = [((grp_index + step) & (n_grp - 1)) * quarter for step in range(4)]
    turn = ((n_grp - grp_index) & (n_grp - 1)) * quarter
    part, place, starts, turn = lax.optimization_barrier((part, place, starts, turn))

    def columns(array, step):
        return slice_at(array, starts[step], quarter, array.ndim - 1)

    far = columns(part, 2)
    far_up = shift(far[:half], 1)
    far_down = shift(far[half:], -1)
    left_bf, right_bf = left_root[0].astype(BF16), right_root[0].astype(BF16)
    left_low, left_high = left_bf[: quarter // 2], left_bf[quarter // 2 :]
    later, left_low, left_high, far_up, far_down = lax.optimization_barrier(
        (part, left_low, left_high, far_up, far_down)
    )
    up = columns(later, 1)
    down = columns(later, 3)
    up_direct = shift(up[half:], 1)
    down_direct = shift(down[:half], -1)
    up_sum = shift((up[:half].astype(F32) + far_up.astype(F32)).astype(BF16), 1)
    down_sum = shift((down[half:].astype(F32) + far_down.astype(F32)).astype(BF16), -1)
    left_prev_low = shift(left_low, 1)
    left_next_high = shift(left_high, -1)

    key = (assign % n_own * per_owner + assign // n_own).astype(jnp.int32)
    right_parts = [columns(right_bf, step) for step in range(4)]
    sums, left_prev_low, left_next_high, right_parts = lax.optimization_barrier(
        ((up_sum, up_direct, down_direct, down_sum), left_prev_low, left_next_high, right_parts)
    )

    sorted_grad, first_next, second_next = pack(
        place, key, block_bounds, part, sums, first_moment, second_moment
    )
    owned = lax.all_to_all(sorted_grad, "own", split_axis=0, concat_axis=0, tiled=True)
    left_far_low = shift(left_prev_low, 1)
    left_far_high = shift(left_next_high, -1)
    left_prev_high = shift(left_high, 1)
    left_next_low = shift(left_low, -1)
    roots = [right_parts[0]] + [shift(right_parts[step], step) for step in (3, 2, 1)]
    lefts = [
        left_bf,
        left_next_low,
        left_next_high,
        left_far_low,
        left_far_high,
        left_prev_low,
        left_prev_high,
    ]

    owned, lefts, roots = lax.optimization_barrier((owned, lefts, roots))
    own_cols = jnp.concatenate(
        [owned[:, :shard_rows], owned[:, shard_rows : 2 * shard_rows]], axis=2
    )
    adam = owned[:, 2 * shard_rows :].reshape(n_own * shard_rows // 2, 128)
    low, high = own_cols[:half], own_cols[half:]
    prev_low = shift(low, 1)
    next_high = shift(high, -1)
    prev_high = shift(high, 1)
    next_low = shift(low, -1)
    far_low = shift(prev_low, 1)
    far_high = shift(next_high, -1)
    pieces = [low, high, next_low, next_high, far_low, far_high, prev_low, prev_high]
    pieces = [piece.reshape(width // 2, quarter) for piece in pieces]

    precond, norms = precondition(place, pieces, roots, lefts, adam)
    norms = [norms] + [shift(norms, step) for step in (1, 2, 3)]
    grafted = graft(precond, norms).reshape(n_own, shard_rows, quarter)
    pieces, grafted = lax.optimization_barrier((pieces, grafted))
    back = lax.all_to_all(grafted, "own", split_axis=0, concat_axis=0, tiled=True)

    whole = jnp.concatenate([jnp.concatenate(pieces[i::2], axis=1) for i in (0, 1)], axis=0)
    rows = slice_at(whole, starts[0], quarter, 0)
    left_acc = STAT_DECAY * left_stat + dot(rows, whole, ((1,), (1,)))[None]
    cross = dot(whole[:, :quarter], whole, ((0,), (0,)))
    cross = jnp.concatenate([cross, cross], axis=1)
    cross = slice_at(cross, turn, width, 1)
    right_acc = STAT_DECAY * right_stat + cross[None]

    update = finish(place, key, block_bounds, back)
    return (update, first_next, second_next, left_acc, right_acc)


def solution(mesh):
    placed = (
        P("grp", None, "own", None),
        P(),
        P(),
        P("own", "grp", None),
        P("own", "grp", None),
        P("own", "grp", None),
        P("own", "grp", None),
        P(None, "own", "grp"),
        P(None, "own", "grp"),
    )
    return jax.shard_map(
        on_device,
        mesh=mesh,
        in_specs=placed,
        out_specs=(
            P(None, "own", "grp"),
            P(None, "own", "grp"),
            P(None, "own", "grp"),
            P("own", "grp", None),
            P("own", "grp", None),
        ),
        check_vma=False,
    )
```

```python
import functools

import jax
import jax.numpy as jnp
from jax import lax
from jax.experimental import pallas as pl
from jax.experimental.pallas import tpu as pltpu
from jax.sharding import PartitionSpec as P

BETA_FIRST = 0.9
BETA_SECOND = 0.95
BIAS_FIRST = 1.0 - 0.9**10
BIAS_SECOND = 1.0 - 0.95**10
ADAM_EPS = 1e-08
STAT_DECAY = 0.95
NORM_EPS = 1e-06
F32 = jnp.float32
BF16 = jnp.bfloat16
MIB = 1024 * 1024
VMEM = pltpu.VMEM
LONG = pl.CostEstimate(flops=2 * 10**11, bytes_accessed=10**9, transcendentals=0)


def shift(array, step):
    n = lax.axis_size("grp")
    return lax.ppermute(array, "grp", [(i, (i + step) % n) for i in range(n)])


def slots_of(assign, n_own, per_owner):
    return (assign % n_own * per_owner + assign // n_own).astype(jnp.int32)


def in_hbm(array):
    return pltpu.with_memory_space_constraint(array, pltpu.HBM)


def slice_at(array, start, size, axis):
    starts = [start if i == axis else 0 for i in range(array.ndim)]
    sizes = [size if i == axis else n for i, n in enumerate(array.shape)]
    return lax.dynamic_slice(array, starts, sizes, allow_negative_indices=False)


def dot(a, b, dims):
    return lax.dot_general(a, b, (dims, ((), ())), preferred_element_type=F32)


def inside(bounds, block, rows, cols):
    row = lax.broadcasted_iota(jnp.int32, (rows, cols), 0) + lax.axis_index("own") * rows
    col = lax.broadcasted_iota(jnp.int32, (rows, cols), 1) + lax.axis_index("grp") * cols
    row_off, col_off, n_rows, n_cols = [bounds[4 * block + i] for i in range(4)]
    return (row < n_rows - row_off) & (col < n_cols - col_off)


def gather_kernel(place, own, up_direct, down_direct, out):
    half = own.shape[1]

    def step(i, carry):
        out[0, i] = own[0, i].astype(F32) + down_direct[i].astype(F32)
        out[1, i] = own[1, i].astype(F32) + up_direct[i].astype(F32)
        return carry

    lax.fori_loop(0, half, step, 0, unroll=4)


def gather(place, part, up_direct, down_direct):
    blocks, rows, width = part.shape
    half, cols = blocks // 2, up_direct.shape[2]
    whole = pl.BlockSpec(up_direct.shape, lambda i, *_: (0, 0, 0))
    return pl.pallas_call(
        gather_kernel,
        out_shape=jax.ShapeDtypeStruct((2, half, rows, cols), F32),
        grid_spec=pltpu.PrefetchScalarGridSpec(
            num_scalar_prefetch=1,
            grid=(1,),
            in_specs=[
                pl.BlockSpec((2, half, rows, cols), lambda i, place: (0, 0, 0, place[0])),
                whole,
                whole,
            ],
            out_specs=pl.BlockSpec((2, half, rows, cols), lambda i, *_: (0, 0, 0, 0)),
        ),
        compiler_params=pltpu.CompilerParams(vmem_limit_bytes=8 * MIB),
        cost_estimate=LONG,
    )(place, part.reshape(2, half, rows, width), up_direct, down_direct)


def pack_kernel(
    key, bounds, partial, up_sum, down_sum, first, second, out, first_out, second_out
):
    _, count, rows, cols = partial.shape
    half = out.shape[0] // 2
    begin = pl.program_id(0) * count
    lanes = 128

    def one(side, i, value):
        block = side * half + begin + i
        ok = inside(bounds, block, rows, cols)
        grad = jnp.where(ok, value, 0.0)
        first_next = BETA_FIRST * first[side, i] + (1.0 - BETA_FIRST) * grad
        second_next = BETA_SECOND * second[side, i] + (1.0 - BETA_SECOND) * grad * grad
        first_out[side, i] = first_next
        second_out[side, i] = second_next
        adam = first_next / (jnp.sqrt(second_next) + ADAM_EPS * BIAS_SECOND**0.5)
        square = jnp.where(ok, adam * adam, 0.0)
        square = square[:, :lanes] + square[:, lanes:]
        square = square[: rows // 2] + square[rows // 2 :]
        piece = jnp.concatenate([grad[:, :lanes], grad[:, lanes:], square], axis=0)
        out[key[block]] = piece.astype(BF16)

    def step(i, carry):
        one(0, i, partial[0, i] + up_sum[i].astype(F32))
        one(1, i, partial[1, i] + down_sum[i].astype(F32))
        return carry

    lax.fori_loop(0, count, step, 0, unroll=4)


def pack(key, bounds, partial, up_sum, down_sum, first, second):
    _, half, rows, cols = partial.shape
    blocks = 2 * half
    steps = 4 if half >= 16 else 1
    count = half // steps
    piece = 2 * rows + rows // 2
    moment = pl.BlockSpec((2, count, rows, cols), lambda i, *_: (0, i, 0, 0))
    halves = jax.ShapeDtypeStruct((2, half, rows, cols), F32)
    out, first_next, second_next = pl.pallas_call(
        pack_kernel,
        out_shape=(pltpu.HBM((blocks, piece, 128), BF16), halves, halves),
        grid_spec=pltpu.PrefetchScalarGridSpec(
            num_scalar_prefetch=2,
            grid=(steps,),
            in_specs=[
                moment,
                pl.BlockSpec((count, rows, cols), lambda i, *_: (i, 0, 0)),
                pl.BlockSpec((count, rows, cols), lambda i, *_: (i, 0, 0)),
                moment,
                moment,
            ],
            out_specs=[
                pl.BlockSpec((blocks, piece, 128), lambda i, *_: (0, 0, 0)),
                moment,
                moment,
            ],
        ),
        compiler_params=pltpu.CompilerParams(vmem_limit_bytes=10 * MIB),
    )(
        key,
        bounds,
        partial,
        up_sum,
        down_sum,
        in_hbm(first.reshape(halves.shape)),
        in_hbm(second.reshape(halves.shape)),
    )
    return out, first_next.reshape(first.shape), second_next.reshape(second.shape)


def relay_kernel(prev, following, low, high):
    rows = low.shape[0]
    low[...] = prev[pl.ds(0, rows), :]
    high[...] = following[pl.ds(rows, rows), :]


def relay(prev, following):
    rows, width = prev.shape
    half = jax.ShapeDtypeStruct((rows // 2, width), BF16)
    return pl.pallas_call(
        relay_kernel,
        out_shape=(half, half),
        in_specs=[pl.BlockSpec(memory_space=VMEM)] * 2,
        out_specs=(pl.BlockSpec(memory_space=VMEM),) * 2,
        compiler_params=pltpu.CompilerParams(vmem_limit_bytes=6 * MIB),
        cost_estimate=LONG,
    )(prev, following)


def finish_kernel(key, bounds, back, out):
    blocks, rows, cols = out.shape

    def step(block, carry):
        ok = inside(bounds, block, rows, cols)
        out[block] = jnp.where(ok, back[key[block]].astype(F32), 0.0).astype(BF16)
        return carry

    lax.fori_loop(0, blocks, step, 0, unroll=4)


def finish(key, bounds, back):
    whole = pl.BlockSpec(back.shape, lambda i, *_: (0, 0, 0))
    return pl.pallas_call(
        finish_kernel,
        out_shape=jax.ShapeDtypeStruct(back.shape, BF16),
        grid_spec=pltpu.PrefetchScalarGridSpec(
            num_scalar_prefetch=2, grid=(1,), in_specs=[whole], out_specs=whole
        ),
        compiler_params=pltpu.CompilerParams(vmem_limit_bytes=6 * MIB),
    )(key, bounds, back)


def precond_kernel(*refs):
    own_low, own_high, next_low, next_high, far_low, far_high, prev_low, prev_high = refs[:8]
    roots, lefts, (adam, out, norms, mixed) = refs[8:12], refs[12:17], refs[17:]
    width, quarter = out.shape
    half = width // 2
    me = lax.axis_index("grp")
    n = width // quarter
    for top, parts in (
        (0, (own_low, next_low, far_low, prev_low)),
        (half, (own_high, next_high, far_high, prev_high)),
    ):
        for row in range(0, half, quarter):
            total = jnp.zeros((quarter, quarter), F32)
            for piece, root in zip(parts, roots):
                total += dot(piece[pl.ds(row, quarter), :], root[...], ((1,), (0,)))
            mixed[pl.ds(top + row, quarter), :] = total.astype(BF16)
    square = jnp.zeros((8, quarter), F32)
    eighth = quarter // 2
    places = ((0, 0), (1, 0), (2, 0), (2, eighth), (3, 0))
    for (step, extra), left in zip(places, lefts):
        base = lax.rem(me + step, n) * quarter + extra
        rows = left.shape[0]
        value = dot(left[...], mixed[...], ((1,), (0,)))
        out[pl.ds(pl.multiple_of(base, eighth), rows), :] = value
        square += jnp.sum((value * value).reshape(rows // 8, 8, quarter), axis=0)
    norms[...] = jnp.zeros_like(norms)
    norms[0:1, :] = jnp.broadcast_to(jnp.sum(square), (1, 128))
    norms[1:2, :] = jnp.broadcast_to(jnp.sum(adam[...].astype(F32)), (1, 128))


def precondition(pieces, roots, lefts, adam):
    rows, quarter = pieces[0].shape
    operands = (*pieces, *map(in_hbm, roots), *map(in_hbm, lefts), adam)
    return pl.pallas_call(
        precond_kernel,
        out_shape=(
            jax.ShapeDtypeStruct((2 * rows, quarter), F32),
            jax.ShapeDtypeStruct((8, 128), F32),
        ),
        in_specs=[pl.BlockSpec(memory_space=VMEM)] * len(operands),
        out_specs=(pl.BlockSpec(memory_space=VMEM),) * 2,
        scratch_shapes=[VMEM((2 * rows, quarter), BF16)],
        compiler_params=pltpu.CompilerParams(vmem_limit_bytes=12 * MIB),
    )(*operands)


def graft_kernel(cells, precond, first, second, third, fourth, out):
    sums = first[...] + second[...] + third[...] + fourth[...]
    pre, adam = sums[0:1, :], sums[1:2, :]
    adam = adam * (BIAS_SECOND / (BIAS_FIRST * BIAS_FIRST))
    scale = -jnp.sqrt(adam / cells) / jnp.sqrt(pre / cells + NORM_EPS)
    width, quarter = out.shape
    scale = jnp.concatenate([scale] * (quarter // 128), axis=1)
    out[...] = (scale * precond[...]).astype(BF16)


def graft(precond, norms):
    width, quarter = precond.shape
    tiles = 4
    rows = width // tiles
    small = pl.BlockSpec((8, 128), lambda i: (0, 0))
    return pl.pallas_call(
        functools.partial(graft_kernel, float(width * width)),
        out_shape=jax.ShapeDtypeStruct((width, quarter), BF16),
        grid=(tiles,),
        in_specs=[pl.BlockSpec((rows, quarter), lambda i: (i, 0))] + [small] * 4,
        out_specs=pl.BlockSpec((rows, quarter), lambda i: (i, 0)),
        compiler_params=pltpu.CompilerParams(vmem_limit_bytes=6 * MIB),
    )(precond, *norms)


def on_device(
    grad_parts,
    assign,
    block_bounds,
    left_root,
    right_root,
    left_stat,
    right_stat,
    first_moment,
    second_moment,
):
    n_own = lax.axis_size("own")
    n_grp = lax.axis_size("grp")
    grp_index = lax.axis_index("grp")
    total_blocks = assign.shape[0]
    per_owner = total_blocks // n_own
    shard_rows = grad_parts.shape[2]
    width = grad_parts.shape[3]
    quarter = width // n_grp
    half = total_blocks // 2
    part = grad_parts[0]
    place = grp_index.reshape(1).astype(jnp.int32)
    starts = [((grp_index + step) & (n_grp - 1)) * quarter for step in range(4)]
    turn = ((n_grp - grp_index) & (n_grp - 1)) * quarter
    part, place, starts, turn = lax.optimization_barrier((part, place, starts, turn))

    def columns(array, step):
        return slice_at(array, starts[step], quarter, array.ndim - 1)

    far = columns(part, 2)
    up = columns(part, 1)
    down = columns(part, 3)
    far_up = shift(far[:half], 1)
    far_down = shift(far[half:], -1)
    up_direct = shift(up[half:], 1)
    down_direct = shift(down[:half], -1)
    up_sum = shift((up[:half].astype(F32) + far_up.astype(F32)).astype(BF16), 1)
    down_sum = shift((down[half:].astype(F32) + far_down.astype(F32)).astype(BF16), -1)
    key, bounds = slots_of(assign, n_own, per_owner), block_bounds.reshape(-1)
    up_direct, down_direct, key, bounds = lax.optimization_barrier(
        (up_direct, down_direct, key, bounds)
    )
    partial = gather(place, part, up_direct, down_direct)

    left_bf, right_bf = left_root[0].astype(BF16), right_root[0].astype(BF16)
    right_parts = [columns(right_bf, step) for step in range(4)]
    left_bf, right_parts, up_sum, down_sum, partial = lax.optimization_barrier(
        (left_bf, right_parts, up_sum, down_sum, partial)
    )
    sorted_grad, first_next, second_next = pack(
        key, bounds, partial, up_sum, down_sum, first_moment, second_moment
    )
    owned = lax.all_to_all(sorted_grad, "own", split_axis=0, concat_axis=0, tiled=True)
    left_prev = shift(left_bf, 1)
    left_next = shift(left_bf, -1)
    far_halves = relay(left_prev, left_next)
    left_far_low = shift(far_halves[0], 1)
    left_far_high = shift(far_halves[1], -1)
    right_parts, far_halves = lax.optimization_barrier((right_parts, far_halves))
    roots = [right_parts[0]] + [shift(right_parts[step], step) for step in (3, 2, 1)]
    lefts = [left_bf, left_next, left_far_low, left_far_high, left_prev]

    owned, lefts, roots = lax.optimization_barrier((owned, lefts, roots))
    own_cols = jnp.concatenate(
        [owned[:, :shard_rows], owned[:, shard_rows : 2 * shard_rows]], axis=2
    )
    adam = owned[:, 2 * shard_rows :].reshape(n_own * shard_rows // 2, 128)
    low, high = own_cols[:half], own_cols[half:]
    prev_low = shift(low, 1)
    next_high = shift(high, -1)
    prev_high = shift(high, 1)
    next_low = shift(low, -1)
    far_low = shift(prev_low, 1)
    far_high = shift(next_high, -1)
    pieces = [low, high, next_low, next_high, far_low, far_high, prev_low, prev_high]
    flat = [piece.reshape(width // 2, quarter) for piece in pieces]
    precond, norms = precondition(flat, roots, lefts, adam)
    norms = [norms] + [shift(norms, step) for step in (1, 2, 3)]
    grafted = graft(precond, norms).reshape(n_own, shard_rows, quarter)
    pieces, grafted, assign, bounds = lax.optimization_barrier(
        (pieces, grafted, assign, block_bounds)
    )
    key, bounds = slots_of(assign, n_own, per_owner), bounds.reshape(-1)
    back = lax.all_to_all(grafted, "own", split_axis=0, concat_axis=0, tiled=True)

    whole = jnp.concatenate(
        [jnp.concatenate(pieces[i : i + 2], axis=0) for i in (0, 2, 4, 6)], axis=2
    ).reshape(width, width)
    rows = slice_at(whole, starts[0], quarter, 0)
    left_acc = STAT_DECAY * left_stat + dot(rows, whole, ((1,), (1,)))[None]
    cross = dot(whole[:, :quarter], whole, ((0,), (0,)))
    cross = jnp.concatenate([cross, cross], axis=1)
    cross = slice_at(cross, turn, width, 1)
    right_acc = STAT_DECAY * right_stat + cross[None]

    update = finish(key, bounds, back)
    return (update, first_next, second_next, left_acc, right_acc)


def solution(mesh):
    placed = (
        P("grp", None, "own", None),
        P(),
        P(),
        P("own", "grp", None),
        P("own", "grp", None),
        P("own", "grp", None),
        P("own", "grp", None),
        P(None, "own", "grp"),
        P(None, "own", "grp"),
    )
    return jax.shard_map(
        on_device,
        mesh=mesh,
        in_specs=placed,
        out_specs=(
            P(None, "own", "grp"),
            P(None, "own", "grp"),
            P(None, "own", "grp"),
            P("own", "grp", None),
            P("own", "grp", None),
        ),
        check_vma=False,
    )
```

```python
import functools

import jax
import jax.numpy as jnp
from jax import lax
from jax.experimental import pallas as pl
from jax.experimental.pallas import tpu as pltpu
from jax.sharding import PartitionSpec as P

BETA_FIRST = 0.9
BETA_SECOND = 0.95
BIAS_FIRST = 1.0 - 0.9**10
BIAS_SECOND = 1.0 - 0.95**10
ADAM_EPS = 1e-08
STAT_DECAY = 0.95
NORM_EPS = 1e-06
F32 = jnp.float32
BF16 = jnp.bfloat16
MIB = 1024 * 1024
VMEM = pltpu.VMEM
LONG = pl.CostEstimate(flops=2 * 10**11, bytes_accessed=10**9, transcendentals=0)


def shift(array, step):
    n = lax.axis_size("grp")
    return lax.ppermute(array, "grp", [(i, (i + step) % n) for i in range(n)])


def slots_of(assign, n_own, per_owner):
    return (assign % n_own * per_owner + assign // n_own).astype(jnp.int32)


def in_hbm(array):
    return pltpu.with_memory_space_constraint(array, pltpu.HBM)


def slice_at(array, start, size, axis):
    starts = [start if i == axis else 0 for i in range(array.ndim)]
    sizes = [size if i == axis else n for i, n in enumerate(array.shape)]
    return lax.dynamic_slice(array, starts, sizes, allow_negative_indices=False)


def dot(a, b, dims):
    return lax.dot_general(a, b, (dims, ((), ())), preferred_element_type=F32)


def inside(bounds, block, rows, cols):
    row_off, col_off, n_rows, n_cols = [bounds[4 * block + i] for i in range(4)]
    row, col = lax.axis_index("own") * rows, lax.axis_index("grp") * cols
    return (row < n_rows - row_off) & (col < n_cols - col_off)


def split_kernel(cuts, part, *refs):
    outs, sems = refs[: len(cuts)], refs[len(cuts)]
    quarter = outs[0].shape[2]
    copies = []
    for i, ((first, step), out) in enumerate(zip(cuts, outs)):
        col = ((lax.axis_index("grp") + step) & 3) * quarter
        source = part.at[0, pl.ds(first, out.shape[0]), :, pl.ds(pl.multiple_of(col, quarter), quarter)]
        copies.append(pltpu.make_async_copy(source, out, sems.at[i]))
    for copy in copies:
        copy.start()
    for copy in copies:
        copy.wait()


def split(part, cuts, quarter):
    rows = part.shape[2]
    return pl.pallas_call(
        functools.partial(split_kernel, tuple((first, step) for first, _, step in cuts)),
        out_shape=tuple(
            pltpu.HBM((count, rows, quarter), BF16) for _, count, _ in cuts
        ),
        in_specs=[pl.BlockSpec(memory_space=pl.ANY)],
        out_specs=(pl.BlockSpec(memory_space=pl.ANY),) * len(cuts),
        scratch_shapes=[pltpu.SemaphoreType.DMA((len(cuts),))],
        compiler_params=pltpu.CompilerParams(vmem_limit_bytes=2 * MIB),
    )(in_hbm(part))


def add_kernel(up, far_up, down, far_down, up_out, down_out):
    up_out[...] = (up[...].astype(F32) + far_up[...].astype(F32)).astype(BF16)
    down_out[...] = (down[...].astype(F32) + far_down[...].astype(F32)).astype(BF16)


def add(*arrays):
    shape = jax.ShapeDtypeStruct(arrays[0].shape, BF16)
    return pl.pallas_call(
        add_kernel,
        out_shape=(shape, shape),
        in_specs=[pl.BlockSpec(memory_space=VMEM)] * 4,
        out_specs=(pl.BlockSpec(memory_space=VMEM),) * 2,
        compiler_params=pltpu.CompilerParams(vmem_limit_bytes=4 * MIB),
    )(*arrays)


def roots_kernel(left, right, up, down, own):
    _, units, _, cols = (1, *up.shape)
    rows = up.shape[1]

    def root(half, step):
        col = ((lax.axis_index("grp") + step) & 3) * cols
        col = pl.ds(pl.multiple_of(col, cols), cols)
        return right[0, pl.ds(half * rows, rows), col].astype(BF16)

    for half in range(2):
        own[half] = root(half, 0)
        up[9 + half] = root(half, 1)
        down[9 + half] = root(half, 3)
        for c in range(4):
            unit = left[0, pl.ds(half * rows, rows), pl.ds(c * cols, cols)].astype(BF16)
            up[5 * half + c] = unit
            down[5 - 5 * half + c] = unit
    up[4] = root(0, 2)
    down[4] = root(1, 2)


def root_pieces(left, right):
    _, rows, width = left.shape
    unit = (rows // 2, width // 4)
    return pl.pallas_call(
        roots_kernel,
        out_shape=(
            pltpu.HBM((11, *unit), BF16),
            pltpu.HBM((11, *unit), BF16),
            pltpu.HBM((2, *unit), BF16),
        ),
        grid=(1,),
        in_specs=[pl.BlockSpec(left.shape, lambda i: (0, 0, 0))] * 2,
        out_specs=tuple(pl.BlockSpec((n, *unit), lambda i: (0, 0, 0)) for n in (11, 11, 2)),
        compiler_params=pltpu.CompilerParams(vmem_limit_bytes=8 * MIB),
    )(in_hbm(left), in_hbm(right))


def gather_kernel(own, up_direct, down_direct, out):
    half = up_direct.shape[0]

    def step(i, carry):
        out[0, i] = own[i].astype(F32) + down_direct[i].astype(F32)
        out[1, i] = own[i + half].astype(F32) + up_direct[i].astype(F32)
        return carry

    lax.fori_loop(0, half, step, 0, unroll=4)


def gather(own, up_direct, down_direct):
    return pl.pallas_call(
        gather_kernel,
        out_shape=jax.ShapeDtypeStruct((2, *up_direct.shape), F32),
        in_specs=[pl.BlockSpec(memory_space=VMEM)] * 3,
        out_specs=pl.BlockSpec(memory_space=VMEM),
        compiler_params=pltpu.CompilerParams(vmem_limit_bytes=6 * MIB),
        cost_estimate=LONG,
    )(own, up_direct, down_direct)


def pack_kernel(
    key, bounds, partial, up_sum, down_sum, first, second, out, first_out, second_out
):
    _, count, rows, cols = partial.shape
    half = out.shape[0] // 2
    begin = pl.program_id(0) * count
    lanes = 128

    def one(side, i, value):
        block = side * half + begin + i
        keep = jnp.where(inside(bounds, block, rows, cols), 1.0, 0.0)
        grad = value * keep
        first_next = BETA_FIRST * first[side, i] + (1.0 - BETA_FIRST) * grad
        second_next = BETA_SECOND * second[side, i] + (1.0 - BETA_SECOND) * grad * grad
        first_out[side, i] = first_next
        second_out[side, i] = second_next
        root = second_next * lax.rsqrt(second_next)
        adam = first_next * pl.reciprocal(root + ADAM_EPS * BIAS_SECOND**0.5)
        square = adam * adam
        square = square[:, :lanes] + square[:, lanes:]
        square = (square[: rows // 2] + square[rows // 2 :]) * keep
        piece = jnp.concatenate([grad[:, :lanes], grad[:, lanes:], square], axis=0)
        out[key[block]] = piece.astype(BF16)

    def step(i, carry):
        one(0, i, partial[0, i] + up_sum[i].astype(F32))
        one(1, i, partial[1, i] + down_sum[i].astype(F32))
        return carry

    lax.fori_loop(0, count, step, 0, unroll=4)


def pack(key, bounds, partial, up_sum, down_sum, first, second):
    _, half, rows, cols = partial.shape
    blocks = 2 * half
    steps = 4 if half >= 16 else 1
    count = half // steps
    piece = 2 * rows + rows // 2
    moment = pl.BlockSpec((2, count, rows, cols), lambda i, *_: (0, i, 0, 0))
    halves = jax.ShapeDtypeStruct((2, half, rows, cols), F32)
    out, first_next, second_next = pl.pallas_call(
        pack_kernel,
        out_shape=(pltpu.HBM((blocks, piece, 128), BF16), halves, halves),
        grid_spec=pltpu.PrefetchScalarGridSpec(
            num_scalar_prefetch=2,
            grid=(steps,),
            in_specs=[
                moment,
                pl.BlockSpec((count, rows, cols), lambda i, *_: (i, 0, 0)),
                pl.BlockSpec((count, rows, cols), lambda i, *_: (i, 0, 0)),
                moment,
                moment,
            ],
            out_specs=[
                pl.BlockSpec((blocks, piece, 128), lambda i, *_: (0, 0, 0)),
                moment,
                moment,
            ],
        ),
        compiler_params=pltpu.CompilerParams(vmem_limit_bytes=10 * MIB),
    )(
        key,
        bounds,
        partial,
        up_sum,
        down_sum,
        in_hbm(first.reshape(halves.shape)),
        in_hbm(second.reshape(halves.shape)),
    )
    return out, first_next.reshape(first.shape), second_next.reshape(second.shape)


def relay_kernel(prev, following, up, down):
    units = up.shape[0]
    up[...] = prev[pl.ds(0, units)]
    down[...] = following[pl.ds(0, units)]


def relay(prev, following):
    shape = jax.ShapeDtypeStruct((5, *prev.shape[1:]), BF16)
    return pl.pallas_call(
        relay_kernel,
        out_shape=(shape, shape),
        in_specs=[pl.BlockSpec(memory_space=VMEM)] * 2,
        out_specs=(pl.BlockSpec(memory_space=VMEM),) * 2,
        compiler_params=pltpu.CompilerParams(vmem_limit_bytes=6 * MIB),
        cost_estimate=LONG,
    )(prev, following)


def finish_kernel(key, bounds, back, out):
    blocks, rows, cols = out.shape

    def step(block, carry):
        ok = inside(bounds, block, rows, cols)
        out[block] = jnp.where(ok, back[key[block]], jnp.zeros((), BF16))
        return carry

    lax.fori_loop(0, blocks, step, 0, unroll=8)


def finish(key, bounds, back):
    whole = pl.BlockSpec(back.shape, lambda i, *_: (0, 0, 0))
    return pl.pallas_call(
        finish_kernel,
        out_shape=jax.ShapeDtypeStruct(back.shape, BF16),
        grid_spec=pltpu.PrefetchScalarGridSpec(
            num_scalar_prefetch=2, grid=(1,), in_specs=[whole], out_specs=whole
        ),
        compiler_params=pltpu.CompilerParams(vmem_limit_bytes=6 * MIB),
    )(key, bounds, back)


def precond_kernel(*refs):
    own_low, own_high, next_low, next_high, far_low, far_high, prev_low, prev_high = refs[:8]
    adam, sources, (out, norms) = refs[8], refs[9:15], refs[15:17]
    mixed, held, sems = refs[17], refs[18:24], refs[24]
    width, quarter = out.shape
    half = width // 2
    me = lax.axis_index("grp")
    n = width // quarter
    copies = [pltpu.make_async_copy(*args) for args in zip(sources, held, [sems.at[i] for i in range(6)])]
    for copy in copies:
        copy.start()
    root, up, up_prev, down_next, up_far, down_far = held
    for copy in copies:
        copy.wait()

    def joined(low, high):
        return jnp.concatenate([low, high], axis=0)

    roots = (
        joined(root[0], root[1]),
        joined(down_next[9], down_next[10]),
        joined(up_far[4], down_far[4]),
        joined(up_prev[9], up_prev[10]),
    )
    for top, parts in (
        (0, (own_low, next_low, far_low, prev_low)),
        (half, (own_high, next_high, far_high, prev_high)),
    ):
        for row in range(0, half, quarter):
            total = jnp.zeros((quarter, quarter), F32)
            for piece, right in zip(parts, roots):
                total += dot(piece[pl.ds(row, quarter), :], right, ((1,), (0,)))
            mixed[pl.ds(top + row, quarter), :] = total.astype(BF16)
    square = jnp.zeros((8, quarter), F32)
    for step, (low, first), (high, second) in (
        (0, (up, 0), (up, 5)),
        (1, (down_next, 5), (down_next, 0)),
        (2, (up_far, 0), (down_far, 0)),
        (3, (up_prev, 0), (up_prev, 5)),
    ):
        left = jnp.concatenate([joined(low[first + c], high[second + c]) for c in range(n)], axis=1)
        value = dot(left, mixed[...], ((1,), (0,)))
        base = ((me + step) & (n - 1)) * quarter
        out[pl.ds(pl.multiple_of(base, quarter), quarter), :] = value
        square += jnp.sum((value * value).reshape(quarter // 8, 8, quarter), axis=0)
    norms[...] = jnp.zeros_like(norms)
    norms[0:1, :] = jnp.broadcast_to(jnp.sum(square), (1, 128))
    norms[1:2, :] = jnp.broadcast_to(jnp.sum(adam[...].astype(F32)), (1, 128))


def precondition(pieces, adam, sources):
    rows, quarter = pieces[0].shape
    operands = (*pieces, adam)
    return pl.pallas_call(
        precond_kernel,
        out_shape=(
            jax.ShapeDtypeStruct((2 * rows, quarter), F32),
            jax.ShapeDtypeStruct((8, 128), F32),
        ),
        in_specs=[pl.BlockSpec(memory_space=VMEM)] * len(operands)
        + [pl.BlockSpec(memory_space=pl.ANY)] * len(sources),
        out_specs=(pl.BlockSpec(memory_space=VMEM),) * 2,
        scratch_shapes=[
            VMEM((2 * rows, quarter), BF16),
            *[VMEM(source.shape, BF16) for source in sources],
            pltpu.SemaphoreType.DMA((len(sources),)),
        ],
        compiler_params=pltpu.CompilerParams(vmem_limit_bytes=14 * MIB),
    )(*operands, *map(in_hbm, sources))


def graft_kernel(cells, precond, first, second, third, fourth, out):
    sums = first[...] + second[...] + third[...] + fourth[...]
    pre, adam = sums[0:1, :], sums[1:2, :]
    adam = adam * (BIAS_SECOND / (BIAS_FIRST * BIAS_FIRST))
    scale = -jnp.sqrt(adam / cells) / jnp.sqrt(pre / cells + NORM_EPS)
    width, quarter = out.shape
    scale = jnp.concatenate([scale] * (quarter // 128), axis=1)
    out[...] = (scale * precond[...]).astype(BF16)


def graft(precond, norms):
    width, quarter = precond.shape
    tiles = 4
    rows = width // tiles
    small = pl.BlockSpec((8, 128), lambda i: (0, 0))
    return pl.pallas_call(
        functools.partial(graft_kernel, float(width * width)),
        out_shape=jax.ShapeDtypeStruct((width, quarter), BF16),
        grid=(tiles,),
        in_specs=[pl.BlockSpec((rows, quarter), lambda i: (i, 0))] + [small] * 4,
        out_specs=pl.BlockSpec((rows, quarter), lambda i: (i, 0)),
        compiler_params=pltpu.CompilerParams(vmem_limit_bytes=6 * MIB),
    )(precond, *norms)


def on_device(
    grad_parts,
    assign,
    block_bounds,
    left_root,
    right_root,
    left_stat,
    right_stat,
    first_moment,
    second_moment,
):
    n_own = lax.axis_size("own")
    n_grp = lax.axis_size("grp")
    grp_index = lax.axis_index("grp")
    total_blocks = assign.shape[0]
    per_owner = total_blocks // n_own
    shard_rows = grad_parts.shape[2]
    width = grad_parts.shape[3]
    quarter = width // n_grp
    half = total_blocks // 2
    turn = ((n_grp - grp_index) & (n_grp - 1)) * quarter
    first_row = grp_index * quarter
    grad_parts, turn, first_row = lax.optimization_barrier((grad_parts, turn, first_row))

    far_low, far_high = split(grad_parts, ((0, half, 2), (half, half, 2)), quarter)
    far_up = shift(far_low, 1)
    far_down = shift(far_high, -1)
    later, _, _ = lax.optimization_barrier((grad_parts, far_low, far_high))
    up_low, up_high, down_low, down_high, own = split(
        later,
        ((0, half, 1), (half, half, 1), (0, half, 3), (half, half, 3), (0, total_blocks, 0)),
        quarter,
    )
    up_direct = shift(up_high, 1)
    down_direct = shift(down_low, -1)
    up_sum, down_sum = add(up_low, far_up, down_high, far_down)
    up_sum = shift(up_sum, 1)
    down_sum = shift(down_sum, -1)
    key, bounds = slots_of(assign, n_own, per_owner), block_bounds.reshape(-1)
    left_root, right_root, _, _ = lax.optimization_barrier((left_root, right_root, far_low, far_high))
    roots_up, roots_down, root_own = root_pieces(left_root, right_root)
    up_direct, down_direct, key, bounds, roots_up, roots_down, root_own = lax.optimization_barrier(
        (up_direct, down_direct, key, bounds, roots_up, roots_down, root_own)
    )
    partial = gather(own, up_direct, down_direct)

    roots_up, roots_down, up_sum, down_sum, partial = lax.optimization_barrier(
        (roots_up, roots_down, up_sum, down_sum, partial)
    )
    sorted_grad, first_next, second_next = pack(
        key, bounds, partial, up_sum, down_sum, first_moment, second_moment
    )
    owned = lax.all_to_all(sorted_grad, "own", split_axis=0, concat_axis=0, tiled=True)
    roots_prev = shift(roots_up, 1)
    roots_next = shift(roots_down, -1)
    onward = relay(roots_prev, roots_next)
    far_roots = [shift(onward[0], 1), shift(onward[1], -1)]
    roots = [root_own, roots_up, roots_prev, roots_next, *far_roots]

    owned, roots = lax.optimization_barrier((owned, roots))
    own_cols = jnp.concatenate(
        [owned[:, :shard_rows], owned[:, shard_rows : 2 * shard_rows]], axis=2
    )
    adam = owned[:, 2 * shard_rows :].reshape(n_own * shard_rows // 2, 128)
    low, high = own_cols[:half], own_cols[half:]
    prev_low = shift(low, 1)
    next_high = shift(high, -1)
    prev_high = shift(high, 1)
    next_low = shift(low, -1)
    far_low = shift(prev_low, 1)
    far_high = shift(next_high, -1)
    pieces = [low, high, next_low, next_high, far_low, far_high, prev_low, prev_high]
    flat = [piece.reshape(width // 2, quarter) for piece in pieces]
    precond, norms = precondition(flat, adam, roots)
    norms = [norms] + [shift(norms, step) for step in (1, 2, 3)]
    grafted = graft(precond, norms).reshape(n_own, shard_rows, quarter)
    pieces, grafted, assign, bounds = lax.optimization_barrier(
        (pieces, grafted, assign, block_bounds)
    )
    key, bounds = slots_of(assign, n_own, per_owner), bounds.reshape(-1)
    back = lax.all_to_all(grafted, "own", split_axis=0, concat_axis=0, tiled=True)

    whole = jnp.concatenate(
        [jnp.concatenate(pieces[i : i + 2], axis=0) for i in (0, 2, 4, 6)], axis=2
    ).reshape(width, width)
    rows = slice_at(whole, first_row, quarter, 0)
    left_acc = STAT_DECAY * left_stat + dot(rows, whole, ((1,), (1,)))[None]
    cross = dot(whole[:, :quarter], whole, ((0,), (0,)))
    cross = jnp.concatenate([cross, cross], axis=1)
    cross = slice_at(cross, turn, width, 1)
    right_acc = STAT_DECAY * right_stat + cross[None]

    update = finish(key, bounds, back)
    return (update, first_next, second_next, left_acc, right_acc)


def solution(mesh):
    placed = (
        P("grp", None, "own", None),
        P(),
        P(),
        P("own", "grp", None),
        P("own", "grp", None),
        P("own", "grp", None),
        P("own", "grp", None),
        P(None, "own", "grp"),
        P(None, "own", "grp"),
    )
    return jax.shard_map(
        on_device,
        mesh=mesh,
        in_specs=placed,
        out_specs=(
            P(None, "own", "grp"),
            P(None, "own", "grp"),
            P(None, "own", "grp"),
            P("own", "grp", None),
            P("own", "grp", None),
        ),
        check_vma=False,
    )
```

```python
import functools

import jax
import jax.numpy as jnp
from jax import lax
from jax.experimental import pallas as pl
from jax.experimental.pallas import tpu as pltpu
from jax.sharding import PartitionSpec as P

BETA_FIRST = 0.9
BETA_SECOND = 0.95
BIAS_FIRST = 1.0 - 0.9**10
BIAS_SECOND = 1.0 - 0.95**10
ADAM_EPS = 1e-08
STAT_DECAY = 0.95
NORM_EPS = 1e-06
F32 = jnp.float32
BF16 = jnp.bfloat16
MIB = 1024 * 1024
VMEM = pltpu.VMEM
LONG = pl.CostEstimate(flops=2 * 10**11, bytes_accessed=10**9, transcendentals=0)


def shift(array, step):
    n = lax.axis_size("grp")
    return lax.ppermute(array, "grp", [(i, (i + step) % n) for i in range(n)])


def slots_of(assign, n_own, per_owner):
    return (assign % n_own * per_owner + assign // n_own).astype(jnp.int32)


def in_hbm(array):
    return pltpu.with_memory_space_constraint(array, pltpu.HBM)


def slice_at(array, start, size, axis):
    starts = [start if i == axis else 0 for i in range(array.ndim)]
    sizes = [size if i == axis else n for i, n in enumerate(array.shape)]
    return lax.dynamic_slice(array, starts, sizes, allow_negative_indices=False)


def dot(a, b, dims):
    return lax.dot_general(a, b, (dims, ((), ())), preferred_element_type=F32)


def inside(bounds, block, rows, cols):
    row_off, col_off, n_rows, n_cols = [bounds[4 * block + i] for i in range(4)]
    row, col = lax.axis_index("own") * rows, lax.axis_index("grp") * cols
    return (row < n_rows - row_off) & (col < n_cols - col_off)


def add_kernel(up, far_up, down, far_down, up_out, down_out):
    up_out[...] = (up[...].astype(F32) + far_up[...].astype(F32)).astype(BF16)
    down_out[...] = (down[...].astype(F32) + far_down[...].astype(F32)).astype(BF16)


def add(*arrays):
    shape = jax.ShapeDtypeStruct(arrays[0].shape, BF16)
    return pl.pallas_call(
        add_kernel,
        out_shape=(shape, shape),
        in_specs=[pl.BlockSpec(memory_space=VMEM)] * 4,
        out_specs=(pl.BlockSpec(memory_space=VMEM),) * 2,
        compiler_params=pltpu.CompilerParams(vmem_limit_bytes=4 * MIB),
    )(*arrays)


def roots_kernel(left, right, up, down, own):
    _, units, _, cols = (1, *up.shape)
    rows = up.shape[1]

    def root(half, step):
        col = ((lax.axis_index("grp") + step) & 3) * cols
        col = pl.ds(pl.multiple_of(col, cols), cols)
        return right[0, pl.ds(half * rows, rows), col].astype(BF16)

    for half in range(2):
        own[half] = root(half, 0)
        up[9 + half] = root(half, 1)
        down[9 + half] = root(half, 3)
        for c in range(4):
            unit = left[0, pl.ds(half * rows, rows), pl.ds(c * cols, cols)].astype(BF16)
            up[5 * half + c] = unit
            down[5 - 5 * half + c] = unit
    up[4] = root(0, 2)
    down[4] = root(1, 2)


def root_pieces(left, right):
    _, rows, width = left.shape
    unit = (rows // 2, width // 4)
    return pl.pallas_call(
        roots_kernel,
        out_shape=(
            pltpu.HBM((11, *unit), BF16),
            pltpu.HBM((11, *unit), BF16),
            pltpu.HBM((2, *unit), BF16),
        ),
        grid=(1,),
        in_specs=[pl.BlockSpec(left.shape, lambda i: (0, 0, 0))] * 2,
        out_specs=tuple(pl.BlockSpec((n, *unit), lambda i: (0, 0, 0)) for n in (11, 11, 2)),
        compiler_params=pltpu.CompilerParams(vmem_limit_bytes=8 * MIB),
    )(in_hbm(left), in_hbm(right))


def gather_kernel(own, up_direct, down_direct, first, second, out, first_out, second_out):
    half = up_direct.shape[0]

    def step(i, carry):
        out[0, i] = own[i].astype(F32) + down_direct[i].astype(F32)
        out[1, i] = own[i + half].astype(F32) + up_direct[i].astype(F32)
        return carry

    lax.fori_loop(0, half, step, 0, unroll=4)
    first_out[...] = BETA_FIRST * first[...]
    second_out[...] = BETA_SECOND * second[...]


def gather(own, up_direct, down_direct, first, second):
    shape = jax.ShapeDtypeStruct((2, *up_direct.shape), F32)
    return pl.pallas_call(
        gather_kernel,
        out_shape=(shape,) * 3,
        in_specs=[pl.BlockSpec(memory_space=VMEM)] * 5,
        out_specs=(pl.BlockSpec(memory_space=VMEM),) * 3,
        compiler_params=pltpu.CompilerParams(vmem_limit_bytes=10 * MIB),
        cost_estimate=LONG,
    )(own, up_direct, down_direct, first.reshape(shape.shape), second.reshape(shape.shape))


def pack_kernel(
    key, bounds, partial, up_sum, down_sum, first, second, out, first_out, second_out
):
    _, half, rows, cols = partial.shape
    count = first_out.shape[1]
    begin = pl.program_id(0) * count
    lanes = cols // 2

    def one(side, i, value):
        at = begin + i
        block = side * half + at
        keep = jnp.where(inside(bounds, block, rows, cols), 1.0, 0.0)
        grad = value * keep
        first_next = first[side, at] + (1.0 - BETA_FIRST) * grad
        second_next = second[side, at] + (1.0 - BETA_SECOND) * grad * grad
        first_out[side, i] = first_next
        second_out[side, i] = second_next
        root = second_next * lax.rsqrt(second_next)
        adam = first_next * pl.reciprocal(root + ADAM_EPS * BIAS_SECOND**0.5)
        square = adam * adam
        square = square[:, :lanes] + square[:, lanes:]
        square = (square[: rows // 2] + square[rows // 2 :]) * keep
        piece = jnp.concatenate([grad[:, :lanes], grad[:, lanes:], square], axis=0)
        out[key[block]] = piece.astype(BF16)

    def step(i, carry):
        at = begin + i
        one(0, i, partial[0, at] + up_sum[at].astype(F32))
        one(1, i, partial[1, at] + down_sum[at].astype(F32))
        return carry

    lax.fori_loop(0, count, step, 0, unroll=4)


def pack(key, bounds, partial, up_sum, down_sum, first, second):
    _, half, rows, cols = partial.shape
    blocks, lanes = 2 * half, cols // 2
    steps = 4 if half >= 16 else 1
    moment = pl.BlockSpec((2, half // steps, rows, cols), lambda i, *_: (0, i, 0, 0))
    halves = pltpu.HBM((2, half, rows, cols), F32)
    piece = (blocks, 2 * rows + rows // 2, lanes)
    out, first_next, second_next = pl.pallas_call(
        pack_kernel,
        out_shape=(pltpu.HBM(piece, BF16), halves, halves),
        grid_spec=pltpu.PrefetchScalarGridSpec(
            num_scalar_prefetch=2,
            grid=(steps,),
            in_specs=[pl.BlockSpec(memory_space=VMEM)] * 5,
            out_specs=[pl.BlockSpec(piece, lambda i, *_: (0, 0, 0)), moment, moment],
        ),
        compiler_params=pltpu.CompilerParams(vmem_limit_bytes=14 * MIB),
    )(key, bounds, partial, up_sum, down_sum, first, second)
    shape = (blocks, rows, cols)
    return out, first_next.reshape(shape), second_next.reshape(shape)


def relay_kernel(prev, following, up, down):
    units = up.shape[0]
    up[...] = prev[pl.ds(0, units)]
    down[...] = following[pl.ds(0, units)]


def relay(prev, following):
    shape = jax.ShapeDtypeStruct((5, *prev.shape[1:]), BF16)
    return pl.pallas_call(
        relay_kernel,
        out_shape=(shape, shape),
        in_specs=[pl.BlockSpec(memory_space=VMEM)] * 2,
        out_specs=(pl.BlockSpec(memory_space=VMEM),) * 2,
        compiler_params=pltpu.CompilerParams(vmem_limit_bytes=6 * MIB),
        cost_estimate=LONG,
    )(prev, following)


def finish_kernel(key, bounds, back, out):
    blocks, rows, cols = out.shape

    def step(block, carry):
        ok = inside(bounds, block, rows, cols)
        out[block] = jnp.where(ok, back[key[block]], jnp.zeros((), BF16))
        return carry

    lax.fori_loop(0, blocks, step, 0, unroll=8)


def finish(key, bounds, back):
    whole = pl.BlockSpec(back.shape, lambda i, *_: (0, 0, 0))
    return pl.pallas_call(
        finish_kernel,
        out_shape=jax.ShapeDtypeStruct(back.shape, BF16),
        grid_spec=pltpu.PrefetchScalarGridSpec(
            num_scalar_prefetch=2, grid=(1,), in_specs=[whole], out_specs=whole
        ),
        compiler_params=pltpu.CompilerParams(vmem_limit_bytes=6 * MIB),
    )(key, bounds, back)


def precond_kernel(*refs):
    pieces, adam, sources, (out, norms) = refs[:8], refs[8], refs[9:15], refs[15:17]
    mixed, held, sems = refs[17], refs[18:24], refs[24]
    width, quarter = out.shape
    half = width // 2
    me = lax.axis_index("grp")
    n = width // quarter
    copies = [
        pltpu.make_async_copy(source, place, sems.at[i])
        for i, (source, place) in enumerate(zip(sources, held))
    ]
    for copy in copies:
        copy.start()
    root, up, up_prev, down_next, up_far, down_far = held
    for copy in copies:
        copy.wait()
    right = jnp.concatenate(
        [
            root[0],
            root[1],
            down_next[9],
            down_next[10],
            up_far[4],
            down_far[4],
            up_prev[9],
            up_prev[10],
        ],
        axis=0,
    )
    for row in range(0, width, quarter):
        parts = [ref[pl.ds(row % half, quarter), :] for ref in pieces[row // half :: 2]]
        value = dot(jnp.concatenate(parts, axis=1), right, ((1,), (0,)))
        mixed[pl.ds(row, quarter), :] = value.astype(BF16)
    square = jnp.zeros((8, quarter), F32)
    for step, (low, first), (high, second) in (
        (0, (up, 0), (up, 5)),
        (1, (down_next, 5), (down_next, 0)),
        (2, (up_far, 0), (down_far, 0)),
        (3, (up_prev, 0), (up_prev, 5)),
    ):
        units = [jnp.concatenate([low[first + c], high[second + c]], axis=0) for c in range(n)]
        value = dot(jnp.concatenate(units, axis=1), mixed[...], ((1,), (0,)))
        base = ((me + step) & (n - 1)) * quarter
        out[pl.ds(pl.multiple_of(base, quarter), quarter), :] = value
        square += jnp.sum((value * value).reshape(quarter // 8, 8, quarter), axis=0)
    norms[...] = jnp.zeros_like(norms)
    norms[0:1, :] = jnp.broadcast_to(jnp.sum(square), (1, 128))
    norms[1:2, :] = jnp.broadcast_to(jnp.sum(adam[...].astype(F32)), (1, 128))


def precondition(pieces, adam, sources):
    rows, quarter = pieces[0].shape
    operands = (*pieces, adam)
    return pl.pallas_call(
        precond_kernel,
        out_shape=(
            jax.ShapeDtypeStruct((2 * rows, quarter), F32),
            jax.ShapeDtypeStruct((8, 128), F32),
        ),
        in_specs=[pl.BlockSpec(memory_space=VMEM)] * len(operands)
        + [pl.BlockSpec(memory_space=pl.ANY)] * len(sources),
        out_specs=(pl.BlockSpec(memory_space=VMEM),) * 2,
        scratch_shapes=[
            VMEM((2 * rows, quarter), BF16),
            *[VMEM(source.shape, BF16) for source in sources],
            pltpu.SemaphoreType.DMA((len(sources),)),
        ],
        compiler_params=pltpu.CompilerParams(vmem_limit_bytes=14 * MIB),
    )(*operands, *map(in_hbm, sources))


def graft_kernel(cells, precond, first, second, third, fourth, out):
    sums = first[...] + second[...] + third[...] + fourth[...]
    pre, adam = sums[0:1, :], sums[1:2, :]
    adam = adam * (BIAS_SECOND / (BIAS_FIRST * BIAS_FIRST))
    scale = -jnp.sqrt(adam / cells) / jnp.sqrt(pre / cells + NORM_EPS)
    width, quarter = out.shape
    scale = jnp.concatenate([scale] * (quarter // 128), axis=1)
    out[...] = (scale * precond[...]).astype(BF16)


def graft(precond, norms):
    width, quarter = precond.shape
    tiles = 4
    rows = width // tiles
    small = pl.BlockSpec((8, 128), lambda i: (0, 0))
    return pl.pallas_call(
        functools.partial(graft_kernel, float(width * width)),
        out_shape=jax.ShapeDtypeStruct((width, quarter), BF16),
        grid=(tiles,),
        in_specs=[pl.BlockSpec((rows, quarter), lambda i: (i, 0))] + [small] * 4,
        out_specs=pl.BlockSpec((rows, quarter), lambda i: (i, 0)),
        compiler_params=pltpu.CompilerParams(vmem_limit_bytes=6 * MIB),
    )(precond, *norms)


def on_device(
    grad_parts,
    assign,
    block_bounds,
    left_root,
    right_root,
    left_stat,
    right_stat,
    first_moment,
    second_moment,
):
    n_own = lax.axis_size("own")
    n_grp = lax.axis_size("grp")
    grp_index = lax.axis_index("grp")
    total_blocks = assign.shape[0]
    per_owner = total_blocks // n_own
    shard_rows = grad_parts.shape[2]
    width = grad_parts.shape[3]
    quarter = width // n_grp
    half = total_blocks // 2
    starts = [((grp_index + step) & (n_grp - 1)) * quarter for step in range(4)]
    turn = ((n_grp - grp_index) & (n_grp - 1)) * quarter
    grad_parts, starts, turn = lax.optimization_barrier((grad_parts, starts, turn))

    def columns(array, step):
        return slice_at(array, starts[step], quarter, array.ndim - 1)

    part = grad_parts[0]
    far = columns(part, 2)
    far_low, far_high = lax.optimization_barrier((far[:half], far[half:]))
    far_up = shift(far_low, 1)
    far_down = shift(far_high, -1)
    later, left_root, right_root, _, _ = lax.optimization_barrier(
        (part, left_root, right_root, far_low, far_high)
    )
    up, down = columns(later, 1), columns(later, 3)
    up_low, up_high, down_low, down_high, own = lax.optimization_barrier(
        (up[:half], up[half:], down[:half], down[half:], columns(later, 0))
    )
    up_direct = shift(up_high, 1)
    down_direct = shift(down_low, -1)
    up_sum, down_sum = add(up_low, far_up, down_high, far_down)
    up_sum = shift(up_sum, 1)
    down_sum = shift(down_sum, -1)
    key, bounds = slots_of(assign, n_own, per_owner), block_bounds.reshape(-1)
    roots_up, roots_down, root_own = root_pieces(left_root, right_root)
    up_direct, down_direct, key, bounds, roots_up, roots_down, root_own = lax.optimization_barrier(
        (up_direct, down_direct, key, bounds, roots_up, roots_down, root_own)
    )
    partial, first, second = gather(own, up_direct, down_direct, first_moment, second_moment)

    roots_up, roots_down, up_sum, down_sum, partial = lax.optimization_barrier(
        (roots_up, roots_down, up_sum, down_sum, partial)
    )
    sorted_grad, first_next, second_next = pack(
        key, bounds, partial, up_sum, down_sum, first, second
    )
    owned = lax.all_to_all(sorted_grad, "own", split_axis=0, concat_axis=0, tiled=True)
    roots_prev = shift(roots_up, 1)
    roots_next = shift(roots_down, -1)
    onward = relay(roots_prev, roots_next)
    far_roots = [shift(onward[0], 1), shift(onward[1], -1)]
    roots = [root_own, roots_up, roots_prev, roots_next, *far_roots]

    owned, roots = lax.optimization_barrier((owned, roots))
    own_cols = jnp.concatenate(
        [owned[:, :shard_rows], owned[:, shard_rows : 2 * shard_rows]], axis=2
    )
    adam = owned[:, 2 * shard_rows :].reshape(-1, quarter // 2)
    low, high = own_cols[:half], own_cols[half:]
    prev_low = shift(low, 1)
    next_high = shift(high, -1)
    prev_high = shift(high, 1)
    next_low = shift(low, -1)
    far_low = shift(prev_low, 1)
    far_high = shift(next_high, -1)
    pieces = [low, high, next_low, next_high, far_low, far_high, prev_low, prev_high]
    flat = [piece.reshape(-1, quarter) for piece in pieces]
    precond, norms = precondition(flat, adam, roots)
    norms = [norms] + [shift(norms, step) for step in (1, 2, 3)]
    grafted = graft(precond, norms).reshape(n_own, shard_rows, quarter)
    pieces, grafted, assign, bounds = lax.optimization_barrier(
        (pieces, grafted, assign, block_bounds)
    )
    key, bounds = slots_of(assign, n_own, per_owner), bounds.reshape(-1)
    back = lax.all_to_all(grafted, "own", split_axis=0, concat_axis=0, tiled=True)

    whole = jnp.concatenate(
        [jnp.concatenate(pieces[i : i + 2]) for i in (0, 2, 4, 6)], axis=2
    ).reshape(width, width)
    rows = slice_at(whole, starts[0], quarter, 0)
    left_acc = STAT_DECAY * left_stat + dot(rows, whole, ((1,), (1,)))[None]
    cross = dot(whole[:, :quarter], whole, ((0,), (0,)))
    cross = jnp.concatenate([cross, cross], axis=1)
    cross = slice_at(cross, turn, width, 1)
    right_acc = STAT_DECAY * right_stat + cross[None]

    update = finish(key, bounds, back)
    return (update, first_next, second_next, left_acc, right_acc)


def solution(mesh):
    placed = (
        P("grp", None, "own", None),
        P(),
        P(),
        P("own", "grp", None),
        P("own", "grp", None),
        P("own", "grp", None),
        P("own", "grp", None),
        P(None, "own", "grp"),
        P(None, "own", "grp"),
    )
    return jax.shard_map(
        on_device,
        mesh=mesh,
        in_specs=placed,
        out_specs=(
            P(None, "own", "grp"),
            P(None, "own", "grp"),
            P(None, "own", "grp"),
            P("own", "grp", None),
            P("own", "grp", None),
        ),
        check_vma=False,
    )
```

```python
import functools

import jax
import jax.numpy as jnp
from jax import lax
from jax.experimental import pallas as pl
from jax.experimental.pallas import tpu as pltpu
from jax.sharding import PartitionSpec as P

BETA_FIRST = 0.9
BETA_SECOND = 0.95
BIAS_FIRST = 1.0 - 0.9**10
BIAS_SECOND = 1.0 - 0.95**10
ADAM_EPS = 1e-08
STAT_DECAY = 0.95
NORM_EPS = 1e-06
F32 = jnp.float32
BF16 = jnp.bfloat16
ORDER = (
    33, 58, 20, 47, 9, 3, 13, 23, 32, 10, 21, 15, 57, 18, 60, 38,
    49, 11, 52, 31, 40, 34, 61, 55, 0, 27, 53, 46, 24, 2, 28, 54,
    1, 26, 5, 63, 8, 51, 12, 39, 16, 43, 4, 30, 56, 35, 44, 22,
    48, 59, 36, 14, 41, 50, 29, 7, 17, 42, 37, 62, 25, 19, 45, 6,
)
MIB = 1024 * 1024
VMEM = pltpu.VMEM
LONG = pl.CostEstimate(flops=2 * 10**11, bytes_accessed=10**9, transcendentals=0)


def shift(array, step):
    n = lax.axis_size("grp")
    return lax.ppermute(array, "grp", [(i, (i + step) % n) for i in range(n)])


def places_of(assign, n_own, per_owner, order):
    place = [order.index(slot) for slot in range(len(order))]
    key = assign % n_own * per_owner + assign // n_own
    return jnp.asarray(place, jnp.int32)[key]


def in_hbm(array):
    return pltpu.with_memory_space_constraint(array, pltpu.HBM)


def slice_at(array, start, size, axis):
    starts = [start if i == axis else 0 for i in range(array.ndim)]
    sizes = [size if i == axis else n for i, n in enumerate(array.shape)]
    return lax.dynamic_slice(array, starts, sizes, allow_negative_indices=False)


def dot(a, b, dims):
    return lax.dot_general(a, b, (dims, ((), ())), preferred_element_type=F32)


def inside(bounds, block, rows, cols):
    row_off, col_off, n_rows, n_cols = [bounds[4 * block + i] for i in range(4)]
    row, col = lax.axis_index("own") * rows, lax.axis_index("grp") * cols
    return (row < n_rows - row_off) & (col < n_cols - col_off)


def add_kernel(up, far_up, down, far_down, up_out, down_out):
    up_out[...] = (up[...].astype(F32) + far_up[...].astype(F32)).astype(BF16)
    down_out[...] = (down[...].astype(F32) + far_down[...].astype(F32)).astype(BF16)


def add(*arrays):
    shape = jax.ShapeDtypeStruct(arrays[0].shape, BF16)
    return pl.pallas_call(
        add_kernel,
        out_shape=(shape, shape),
        in_specs=[pl.BlockSpec(memory_space=VMEM)] * 4,
        out_specs=(pl.BlockSpec(memory_space=VMEM),) * 2,
        compiler_params=pltpu.CompilerParams(vmem_limit_bytes=4 * MIB),
    )(*arrays)


def roots_kernel(left, right, up, down, own):
    _, units, _, cols = (1, *up.shape)
    rows = up.shape[1]

    def root(half, step):
        col = ((lax.axis_index("grp") + step) & 3) * cols
        col = pl.ds(pl.multiple_of(col, cols), cols)
        return right[0, pl.ds(half * rows, rows), col].astype(BF16)

    for half in range(2):
        own[half] = root(half, 0)
        up[9 + half] = root(half, 1)
        down[9 + half] = root(half, 3)
        for c in range(4):
            unit = left[0, pl.ds(half * rows, rows), pl.ds(c * cols, cols)].astype(BF16)
            up[5 * half + c] = unit
            down[5 - 5 * half + c] = unit
    up[4] = root(0, 2)
    down[4] = root(1, 2)


def root_pieces(left, right):
    _, rows, width = left.shape
    unit = (rows // 2, width // 4)
    return pl.pallas_call(
        roots_kernel,
        out_shape=(
            pltpu.HBM((11, *unit), BF16),
            pltpu.HBM((11, *unit), BF16),
            pltpu.HBM((2, *unit), BF16),
        ),
        grid=(1,),
        in_specs=[pl.BlockSpec(left.shape, lambda i: (0, 0, 0))] * 2,
        out_specs=tuple(pl.BlockSpec((n, *unit), lambda i: (0, 0, 0)) for n in (11, 11, 2)),
        compiler_params=pltpu.CompilerParams(vmem_limit_bytes=8 * MIB),
    )(in_hbm(left), in_hbm(right))


def gather_kernel(own, up_direct, down_direct, first, second, out, first_out, second_out):
    half = up_direct.shape[0]

    def step(i, carry):
        out[0, i] = own[i].astype(F32) + down_direct[i].astype(F32)
        out[1, i] = own[i + half].astype(F32) + up_direct[i].astype(F32)
        return carry

    lax.fori_loop(0, half, step, 0, unroll=4)
    first_out[...] = BETA_FIRST * first[...]
    second_out[...] = BETA_SECOND * second[...]


def gather(own, up_direct, down_direct, first, second):
    shape = jax.ShapeDtypeStruct((2, *up_direct.shape), F32)
    return pl.pallas_call(
        gather_kernel,
        out_shape=(shape,) * 3,
        in_specs=[pl.BlockSpec(memory_space=VMEM)] * 5,
        out_specs=(pl.BlockSpec(memory_space=VMEM),) * 3,
        compiler_params=pltpu.CompilerParams(vmem_limit_bytes=10 * MIB),
        cost_estimate=LONG,
    )(own, up_direct, down_direct, first.reshape(shape.shape), second.reshape(shape.shape))


def pack_kernel(
    key, bounds, partial, up_sum, down_sum, first, second, out, first_out, second_out
):
    _, half, rows, cols = partial.shape
    count = first_out.shape[1]
    begin = pl.program_id(0) * count
    lanes = cols // 2

    def one(side, i, value):
        at = begin + i
        block = side * half + at
        keep = jnp.where(inside(bounds, block, rows, cols), 1.0, 0.0)
        grad = value * keep
        first_next = first[side, at] + (1.0 - BETA_FIRST) * grad
        second_next = second[side, at] + (1.0 - BETA_SECOND) * grad * grad
        first_out[side, i] = first_next
        second_out[side, i] = second_next
        root = second_next * lax.rsqrt(second_next)
        adam = first_next * pl.reciprocal(root + ADAM_EPS * BIAS_SECOND**0.5)
        square = adam * adam
        square = square[:, :lanes] + square[:, lanes:]
        square = (square[: rows // 2] + square[rows // 2 :]) * keep
        piece = jnp.concatenate([grad[:, :lanes], grad[:, lanes:], square], axis=0)
        out[key[block]] = piece.astype(BF16)

    def step(i, carry):
        at = begin + i
        one(0, i, partial[0, at] + up_sum[at].astype(F32))
        one(1, i, partial[1, at] + down_sum[at].astype(F32))
        return carry

    lax.fori_loop(0, count, step, 0, unroll=4)


def pack(key, bounds, partial, up_sum, down_sum, first, second):
    _, half, rows, cols = partial.shape
    blocks, lanes = 2 * half, cols // 2
    steps = 4 if half >= 16 else 1
    moment = pl.BlockSpec((2, half // steps, rows, cols), lambda i, *_: (0, i, 0, 0))
    halves = pltpu.HBM((2, half, rows, cols), F32)
    piece = (blocks, 2 * rows + rows // 2, lanes)
    out, first_next, second_next = pl.pallas_call(
        pack_kernel,
        out_shape=(pltpu.HBM(piece, BF16), halves, halves),
        grid_spec=pltpu.PrefetchScalarGridSpec(
            num_scalar_prefetch=2,
            grid=(steps,),
            in_specs=[pl.BlockSpec(memory_space=VMEM)] * 5,
            out_specs=[pl.BlockSpec(piece, lambda i, *_: (0, 0, 0)), moment, moment],
        ),
        compiler_params=pltpu.CompilerParams(vmem_limit_bytes=14 * MIB),
    )(key, bounds, partial, up_sum, down_sum, first, second)
    shape = (blocks, rows, cols)
    return out, first_next.reshape(shape), second_next.reshape(shape)


def relay_kernel(prev, following, up, down):
    units = up.shape[0]
    up[...] = prev[pl.ds(0, units)]
    down[...] = following[pl.ds(0, units)]


def relay(prev, following):
    shape = jax.ShapeDtypeStruct((5, *prev.shape[1:]), BF16)
    return pl.pallas_call(
        relay_kernel,
        out_shape=(shape, shape),
        in_specs=[pl.BlockSpec(memory_space=VMEM)] * 2,
        out_specs=(pl.BlockSpec(memory_space=VMEM),) * 2,
        compiler_params=pltpu.CompilerParams(vmem_limit_bytes=6 * MIB),
        cost_estimate=LONG,
    )(prev, following)


def unpack_kernel(order, owned, low, high, adam):
    half, rows, cols = low.shape
    total = jnp.zeros(adam.shape, F32)
    for i, place in enumerate(order):
        piece = owned[i].astype(F32)
        value = jnp.concatenate([piece[:rows], piece[rows : 2 * rows]], axis=1).astype(BF16)
        if place < half:
            low[place] = value
        else:
            high[place - half] = value
        total += piece[2 * rows :]
    adam[...] = total


def unpack(order, owned, rows):
    half = owned.shape[0] // 2
    shape = jax.ShapeDtypeStruct((half, rows, 2 * owned.shape[2]), BF16)
    return pl.pallas_call(
        functools.partial(unpack_kernel, order),
        out_shape=(shape, shape, jax.ShapeDtypeStruct((rows // 2, 128), F32)),
        in_specs=[pl.BlockSpec(memory_space=VMEM)],
        out_specs=(pl.BlockSpec(memory_space=VMEM),) * 3,
        compiler_params=pltpu.CompilerParams(vmem_limit_bytes=6 * MIB),
    )(owned)


def finish_kernel(key, bounds, back, out):
    blocks, rows, cols = out.shape

    def step(block, carry):
        ok = inside(bounds, block, rows, cols)
        out[block] = jnp.where(ok, back[key[block]], jnp.zeros((), BF16))
        return carry

    lax.fori_loop(0, blocks, step, 0, unroll=8)


def finish(key, bounds, back):
    whole = pl.BlockSpec(back.shape, lambda i, *_: (0, 0, 0))
    return pl.pallas_call(
        finish_kernel,
        out_shape=jax.ShapeDtypeStruct(back.shape, BF16),
        grid_spec=pltpu.PrefetchScalarGridSpec(
            num_scalar_prefetch=2, grid=(1,), in_specs=[whole], out_specs=whole
        ),
        compiler_params=pltpu.CompilerParams(vmem_limit_bytes=6 * MIB),
    )(key, bounds, back)


def precond_kernel(*refs):
    pieces, adam, sources, (out, norms) = refs[:8], refs[8], refs[9:15], refs[15:17]
    mixed, held, sems = refs[17], refs[18:24], refs[24]
    width, quarter = out.shape
    half = width // 2
    me = lax.axis_index("grp")
    n = width // quarter
    copies = [
        pltpu.make_async_copy(source, place, sems.at[i])
        for i, (source, place) in enumerate(zip(sources, held))
    ]
    for copy in copies:
        copy.start()
    root, up, up_prev, down_next, up_far, down_far = held
    for copy in copies:
        copy.wait()
    right = jnp.concatenate(
        [
            root[0],
            root[1],
            down_next[9],
            down_next[10],
            up_far[4],
            down_far[4],
            up_prev[9],
            up_prev[10],
        ],
        axis=0,
    )
    for row in range(0, width, quarter):
        parts = [ref[pl.ds(row % half, quarter), :] for ref in pieces[row // half :: 2]]
        value = dot(jnp.concatenate(parts, axis=1), right, ((1,), (0,)))
        mixed[pl.ds(row, quarter), :] = value.astype(BF16)
    square = jnp.zeros((8, quarter), F32)
    for step, (low, first), (high, second) in (
        (0, (up, 0), (up, 5)),
        (1, (down_next, 5), (down_next, 0)),
        (2, (up_far, 0), (down_far, 0)),
        (3, (up_prev, 0), (up_prev, 5)),
    ):
        units = [jnp.concatenate([low[first + c], high[second + c]], axis=0) for c in range(n)]
        value = dot(jnp.concatenate(units, axis=1), mixed[...], ((1,), (0,)))
        base = ((me + step) & (n - 1)) * quarter
        out[pl.ds(pl.multiple_of(base, quarter), quarter), :] = value
        square += jnp.sum((value * value).reshape(quarter // 8, 8, quarter), axis=0)
    norms[...] = jnp.zeros_like(norms)
    norms[0:1, :] = jnp.broadcast_to(jnp.sum(square), (1, 128))
    norms[1:2, :] = jnp.broadcast_to(jnp.sum(adam[...]), (1, 128))


def precondition(pieces, adam, sources):
    rows, quarter = pieces[0].shape
    operands = (*pieces, adam)
    return pl.pallas_call(
        precond_kernel,
        out_shape=(
            jax.ShapeDtypeStruct((2 * rows, quarter), F32),
            jax.ShapeDtypeStruct((8, 128), F32),
        ),
        in_specs=[pl.BlockSpec(memory_space=VMEM)] * len(operands)
        + [pl.BlockSpec(memory_space=pl.ANY)] * len(sources),
        out_specs=(pl.BlockSpec(memory_space=VMEM),) * 2,
        scratch_shapes=[
            VMEM((2 * rows, quarter), BF16),
            *[VMEM(source.shape, BF16) for source in sources],
            pltpu.SemaphoreType.DMA((len(sources),)),
        ],
        compiler_params=pltpu.CompilerParams(vmem_limit_bytes=14 * MIB),
    )(*operands, *map(in_hbm, sources))


def graft_kernel(cells, order, precond, first, second, third, fourth, out):
    sums = first[...] + second[...] + third[...] + fourth[...]
    pre, adam = sums[0:1, :], sums[1:2, :]
    adam = adam * (BIAS_SECOND / (BIAS_FIRST * BIAS_FIRST))
    scale = -jnp.sqrt(adam / cells) / jnp.sqrt(pre / cells + NORM_EPS)
    _, rows, quarter = out.shape
    scale = jnp.concatenate([scale] * (quarter // 128), axis=1)
    for i, place in enumerate(order):
        out[i] = (scale * precond[pl.ds(place * rows, rows), :]).astype(BF16)


def graft(order, precond, norms):
    width, quarter = precond.shape
    shape = (len(order), width // len(order), quarter)
    small = pl.BlockSpec((8, 128), lambda i: (0, 0))
    return pl.pallas_call(
        functools.partial(graft_kernel, float(width * width), order),
        out_shape=pltpu.HBM(shape, BF16),
        grid=(1,),
        in_specs=[pl.BlockSpec((width, quarter), lambda i: (0, 0))] + [small] * 4,
        out_specs=pl.BlockSpec(shape, lambda i: (0, 0, 0)),
        compiler_params=pltpu.CompilerParams(vmem_limit_bytes=8 * MIB),
    )(precond, *norms)


def on_device(
    grad_parts,
    assign,
    block_bounds,
    left_root,
    right_root,
    left_stat,
    right_stat,
    first_moment,
    second_moment,
):
    n_own = lax.axis_size("own")
    n_grp = lax.axis_size("grp")
    grp_index = lax.axis_index("grp")
    total_blocks = assign.shape[0]
    per_owner = total_blocks // n_own
    shard_rows = grad_parts.shape[2]
    width = grad_parts.shape[3]
    quarter = width // n_grp
    half = total_blocks // 2
    starts = [((grp_index + step) & (n_grp - 1)) * quarter for step in range(4)]
    turn = ((n_grp - grp_index) & (n_grp - 1)) * quarter
    grad_parts, starts, turn = lax.optimization_barrier((grad_parts, starts, turn))

    def columns(array, step):
        return slice_at(array, starts[step], quarter, array.ndim - 1)

    part = grad_parts[0]
    order = ORDER if len(ORDER) == n_own else tuple(range(n_own))

    def exchange(array):
        groups = [list(order)]
        return lax.all_to_all(array, "own", 0, 0, axis_index_groups=groups, tiled=True)

    far = columns(part, 2)
    far_low, far_high = lax.optimization_barrier((far[:half], far[half:]))
    far_up = shift(far_low, 1)
    far_down = shift(far_high, -1)
    later, left_root, right_root, _, _ = lax.optimization_barrier(
        (part, left_root, right_root, far_low, far_high)
    )
    up, down = columns(later, 1), columns(later, 3)
    up_low, up_high, down_low, down_high, own = lax.optimization_barrier(
        (up[:half], up[half:], down[:half], down[half:], columns(later, 0))
    )
    up_direct = shift(up_high, 1)
    down_direct = shift(down_low, -1)
    up_sum, down_sum = add(up_low, far_up, down_high, far_down)
    up_sum = shift(up_sum, 1)
    down_sum = shift(down_sum, -1)
    key, bounds = places_of(assign, n_own, per_owner, order), block_bounds.reshape(-1)
    roots_up, roots_down, root_own = root_pieces(left_root, right_root)
    up_direct, down_direct, key, bounds, roots_up, roots_down, root_own = lax.optimization_barrier(
        (up_direct, down_direct, key, bounds, roots_up, roots_down, root_own)
    )
    partial, first, second = gather(own, up_direct, down_direct, first_moment, second_moment)

    roots_up, roots_down, up_sum, down_sum, partial = lax.optimization_barrier(
        (roots_up, roots_down, up_sum, down_sum, partial)
    )
    sorted_grad, first_next, second_next = pack(
        key, bounds, partial, up_sum, down_sum, first, second
    )
    owned = exchange(sorted_grad)
    roots_prev = shift(roots_up, 1)
    roots_next = shift(roots_down, -1)
    onward = relay(roots_prev, roots_next)
    far_roots = [shift(onward[0], 1), shift(onward[1], -1)]
    roots = [root_own, roots_up, roots_prev, roots_next, *far_roots]

    owned, roots = lax.optimization_barrier((owned, roots))
    low, high, adam = unpack(order, owned, shard_rows)
    prev_low = shift(low, 1)
    next_high = shift(high, -1)
    prev_high = shift(high, 1)
    next_low = shift(low, -1)
    far_low = shift(prev_low, 1)
    far_high = shift(next_high, -1)
    pieces = [low, high, next_low, next_high, far_low, far_high, prev_low, prev_high]
    flat = [piece.reshape(-1, quarter) for piece in pieces]
    precond, norms = precondition(flat, adam, roots)
    norms = [norms] + [shift(norms, step) for step in (1, 2, 3)]
    grafted = graft(order, precond, norms)
    pieces, grafted, assign, bounds = lax.optimization_barrier(
        (pieces, grafted, assign, block_bounds)
    )
    key, bounds = places_of(assign, n_own, per_owner, order), bounds.reshape(-1)
    back = exchange(grafted)

    whole = jnp.concatenate(
        [jnp.concatenate(pieces[i : i + 2]) for i in (0, 2, 4, 6)], axis=2
    ).reshape(width, width)
    rows = slice_at(whole, starts[0], quarter, 0)
    left_acc = STAT_DECAY * left_stat + dot(rows, whole, ((1,), (1,)))[None]
    cross = dot(whole[:, :quarter], whole, ((0,), (0,)))
    cross = jnp.concatenate([cross, cross], axis=1)
    cross = slice_at(cross, turn, width, 1)
    right_acc = STAT_DECAY * right_stat + cross[None]

    update = finish(key, bounds, back)
    return (update, first_next, second_next, left_acc, right_acc)


def solution(mesh):
    placed = (
        P("grp", None, "own", None),
        P(),
        P(),
        P("own", "grp", None),
        P("own", "grp", None),
        P("own", "grp", None),
        P("own", "grp", None),
        P(None, "own", "grp"),
        P(None, "own", "grp"),
    )
    return jax.shard_map(
        on_device,
        mesh=mesh,
        in_specs=placed,
        out_specs=(
            P(None, "own", "grp"),
            P(None, "own", "grp"),
            P(None, "own", "grp"),
            P("own", "grp", None),
            P("own", "grp", None),
        ),
        check_vma=False,
    )
```

```python
import functools

import jax
import jax.numpy as jnp
from jax import lax
from jax.experimental import pallas as pl
from jax.experimental.pallas import tpu as pltpu
from jax.sharding import PartitionSpec as P

BETA_FIRST = 0.9
BETA_SECOND = 0.95
BIAS_FIRST = 1.0 - 0.9**10
BIAS_SECOND = 1.0 - 0.95**10
ADAM_EPS = 1e-08
STAT_DECAY = 0.95
NORM_EPS = 1e-06
F32 = jnp.float32
BF16 = jnp.bfloat16
ORDER = (
    33, 58, 20, 47, 9, 3, 13, 23, 32, 10, 21, 15, 57, 18, 60, 38,
    49, 11, 52, 31, 40, 34, 61, 55, 0, 27, 53, 46, 24, 2, 28, 54,
    1, 26, 5, 63, 8, 51, 12, 39, 16, 43, 4, 30, 56, 35, 44, 22,
    48, 59, 36, 14, 41, 50, 29, 7, 17, 42, 37, 62, 25, 19, 45, 6,
)
MIB = 1024 * 1024
VMEM = pltpu.VMEM
LONG = pl.CostEstimate(flops=2 * 10**11, bytes_accessed=10**9, transcendentals=0)


def shift(array, step):
    n = lax.axis_size("grp")
    return lax.ppermute(array, "grp", [(i, (i + step) % n) for i in range(n)])


def places_of(assign, n_own, per_owner, order):
    place = [order.index(slot) for slot in range(len(order))]
    key = assign % n_own * per_owner + assign // n_own
    return jnp.asarray(place, jnp.int32)[key]


def in_hbm(array):
    return pltpu.with_memory_space_constraint(array, pltpu.HBM)


def slice_at(array, start, size, axis):
    starts = [start if i == axis else 0 for i in range(array.ndim)]
    sizes = [size if i == axis else n for i, n in enumerate(array.shape)]
    return lax.dynamic_slice(array, starts, sizes, allow_negative_indices=False)


def dot(a, b, dims):
    return lax.dot_general(a, b, (dims, ((), ())), preferred_element_type=F32)


def inside(bounds, rows, cols):
    row, col = lax.axis_index("own") * rows, lax.axis_index("grp") * cols
    ok = (row < bounds[:, 2] - bounds[:, 0]) & (col < bounds[:, 3] - bounds[:, 1])
    return ok.astype(jnp.int32)


def add_kernel(up, far_up, down, far_down, up_out, down_out):
    up_out[...] = (up[...].astype(F32) + far_up[...].astype(F32)).astype(BF16)
    down_out[...] = (down[...].astype(F32) + far_down[...].astype(F32)).astype(BF16)


def add(*arrays):
    shape = jax.ShapeDtypeStruct(arrays[0].shape, BF16)
    return pl.pallas_call(
        add_kernel,
        out_shape=(shape, shape),
        in_specs=[pl.BlockSpec(memory_space=VMEM)] * 4,
        out_specs=(pl.BlockSpec(memory_space=VMEM),) * 2,
        compiler_params=pltpu.CompilerParams(vmem_limit_bytes=4 * MIB),
    )(*arrays)


def roots_kernel(left, right, up, down, own):
    _, units, _, cols = (1, *up.shape)
    rows = up.shape[1]

    def root(half, step):
        col = ((lax.axis_index("grp") + step) & 3) * cols
        col = pl.ds(pl.multiple_of(col, cols), cols)
        return right[0, pl.ds(half * rows, rows), col].astype(BF16)

    for half in range(2):
        own[half] = root(half, 0)
        up[9 + half] = root(half, 1)
        down[9 + half] = root(half, 3)
        for c in range(4):
            unit = left[0, pl.ds(half * rows, rows), pl.ds(c * cols, cols)].astype(BF16)
            up[5 * half + c] = unit
            down[5 - 5 * half + c] = unit
    up[4] = root(0, 2)
    down[4] = root(1, 2)


def root_pieces(left, right):
    _, rows, width = left.shape
    unit = (rows // 2, width // 4)
    return pl.pallas_call(
        roots_kernel,
        out_shape=(
            pltpu.HBM((11, *unit), BF16),
            pltpu.HBM((11, *unit), BF16),
            pltpu.HBM((2, *unit), BF16),
        ),
        grid=(1,),
        in_specs=[pl.BlockSpec(left.shape, lambda i: (0, 0, 0))] * 2,
        out_specs=tuple(pl.BlockSpec((n, *unit), lambda i: (0, 0, 0)) for n in (11, 11, 2)),
        compiler_params=pltpu.CompilerParams(vmem_limit_bytes=8 * MIB),
    )(in_hbm(left), in_hbm(right))


def gather_kernel(own, up_direct, down_direct, first, second, out, first_out, second_out):
    half = up_direct.shape[0]

    def step(i, carry):
        out[0, i] = own[i].astype(F32) + down_direct[i].astype(F32)
        out[1, i] = own[i + half].astype(F32) + up_direct[i].astype(F32)
        return carry

    lax.fori_loop(0, half, step, 0, unroll=4)
    first_out[...] = BETA_FIRST * first[...]
    second_out[...] = BETA_SECOND * second[...]


def gather(own, up_direct, down_direct, first, second):
    shape = jax.ShapeDtypeStruct((2, *up_direct.shape), F32)
    return pl.pallas_call(
        gather_kernel,
        out_shape=(shape,) * 3,
        in_specs=[pl.BlockSpec(memory_space=VMEM)] * 5,
        out_specs=(pl.BlockSpec(memory_space=VMEM),) * 3,
        compiler_params=pltpu.CompilerParams(vmem_limit_bytes=10 * MIB),
        cost_estimate=LONG,
    )(own, up_direct, down_direct, first.reshape(shape.shape), second.reshape(shape.shape))


def pack_kernel(
    key, flags, partial, up_sum, down_sum, first, second, out, first_out, second_out
):
    _, half, rows, cols = partial.shape
    count = first_out.shape[1]
    begin = pl.program_id(0) * count
    lanes = cols // 2

    def one(side, i, value):
        at = begin + i
        block = side * half + at
        keep = flags[block].astype(F32)
        grad = value * keep
        first_next = first[side, at] + (1.0 - BETA_FIRST) * grad
        second_next = second[side, at] + (1.0 - BETA_SECOND) * grad * grad
        first_out[side, i] = first_next
        second_out[side, i] = second_next
        root = second_next * lax.rsqrt(second_next)
        adam = first_next * pl.reciprocal(root + ADAM_EPS * BIAS_SECOND**0.5)
        square = adam * adam
        square = square[:, :lanes] + square[:, lanes:]
        square = (square[: rows // 2] + square[rows // 2 :]) * keep
        piece = jnp.concatenate([grad[:, :lanes], grad[:, lanes:], square], axis=0)
        out[key[block]] = piece.astype(BF16)

    def step(i, carry):
        at = begin + i
        one(0, i, partial[0, at] + up_sum[at].astype(F32))
        one(1, i, partial[1, at] + down_sum[at].astype(F32))
        return carry

    lax.fori_loop(0, count, step, 0, unroll=4)


def pack(key, flags, partial, up_sum, down_sum, first, second):
    _, half, rows, cols = partial.shape
    blocks, lanes = 2 * half, cols // 2
    steps = 2 if half >= 16 else 1
    moment = pl.BlockSpec((2, half // steps, rows, cols), lambda i, *_: (0, i, 0, 0))
    halves = pltpu.HBM((2, half, rows, cols), F32)
    piece = (blocks, 2 * rows + rows // 2, lanes)
    out, first_next, second_next = pl.pallas_call(
        pack_kernel,
        out_shape=(pltpu.HBM(piece, BF16), halves, halves),
        grid_spec=pltpu.PrefetchScalarGridSpec(
            num_scalar_prefetch=2,
            grid=(steps,),
            in_specs=[pl.BlockSpec(memory_space=VMEM)] * 5,
            out_specs=[pl.BlockSpec(piece, lambda i, *_: (0, 0, 0)), moment, moment],
        ),
        compiler_params=pltpu.CompilerParams(vmem_limit_bytes=16 * MIB),
    )(key, flags, partial, up_sum, down_sum, first, second)
    shape = (blocks, rows, cols)
    return out, first_next.reshape(shape), second_next.reshape(shape)


def relay_kernel(prev, following, up, down):
    units = up.shape[0]
    up[...] = prev[pl.ds(0, units)]
    down[...] = following[pl.ds(0, units)]


def relay(prev, following):
    shape = jax.ShapeDtypeStruct((5, *prev.shape[1:]), BF16)
    return pl.pallas_call(
        relay_kernel,
        out_shape=(shape, shape),
        in_specs=[pl.BlockSpec(memory_space=VMEM)] * 2,
        out_specs=(pl.BlockSpec(memory_space=VMEM),) * 2,
        compiler_params=pltpu.CompilerParams(vmem_limit_bytes=6 * MIB),
        cost_estimate=LONG,
    )(prev, following)


def unpack_kernel(order, owned, low, high, adam):
    half, rows, cols = low.shape
    total = jnp.zeros(adam.shape, F32)
    for i, place in enumerate(order):
        piece = owned[i].astype(F32)
        value = jnp.concatenate([piece[:rows], piece[rows : 2 * rows]], axis=1).astype(BF16)
        if place < half:
            low[place] = value
        else:
            high[place - half] = value
        total += piece[2 * rows :]
    adam[...] = total


def unpack(order, owned, rows):
    half = owned.shape[0] // 2
    shape = jax.ShapeDtypeStruct((half, rows, 2 * owned.shape[2]), BF16)
    return pl.pallas_call(
        functools.partial(unpack_kernel, order),
        out_shape=(shape, shape, jax.ShapeDtypeStruct((rows // 2, 128), F32)),
        in_specs=[pl.BlockSpec(memory_space=VMEM)],
        out_specs=(pl.BlockSpec(memory_space=VMEM),) * 3,
        compiler_params=pltpu.CompilerParams(vmem_limit_bytes=6 * MIB),
    )(owned)


def finish_kernel(key, flags, back, out):
    count, rows, cols = out.shape
    begin = pl.program_id(0) * count

    def step(i, carry):
        block = begin + i
        out[i] = jnp.where(flags[block] != 0, back[key[block]], jnp.zeros((), BF16))
        return carry

    lax.fori_loop(0, count, step, 0, unroll=8)


def finish(key, flags, back):
    blocks, rows, cols = back.shape
    steps = 2 if blocks >= 16 else 1
    return pl.pallas_call(
        finish_kernel,
        out_shape=jax.ShapeDtypeStruct(back.shape, BF16),
        grid_spec=pltpu.PrefetchScalarGridSpec(
            num_scalar_prefetch=2,
            grid=(steps,),
            in_specs=[pl.BlockSpec(memory_space=VMEM)],
            out_specs=pl.BlockSpec((blocks // steps, rows, cols), lambda i, *_: (i, 0, 0)),
        ),
        compiler_params=pltpu.CompilerParams(vmem_limit_bytes=6 * MIB),
    )(key, flags, back)


def precond_kernel(*refs):
    pieces, adam, sources, (out, norms) = refs[:8], refs[8], refs[9:15], refs[15:17]
    mixed, held, sems = refs[17], refs[18:24], refs[24]
    width, quarter = out.shape
    half = width // 2
    me = lax.axis_index("grp")
    n = width // quarter
    root, up, up_prev, down_next, up_far, down_far = held
    cuts = [(0, 0, 2), (2, 9, 2), (3, 9, 2), (4, 4, 1), (5, 4, 1)]
    cuts += [(1, 0, 9), (3, 0, 9), (4, 0, 4), (5, 0, 4), (2, 0, 9)]
    copies = []
    for i, (which, first, count) in enumerate(cuts):
        units = pl.ds(first, count)
        source, place = sources[which].at[units], held[which].at[units]
        copies.append(pltpu.make_async_copy(source, place, sems.at[i]))
    for copy in copies:
        copy.start()
    for copy in copies[:5]:
        copy.wait()
    right = jnp.concatenate(
        [
            root[0],
            root[1],
            down_next[9],
            down_next[10],
            up_far[4],
            down_far[4],
            up_prev[9],
            up_prev[10],
        ],
        axis=0,
    )
    for row in range(0, width, quarter):
        parts = [ref[pl.ds(row % half, quarter), :] for ref in pieces[row // half :: 2]]
        value = dot(jnp.concatenate(parts, axis=1), right, ((1,), (0,)))
        mixed[pl.ds(row, quarter), :] = value.astype(BF16)
    for copy in copies[5:]:
        copy.wait()
    square = jnp.zeros((8, quarter), F32)
    for step, (low, first), (high, second) in (
        (0, (up, 0), (up, 5)),
        (1, (down_next, 5), (down_next, 0)),
        (2, (up_far, 0), (down_far, 0)),
        (3, (up_prev, 0), (up_prev, 5)),
    ):
        units = [jnp.concatenate([low[first + c], high[second + c]], axis=0) for c in range(n)]
        value = dot(jnp.concatenate(units, axis=1), mixed[...], ((1,), (0,)))
        base = ((me + step) & (n - 1)) * quarter
        out[pl.ds(pl.multiple_of(base, quarter), quarter), :] = value
        square += jnp.sum((value * value).reshape(quarter // 8, 8, quarter), axis=0)
    norms[...] = jnp.zeros_like(norms)
    norms[0:1, :] = jnp.broadcast_to(jnp.sum(square), (1, 128))
    norms[1:2, :] = jnp.broadcast_to(jnp.sum(adam[...]), (1, 128))


def precondition(pieces, adam, sources):
    rows, quarter = pieces[0].shape
    operands = (*pieces, adam)
    return pl.pallas_call(
        precond_kernel,
        out_shape=(
            jax.ShapeDtypeStruct((2 * rows, quarter), F32),
            jax.ShapeDtypeStruct((8, 128), F32),
        ),
        in_specs=[pl.BlockSpec(memory_space=VMEM)] * len(operands)
        + [pl.BlockSpec(memory_space=pl.ANY)] * len(sources),
        out_specs=(pl.BlockSpec(memory_space=VMEM),) * 2,
        scratch_shapes=[
            VMEM((2 * rows, quarter), BF16),
            *[VMEM(source.shape, BF16) for source in sources],
            pltpu.SemaphoreType.DMA((10,)),
        ],
        compiler_params=pltpu.CompilerParams(vmem_limit_bytes=14 * MIB),
    )(*operands, *map(in_hbm, sources))


def graft_kernel(cells, order, precond, mine, other, out):
    sums = mine[...] + other[...]
    pre, adam = sums[0:1, :], sums[1:2, :]
    adam = adam * (BIAS_SECOND / (BIAS_FIRST * BIAS_FIRST))
    scale = -jnp.sqrt(adam / cells) / jnp.sqrt(pre / cells + NORM_EPS)
    _, rows, quarter = out.shape
    scale = jnp.concatenate([scale] * (quarter // 128), axis=1)
    for i, place in enumerate(order):
        out[i] = (scale * precond[pl.ds(place * rows, rows), :]).astype(BF16)


def graft(order, precond, mine, other):
    width, quarter = precond.shape
    shape = (len(order), width // len(order), quarter)
    small = pl.BlockSpec((8, 128), lambda i: (0, 0))
    return pl.pallas_call(
        functools.partial(graft_kernel, float(width * width), order),
        out_shape=pltpu.HBM(shape, BF16),
        grid=(1,),
        in_specs=[pl.BlockSpec((width, quarter), lambda i: (0, 0))] + [small] * 2,
        out_specs=pl.BlockSpec(shape, lambda i: (0, 0, 0)),
        compiler_params=pltpu.CompilerParams(vmem_limit_bytes=8 * MIB),
    )(precond, mine, other)


def on_device(
    grad_parts,
    assign,
    block_bounds,
    left_root,
    right_root,
    left_stat,
    right_stat,
    first_moment,
    second_moment,
):
    n_own = lax.axis_size("own")
    n_grp = lax.axis_size("grp")
    grp_index = lax.axis_index("grp")
    total_blocks = assign.shape[0]
    per_owner = total_blocks // n_own
    shard_rows = grad_parts.shape[2]
    width = grad_parts.shape[3]
    quarter = width // n_grp
    half = total_blocks // 2
    starts = [((grp_index + step) & (n_grp - 1)) * quarter for step in range(4)]
    turn = ((n_grp - grp_index) & (n_grp - 1)) * quarter
    grad_parts, starts, turn = lax.optimization_barrier((grad_parts, starts, turn))

    def columns(array, step):
        return slice_at(array, starts[step], quarter, array.ndim - 1)

    part = grad_parts[0]
    order = ORDER if len(ORDER) == n_own else tuple(range(n_own))

    def exchange(array):
        groups = [list(order)]
        return lax.all_to_all(array, "own", 0, 0, axis_index_groups=groups, tiled=True)

    far = columns(part, 2)
    far_low, far_high = lax.optimization_barrier((far[:half], far[half:]))
    far_up = shift(far_low, 1)
    far_down = shift(far_high, -1)
    later, _, _ = lax.optimization_barrier((part, far_low, far_high))
    up, down = columns(later, 1), columns(later, 3)
    up_low, up_high, down_low, down_high = lax.optimization_barrier(
        (up[:half], up[half:], down[:half], down[half:])
    )
    up_direct = shift(up_high, 1)
    down_direct = shift(down_low, -1)
    up_sum, down_sum = add(up_low, far_up, down_high, far_down)
    up_sum, down_sum, left_root, right_root, later = lax.optimization_barrier(
        (up_sum, down_sum, left_root, right_root, part)
    )
    own = columns(later, 0)
    up_sum = shift(up_sum, 1)
    down_sum = shift(down_sum, -1)
    key = places_of(assign, n_own, per_owner, order)
    flags = inside(block_bounds, shard_rows, quarter)
    roots_up, roots_down, root_own = root_pieces(left_root, right_root)
    up_direct, down_direct, key, flags, roots_up, roots_down, root_own = lax.optimization_barrier(
        (up_direct, down_direct, key, flags, roots_up, roots_down, root_own)
    )
    partial, first, second = gather(own, up_direct, down_direct, first_moment, second_moment)

    roots_up, roots_down, up_sum, down_sum, partial = lax.optimization_barrier(
        (roots_up, roots_down, up_sum, down_sum, partial)
    )
    sorted_grad, first_next, second_next = pack(
        key, flags, partial, up_sum, down_sum, first, second
    )
    owned = exchange(sorted_grad)
    roots_prev = shift(roots_up, 1)
    roots_next = shift(roots_down, -1)
    onward = relay(roots_prev, roots_next)
    far_roots = [shift(onward[0], 1), shift(onward[1], -1)]
    roots = [root_own, roots_up, roots_prev, roots_next, *far_roots]

    owned, roots = lax.optimization_barrier((owned, roots))
    low, high, adam = unpack(order, owned, shard_rows)
    prev_low = shift(low, 1)
    next_high = shift(high, -1)
    prev_high = shift(high, 1)
    next_low = shift(low, -1)
    far_low = shift(prev_low, 1)
    far_high = shift(next_high, -1)
    pieces = [low, high, next_low, next_high, far_low, far_high, prev_low, prev_high]
    flat = [piece.reshape(-1, quarter) for piece in pieces]
    precond, norms = precondition(flat, adam, roots)
    norms += lax.ppermute(norms, "grp", [(i, i ^ 1) for i in range(n_grp)])
    others = lax.ppermute(norms, "grp", [(i, i ^ 2) for i in range(n_grp)])
    grafted = graft(order, precond, norms, others)
    pieces, grafted = lax.optimization_barrier((pieces, grafted))
    back = exchange(grafted)

    whole = jnp.concatenate(
        [jnp.concatenate(pieces[i : i + 2]) for i in (0, 2, 4, 6)], axis=2
    ).reshape(width, width)
    rows = slice_at(whole, starts[0], quarter, 0)
    left_acc = STAT_DECAY * left_stat + dot(rows, whole, ((1,), (1,)))[None]
    cross = dot(whole[:, :quarter], whole, ((0,), (0,)))
    cross = jnp.concatenate([cross, cross], axis=1)
    cross = slice_at(cross, turn, width, 1)
    right_acc = STAT_DECAY * right_stat + cross[None]

    update = finish(key, flags, back)
    return (update, first_next, second_next, left_acc, right_acc)


def solution(mesh):
    placed = (
        P("grp", None, "own", None),
        P(),
        P(),
        P("own", "grp", None),
        P("own", "grp", None),
        P("own", "grp", None),
        P("own", "grp", None),
        P(None, "own", "grp"),
        P(None, "own", "grp"),
    )
    return jax.shard_map(
        on_device,
        mesh=mesh,
        in_specs=placed,
        out_specs=(
            P(None, "own", "grp"),
            P(None, "own", "grp"),
            P(None, "own", "grp"),
            P("own", "grp", None),
            P("own", "grp", None),
        ),
        check_vma=False,
    )
```

```python
import functools

import jax
import jax.numpy as jnp
from jax import lax
from jax.experimental import pallas as pl
from jax.experimental.pallas import tpu as pltpu
from jax.sharding import PartitionSpec as P

BETA_FIRST = 0.9
BETA_SECOND = 0.95
BIAS_FIRST = 1.0 - 0.9**10
BIAS_SECOND = 1.0 - 0.95**10
ADAM_EPS = 1e-08
STAT_DECAY = 0.95
NORM_EPS = 1e-06
F32 = jnp.float32
BF16 = jnp.bfloat16
ORDER = (
    33, 58, 20, 47, 9, 3, 13, 23, 32, 10, 21, 15, 57, 18, 60, 38,
    49, 11, 52, 31, 40, 34, 61, 55, 0, 27, 53, 46, 24, 2, 28, 54,
    1, 26, 5, 63, 8, 51, 12, 39, 16, 43, 4, 30, 56, 35, 44, 22,
    48, 59, 36, 14, 41, 50, 29, 7, 17, 42, 37, 62, 25, 19, 45, 6,
)
MIB = 1024 * 1024
VMEM = pltpu.VMEM
LONG = pl.CostEstimate(flops=2 * 10**11, bytes_accessed=10**9, transcendentals=0)


def shift(array, step):
    n = lax.axis_size("grp")
    return lax.ppermute(array, "grp", [(i, (i + step) % n) for i in range(n)])


def places_of(assign, n_own, per_owner, order):
    place = [order.index(slot) for slot in range(len(order))]
    key = assign % n_own * per_owner + assign // n_own
    return jnp.asarray(place, jnp.int32)[key]


def in_hbm(array):
    return pltpu.with_memory_space_constraint(array, pltpu.HBM)


def slice_at(array, start, size, axis):
    starts = [start if i == axis else 0 for i in range(array.ndim)]
    sizes = [size if i == axis else n for i, n in enumerate(array.shape)]
    return lax.dynamic_slice(array, starts, sizes, allow_negative_indices=False)


def dot(a, b, dims):
    return lax.dot_general(a, b, (dims, ((), ())), preferred_element_type=F32)


def inside(bounds, rows, cols):
    row, col = lax.axis_index("own") * rows, lax.axis_index("grp") * cols
    ok = (row < bounds[:, 2] - bounds[:, 0]) & (col < bounds[:, 3] - bounds[:, 1])
    return ok.astype(jnp.int32)


def add_kernel(up, far_up, down, far_down, up_out, down_out):
    up_out[...] = (up[...].astype(F32) + far_up[...].astype(F32)).astype(BF16)
    down_out[...] = (down[...].astype(F32) + far_down[...].astype(F32)).astype(BF16)


def add(*arrays):
    shape = jax.ShapeDtypeStruct(arrays[0].shape, BF16)
    return pl.pallas_call(
        add_kernel,
        out_shape=(shape, shape),
        in_specs=[pl.BlockSpec(memory_space=VMEM)] * 4,
        out_specs=(pl.BlockSpec(memory_space=VMEM),) * 2,
        compiler_params=pltpu.CompilerParams(vmem_limit_bytes=4 * MIB),
    )(*arrays)


def roots_kernel(left, right, up, down, own):
    _, units, _, cols = (1, *up.shape)
    rows = up.shape[1]

    def root(half, step):
        col = ((lax.axis_index("grp") + step) & 3) * cols
        col = pl.ds(pl.multiple_of(col, cols), cols)
        return right[0, pl.ds(half * rows, rows), col].astype(BF16)

    for half in range(2):
        own[half] = root(half, 0)
        up[9 + half] = root(half, 1)
        down[9 + half] = root(half, 3)
        for c in range(4):
            unit = left[0, pl.ds(half * rows, rows), pl.ds(c * cols, cols)].astype(BF16)
            up[5 * half + c] = unit
            down[5 - 5 * half + c] = unit
    up[4] = root(0, 2)
    down[4] = root(1, 2)


def root_pieces(left, right):
    _, rows, width = left.shape
    unit = (rows // 2, width // 4)
    return pl.pallas_call(
        roots_kernel,
        out_shape=(
            pltpu.HBM((11, *unit), BF16),
            pltpu.HBM((11, *unit), BF16),
            pltpu.HBM((2, *unit), BF16),
        ),
        grid=(1,),
        in_specs=[pl.BlockSpec(left.shape, lambda i: (0, 0, 0))] * 2,
        out_specs=tuple(pl.BlockSpec((n, *unit), lambda i: (0, 0, 0)) for n in (11, 11, 2)),
        compiler_params=pltpu.CompilerParams(vmem_limit_bytes=8 * MIB),
        cost_estimate=LONG,
    )(in_hbm(left), in_hbm(right))


def gather_kernel(own, up_direct, down_direct, first, second, out, first_out, second_out):
    half = up_direct.shape[0]

    def step(i, carry):
        out[0, i] = own[i].astype(F32) + down_direct[i].astype(F32)
        out[1, i] = own[i + half].astype(F32) + up_direct[i].astype(F32)
        return carry

    lax.fori_loop(0, half, step, 0, unroll=4)
    first_out[...] = BETA_FIRST * first[...]
    second_out[...] = BETA_SECOND * second[...]


def gather(own, up_direct, down_direct, first, second):
    shape = jax.ShapeDtypeStruct((2, *up_direct.shape), F32)
    return pl.pallas_call(
        gather_kernel,
        out_shape=(shape,) * 3,
        in_specs=[pl.BlockSpec(memory_space=VMEM)] * 5,
        out_specs=(pl.BlockSpec(memory_space=VMEM),) * 3,
        compiler_params=pltpu.CompilerParams(vmem_limit_bytes=10 * MIB),
    )(own, up_direct, down_direct, first.reshape(shape.shape), second.reshape(shape.shape))


def pack_kernel(
    key, flags, partial, up_sum, down_sum, first, second, out, squares, first_out, second_out
):
    _, half, rows, cols = partial.shape
    count = first_out.shape[1]
    begin = pl.program_id(0) * count
    lanes = cols // 2

    def one(side, i, value):
        at = begin + i
        block = side * half + at
        keep = flags[block].astype(F32)
        grad = value * keep
        first_next = first[side, at] + (1.0 - BETA_FIRST) * grad
        second_next = second[side, at] + (1.0 - BETA_SECOND) * grad * grad
        first_out[side, i] = first_next
        second_out[side, i] = second_next
        root = second_next * lax.rsqrt(second_next)
        adam = first_next * pl.reciprocal(root + ADAM_EPS * BIAS_SECOND**0.5)
        square = adam * adam
        square = square[:, :lanes] + square[:, lanes:]
        square = (square[: rows // 2] + square[rows // 2 :]) * keep
        place = key[block]
        out[place] = grad.astype(BF16)
        squares[place] = square

    def step(i, carry):
        at = begin + i
        one(0, i, partial[0, at] + up_sum[at].astype(F32))
        one(1, i, partial[1, at] + down_sum[at].astype(F32))
        return carry

    lax.fori_loop(0, count, step, 0, unroll=4)


def pack(key, flags, partial, up_sum, down_sum, first, second):
    _, half, rows, cols = partial.shape
    blocks, lanes = 2 * half, cols // 2
    steps = 2 if half >= 16 else 1
    moment = pl.BlockSpec((2, half // steps, rows, cols), lambda i, *_: (0, i, 0, 0))
    halves = pltpu.HBM((2, half, rows, cols), F32)
    piece, tile = (blocks, rows, cols), (blocks, rows // 2, lanes)
    out, squares, first_next, second_next = pl.pallas_call(
        pack_kernel,
        out_shape=(pltpu.HBM(piece, BF16), pltpu.HBM(tile, F32), halves, halves),
        grid_spec=pltpu.PrefetchScalarGridSpec(
            num_scalar_prefetch=2,
            grid=(steps,),
            in_specs=[pl.BlockSpec(memory_space=VMEM)] * 5,
            out_specs=[
                pl.BlockSpec(piece, lambda i, *_: (0, 0, 0)),
                pl.BlockSpec(tile, lambda i, *_: (0, 0, 0)),
                moment,
                moment,
            ],
        ),
        compiler_params=pltpu.CompilerParams(vmem_limit_bytes=16 * MIB),
    )(key, flags, partial, up_sum, down_sum, first, second)
    shape = (blocks, rows, cols)
    return out, squares, first_next.reshape(shape), second_next.reshape(shape)


def relay_kernel(prev, following, up, down):
    units = up.shape[0]
    up[...] = prev[pl.ds(0, units)]
    down[...] = following[pl.ds(0, units)]


def relay(prev, following):
    shape = jax.ShapeDtypeStruct((5, *prev.shape[1:]), BF16)
    return pl.pallas_call(
        relay_kernel,
        out_shape=(shape, shape),
        in_specs=[pl.BlockSpec(memory_space=VMEM)] * 2,
        out_specs=(pl.BlockSpec(memory_space=VMEM),) * 2,
        compiler_params=pltpu.CompilerParams(vmem_limit_bytes=6 * MIB),
        cost_estimate=LONG,
    )(prev, following)


def unpack_kernel(order, owned, low, high):
    half = low.shape[0]
    for i, place in enumerate(order):
        if place < half:
            low[place] = owned[i]
        else:
            high[place - half] = owned[i]


def unpack(order, owned):
    shape = jax.ShapeDtypeStruct((owned.shape[0] // 2, *owned.shape[1:]), BF16)
    return pl.pallas_call(
        functools.partial(unpack_kernel, order),
        out_shape=(shape, shape),
        in_specs=[pl.BlockSpec(memory_space=VMEM)],
        out_specs=(pl.BlockSpec(memory_space=VMEM),) * 2,
        compiler_params=pltpu.CompilerParams(vmem_limit_bytes=6 * MIB),
    )(owned)


def finish_kernel(key, flags, back, out):
    count, rows, cols = out.shape
    begin = pl.program_id(0) * count

    def step(i, carry):
        block = begin + i
        out[i] = jnp.where(flags[block] != 0, back[key[block]], jnp.zeros((), BF16))
        return carry

    lax.fori_loop(0, count, step, 0, unroll=8)


def finish(key, flags, back):
    blocks, rows, cols = back.shape
    steps = 2 if blocks >= 16 else 1
    return pl.pallas_call(
        finish_kernel,
        out_shape=jax.ShapeDtypeStruct(back.shape, BF16),
        grid_spec=pltpu.PrefetchScalarGridSpec(
            num_scalar_prefetch=2,
            grid=(steps,),
            in_specs=[pl.BlockSpec(memory_space=VMEM)],
            out_specs=pl.BlockSpec((blocks // steps, rows, cols), lambda i, *_: (i, 0, 0)),
        ),
        compiler_params=pltpu.CompilerParams(vmem_limit_bytes=6 * MIB),
    )(key, flags, back)


def precond_kernel(*refs):
    pieces, sources, (out, norms) = refs[:8], refs[8:14], refs[14:16]
    mixed, held, sems = refs[16], refs[17:23], refs[23]
    width, quarter = out.shape
    half = width // 2
    me = lax.axis_index("grp")
    n = width // quarter
    root, up, up_prev, down_next, up_far, down_far = held
    cuts = [(0, 0, 2), (2, 9, 2), (3, 9, 2), (4, 4, 1), (5, 4, 1)]
    cuts += [(1, 0, 9), (3, 0, 9), (4, 0, 4), (5, 0, 4), (2, 0, 9)]
    copies = []
    for i, (which, first, count) in enumerate(cuts):
        units = pl.ds(first, count)
        source, place = sources[which].at[units], held[which].at[units]
        copies.append(pltpu.make_async_copy(source, place, sems.at[i]))
    for copy in copies:
        copy.start()
    for copy in copies[:5]:
        copy.wait()
    right = jnp.concatenate(
        [
            root[0],
            root[1],
            down_next[9],
            down_next[10],
            up_far[4],
            down_far[4],
            up_prev[9],
            up_prev[10],
        ],
        axis=0,
    )
    for row in range(0, width, quarter):
        parts = [ref[pl.ds(row % half, quarter), :] for ref in pieces[row // half :: 2]]
        value = dot(jnp.concatenate(parts, axis=1), right, ((1,), (0,)))
        mixed[pl.ds(row, quarter), :] = value.astype(BF16)
    for copy in copies[5:]:
        copy.wait()
    square = jnp.zeros((8, quarter), F32)
    for step, (low, first), (high, second) in (
        (0, (up, 0), (up, 5)),
        (1, (down_next, 5), (down_next, 0)),
        (2, (up_far, 0), (down_far, 0)),
        (3, (up_prev, 0), (up_prev, 5)),
    ):
        units = [jnp.concatenate([low[first + c], high[second + c]], axis=0) for c in range(n)]
        value = dot(jnp.concatenate(units, axis=1), mixed[...], ((1,), (0,)))
        base = ((me + step) & (n - 1)) * quarter
        out[pl.ds(pl.multiple_of(base, quarter), quarter), :] = value
        square += jnp.sum((value * value).reshape(quarter // 8, 8, quarter), axis=0)
    norms[...] = jnp.zeros_like(norms)
    norms[0:1, :] = jnp.broadcast_to(jnp.sum(square), (1, 128))


def precondition(pieces, sources):
    rows, quarter = pieces[0].shape
    operands = pieces
    return pl.pallas_call(
        precond_kernel,
        out_shape=(
            pltpu.HBM((2 * rows, quarter), F32),
            jax.ShapeDtypeStruct((8, 128), F32),
        ),
        grid=(1,),
        in_specs=[pl.BlockSpec(memory_space=VMEM)] * len(operands)
        + [pl.BlockSpec(memory_space=pl.ANY)] * len(sources),
        out_specs=(
            pl.BlockSpec((2 * rows, quarter), lambda i: (0, 0)),
            pl.BlockSpec((8, 128), lambda i: (0, 0)),
        ),
        scratch_shapes=[
            VMEM((2 * rows, quarter), BF16),
            *[VMEM(source.shape, BF16) for source in sources],
            pltpu.SemaphoreType.DMA((10,)),
        ],
        compiler_params=pltpu.CompilerParams(vmem_limit_bytes=14 * MIB),
    )(*operands, *map(in_hbm, sources))


def graft_kernel(cells, order, precond, shares, first, second, third, fourth, out):
    pre = (first[...] + second[...] + third[...] + fourth[...])[0:1, :]
    adam = jnp.sum(shares[...], axis=0, keepdims=True)
    adam = adam * (BIAS_SECOND / (BIAS_FIRST * BIAS_FIRST))
    scale = -jnp.sqrt(adam / cells) / jnp.sqrt(pre / cells + NORM_EPS)
    _, rows, quarter = out.shape
    scale = jnp.concatenate([scale] * (quarter // 128), axis=1)
    for i, place in enumerate(order):
        out[i] = (scale * precond[pl.ds(place * rows, rows), :]).astype(BF16)


def graft(order, precond, shares, norms):
    width, quarter = precond.shape
    shape = (len(order), width // len(order), quarter)
    small = [pl.BlockSpec(array.shape, lambda i: (0, 0)) for array in (shares, *norms)]
    return pl.pallas_call(
        functools.partial(graft_kernel, float(width * width), order),
        out_shape=pltpu.HBM(shape, BF16),
        grid=(1,),
        in_specs=[pl.BlockSpec((width, quarter), lambda i: (0, 0))] + small,
        out_specs=pl.BlockSpec(shape, lambda i: (0, 0, 0)),
        compiler_params=pltpu.CompilerParams(vmem_limit_bytes=8 * MIB),
    )(in_hbm(precond), shares, *norms)


def on_device(
    grad_parts,
    assign,
    block_bounds,
    left_root,
    right_root,
    left_stat,
    right_stat,
    first_moment,
    second_moment,
):
    n_own = lax.axis_size("own")
    n_grp = lax.axis_size("grp")
    grp_index = lax.axis_index("grp")
    total_blocks = assign.shape[0]
    per_owner = total_blocks // n_own
    shard_rows = grad_parts.shape[2]
    width = grad_parts.shape[3]
    quarter = width // n_grp
    half = total_blocks // 2
    starts = [((grp_index + step) & (n_grp - 1)) * quarter for step in range(4)]
    turn = ((n_grp - grp_index) & (n_grp - 1)) * quarter
    grad_parts, starts, turn = lax.optimization_barrier((grad_parts, starts, turn))

    def columns(array, step):
        return slice_at(array, starts[step], quarter, array.ndim - 1)

    part = grad_parts[0]
    order = ORDER if len(ORDER) == n_own else tuple(range(n_own))

    def exchange(array):
        groups = [list(order)]
        return lax.all_to_all(array, "own", 0, 0, axis_index_groups=groups, tiled=True)

    far = columns(part, 2)
    far_low, far_high = lax.optimization_barrier((far[:half], far[half:]))
    far_up = shift(far_low, 1)
    far_down = shift(far_high, -1)
    later, _, _ = lax.optimization_barrier((part, far_low, far_high))
    up, down = columns(later, 1), columns(later, 3)
    up_low, up_high, down_low, down_high = lax.optimization_barrier(
        (up[:half], up[half:], down[:half], down[half:])
    )
    up_direct = shift(up_high, 1)
    down_direct = shift(down_low, -1)
    up_sum, down_sum = add(up_low, far_up, down_high, far_down)
    up_sum, down_sum, left_root, right_root, later = lax.optimization_barrier(
        (up_sum, down_sum, left_root, right_root, part)
    )
    up_sum = shift(up_sum, 1)
    down_sum = shift(down_sum, -1)
    key = places_of(assign, n_own, per_owner, order)
    flags = inside(block_bounds, shard_rows, quarter)
    roots_up, roots_down, root_own = root_pieces(left_root, right_root)
    later, up_direct, down_direct, key, flags, roots_up, roots_down, root_own = (
        lax.optimization_barrier(
            (later, up_direct, down_direct, key, flags, roots_up, roots_down, root_own)
        )
    )
    own = columns(later, 0)
    partial, first, second = gather(own, up_direct, down_direct, first_moment, second_moment)

    roots_up, roots_down, up_sum, down_sum, partial = lax.optimization_barrier(
        (roots_up, roots_down, up_sum, down_sum, partial)
    )
    sorted_grad, squares, first_next, second_next = pack(
        key, flags, partial, up_sum, down_sum, first, second
    )
    owned = exchange(sorted_grad)
    roots_prev = shift(roots_up, 1)
    roots_next = shift(roots_down, -1)
    onward = relay(roots_prev, roots_next)
    far_roots = [shift(onward[0], 1), shift(onward[1], -1)]
    roots = [root_own, roots_up, roots_prev, roots_next, *far_roots]

    adam_sq = jnp.sum(squares, axis=(1, 2))
    adam_sq = sum(shift(adam_sq, step) for step in (1, 2, 3)) + adam_sq
    owned, roots, adam_sq = lax.optimization_barrier((owned, roots, adam_sq))
    low, high = unpack(order, owned)
    prev_low = shift(low, 1)
    next_high = shift(high, -1)
    prev_high = shift(high, 1)
    next_low = shift(low, -1)
    prev_low, next_high, adam_sq = lax.optimization_barrier((prev_low, next_high, adam_sq))
    shares = exchange(jnp.broadcast_to(adam_sq[:, None, None], (n_own, 1, 128)))
    far_low = shift(prev_low, 1)
    far_high = shift(next_high, -1)
    pieces = [low, high, next_low, next_high, far_low, far_high, prev_low, prev_high]
    flat = [piece.reshape(-1, quarter) for piece in pieces]
    precond, norms = precondition(flat, roots)
    norms = [norms] + [shift(norms, step) for step in (1, 2, 3)]
    grafted = graft(order, precond, shares.reshape(n_own, 128), norms)
    pieces, grafted = lax.optimization_barrier((pieces, grafted))
    back = exchange(grafted)

    whole = jnp.concatenate(
        [jnp.concatenate(pieces[i : i + 2]) for i in (0, 2, 4, 6)], axis=2
    ).reshape(width, width)
    rows = slice_at(whole, starts[0], quarter, 0)
    left_acc = STAT_DECAY * left_stat + dot(rows, whole, ((1,), (1,)))[None]
    cross = dot(whole[:, :quarter], whole, ((0,), (0,)))
    cross = jnp.concatenate([cross, cross], axis=1)
    cross = slice_at(cross, turn, width, 1)
    right_acc = STAT_DECAY * right_stat + cross[None]

    update = finish(key, flags, back)
    return (update, first_next, second_next, left_acc, right_acc)


def solution(mesh):
    placed = (
        P("grp", None, "own", None),
        P(),
        P(),
        P("own", "grp", None),
        P("own", "grp", None),
        P("own", "grp", None),
        P("own", "grp", None),
        P(None, "own", "grp"),
        P(None, "own", "grp"),
    )
    return jax.shard_map(
        on_device,
        mesh=mesh,
        in_specs=placed,
        out_specs=(
            P(None, "own", "grp"),
            P(None, "own", "grp"),
            P(None, "own", "grp"),
            P("own", "grp", None),
            P("own", "grp", None),
        ),
        check_vma=False,
    )
```

```python
import functools

import jax
import jax.numpy as jnp
from jax import lax
from jax.experimental import pallas as pl
from jax.experimental.pallas import tpu as pltpu
from jax.sharding import PartitionSpec as P

BETA_FIRST = 0.9
BETA_SECOND = 0.95
BIAS_FIRST = 1.0 - 0.9**10
BIAS_SECOND = 1.0 - 0.95**10
ADAM_EPS = 1e-08
STAT_DECAY = 0.95
NORM_EPS = 1e-06
F32 = jnp.float32
BF16 = jnp.bfloat16
ORDER = (
    33, 58, 20, 47, 9, 3, 13, 23, 32, 10, 21, 15, 57, 18, 60, 38,
    49, 11, 52, 31, 40, 34, 61, 55, 0, 27, 53, 46, 24, 2, 28, 54,
    1, 26, 5, 63, 8, 51, 12, 39, 16, 43, 4, 30, 56, 35, 44, 22,
    48, 59, 36, 14, 41, 50, 29, 7, 17, 42, 37, 62, 25, 19, 45, 6,
)
MIB = 1024 * 1024
VMEM = pltpu.VMEM
LONG = pl.CostEstimate(flops=2 * 10**11, bytes_accessed=10**9, transcendentals=0)


def shift(array, step):
    n = lax.axis_size("grp")
    return lax.ppermute(array, "grp", [(i, (i + step) % n) for i in range(n)])


def places_of(assign, n_own, per_owner, order):
    place = [order.index(slot) for slot in range(len(order))]
    key = assign % n_own * per_owner + assign // n_own
    return jnp.asarray(place, jnp.int32)[key]


def in_hbm(array):
    return pltpu.with_memory_space_constraint(array, pltpu.HBM)


def slice_at(array, start, size, axis):
    starts = [start if i == axis else 0 for i in range(array.ndim)]
    sizes = [size if i == axis else n for i, n in enumerate(array.shape)]
    return lax.dynamic_slice(array, starts, sizes, allow_negative_indices=False)


def dot(a, b, dims):
    return lax.dot_general(a, b, (dims, ((), ())), preferred_element_type=F32)


def inside(bounds, rows, cols):
    row, col = lax.axis_index("own") * rows, lax.axis_index("grp") * cols
    ok = (row < bounds[:, 2] - bounds[:, 0]) & (col < bounds[:, 3] - bounds[:, 1])
    return ok.astype(jnp.int32)


def add_kernel(up, far_up, down, far_down, up_out, down_out):
    up_out[...] = (up[...].astype(F32) + far_up[...].astype(F32)).astype(BF16)
    down_out[...] = (down[...].astype(F32) + far_down[...].astype(F32)).astype(BF16)


def add(*arrays):
    shape = jax.ShapeDtypeStruct(arrays[0].shape, BF16)
    return pl.pallas_call(
        add_kernel,
        out_shape=(shape, shape),
        in_specs=[pl.BlockSpec(memory_space=VMEM)] * 4,
        out_specs=(pl.BlockSpec(memory_space=VMEM),) * 2,
        compiler_params=pltpu.CompilerParams(vmem_limit_bytes=4 * MIB),
    )(*arrays)


def roots_kernel(left, right, up, down, own):
    _, units, _, cols = (1, *up.shape)
    rows = up.shape[1]

    def root(half, step):
        col = ((lax.axis_index("grp") + step) & 3) * cols
        col = pl.ds(pl.multiple_of(col, cols), cols)
        return right[0, pl.ds(half * rows, rows), col].astype(BF16)

    for half in range(2):
        own[half] = root(half, 0)
        up[9 + half] = root(half, 1)
        down[9 + half] = root(half, 3)
        for c in range(4):
            unit = left[0, pl.ds(half * rows, rows), pl.ds(c * cols, cols)].astype(BF16)
            up[5 * half + c] = unit
            down[5 - 5 * half + c] = unit
    up[4] = root(0, 2)
    down[4] = root(1, 2)


def root_pieces(left, right):
    _, rows, width = left.shape
    unit = (rows // 2, width // 4)
    return pl.pallas_call(
        roots_kernel,
        out_shape=(
            pltpu.HBM((11, *unit), BF16),
            pltpu.HBM((11, *unit), BF16),
            pltpu.HBM((2, *unit), BF16),
        ),
        grid=(1,),
        in_specs=[pl.BlockSpec(left.shape, lambda i: (0, 0, 0))] * 2,
        out_specs=tuple(pl.BlockSpec((n, *unit), lambda i: (0, 0, 0)) for n in (11, 11, 2)),
        compiler_params=pltpu.CompilerParams(vmem_limit_bytes=8 * MIB),
    )(in_hbm(left), in_hbm(right))


def gather_kernel(own, up_direct, down_direct, first, second, out, first_out, second_out):
    half = up_direct.shape[0]

    def step(i, carry):
        out[0, i] = own[i].astype(F32) + down_direct[i].astype(F32)
        out[1, i] = own[i + half].astype(F32) + up_direct[i].astype(F32)
        return carry

    lax.fori_loop(0, half, step, 0, unroll=4)
    first_out[...] = BETA_FIRST * first[...]
    second_out[...] = BETA_SECOND * second[...]


def gather(own, up_direct, down_direct, first, second):
    shape = jax.ShapeDtypeStruct((2, *up_direct.shape), F32)
    return pl.pallas_call(
        gather_kernel,
        out_shape=(shape,) * 3,
        in_specs=[pl.BlockSpec(memory_space=VMEM)] * 5,
        out_specs=(pl.BlockSpec(memory_space=VMEM),) * 3,
        compiler_params=pltpu.CompilerParams(vmem_limit_bytes=10 * MIB),
        cost_estimate=LONG,
    )(own, up_direct, down_direct, first.reshape(shape.shape), second.reshape(shape.shape))


def pack_kernel(
    key, flags, partial, up_sum, down_sum, first, second, out, first_out, second_out
):
    _, half, rows, cols = partial.shape
    count = first_out.shape[1]
    begin = pl.program_id(0) * count
    lanes = cols // 2

    def one(side, i, value):
        at = begin + i
        block = side * half + at
        keep = flags[block].astype(F32)
        grad = value * keep
        first_next = first[side, at] + (1.0 - BETA_FIRST) * grad
        second_next = second[side, at] + (1.0 - BETA_SECOND) * grad * grad
        first_out[side, i] = first_next
        second_out[side, i] = second_next
        root = second_next * lax.rsqrt(second_next)
        adam = first_next * pl.reciprocal(root + ADAM_EPS * BIAS_SECOND**0.5)
        square = adam * adam
        square = square[:, :lanes] + square[:, lanes:]
        square = (square[: rows // 2] + square[rows // 2 :]) * keep
        piece = jnp.concatenate([grad[:, :lanes], grad[:, lanes:], square], axis=0)
        out[key[block]] = piece.astype(BF16)

    def step(i, carry):
        at = begin + i
        one(0, i, partial[0, at] + up_sum[at].astype(F32))
        one(1, i, partial[1, at] + down_sum[at].astype(F32))
        return carry

    lax.fori_loop(0, count, step, 0, unroll=4)


def pack(key, flags, partial, up_sum, down_sum, first, second):
    _, half, rows, cols = partial.shape
    blocks, lanes = 2 * half, cols // 2
    steps = 4 if half >= 16 else 1
    moment = pl.BlockSpec((2, half // steps, rows, cols), lambda i, *_: (0, i, 0, 0))
    halves = pltpu.HBM((2, half, rows, cols), F32)
    piece = (blocks, 2 * rows + rows // 2, lanes)
    out, first_next, second_next = pl.pallas_call(
        pack_kernel,
        out_shape=(pltpu.HBM(piece, BF16), halves, halves),
        grid_spec=pltpu.PrefetchScalarGridSpec(
            num_scalar_prefetch=2,
            grid=(steps,),
            in_specs=[pl.BlockSpec(memory_space=VMEM)] * 5,
            out_specs=[pl.BlockSpec(piece, lambda i, *_: (0, 0, 0)), moment, moment],
        ),
        compiler_params=pltpu.CompilerParams(vmem_limit_bytes=16 * MIB),
    )(key, flags, partial, up_sum, down_sum, first, second)
    shape = (blocks, rows, cols)
    return out, first_next.reshape(shape), second_next.reshape(shape)


def relay_kernel(prev, following, up, down):
    units = up.shape[0]
    up[...] = prev[pl.ds(0, units)]
    down[...] = following[pl.ds(0, units)]


def relay(prev, following):
    shape = jax.ShapeDtypeStruct((5, *prev.shape[1:]), BF16)
    return pl.pallas_call(
        relay_kernel,
        out_shape=(shape, shape),
        in_specs=[pl.BlockSpec(memory_space=VMEM)] * 2,
        out_specs=(pl.BlockSpec(memory_space=VMEM),) * 2,
        compiler_params=pltpu.CompilerParams(vmem_limit_bytes=6 * MIB),
        cost_estimate=LONG,
    )(prev, following)


def unpack_kernel(order, owned, low, high, adam):
    half, rows, cols = low.shape
    total = jnp.zeros(adam.shape, F32)
    for i, place in enumerate(order):
        piece = owned[i]
        value = jnp.concatenate([piece[:rows], piece[rows : 2 * rows]], axis=1)
        if place < half:
            low[place] = value
        else:
            high[place - half] = value
        total += piece.astype(F32)[2 * rows :]
    adam[...] = total


def unpack(order, owned, rows):
    half = owned.shape[0] // 2
    shape = jax.ShapeDtypeStruct((half, rows, 2 * owned.shape[2]), BF16)
    return pl.pallas_call(
        functools.partial(unpack_kernel, order),
        out_shape=(shape, shape, jax.ShapeDtypeStruct((rows // 2, 128), F32)),
        in_specs=[pl.BlockSpec(memory_space=VMEM)],
        out_specs=(pl.BlockSpec(memory_space=VMEM),) * 3,
        compiler_params=pltpu.CompilerParams(vmem_limit_bytes=6 * MIB),
    )(owned)


def finish_kernel(key, flags, back, out):
    count, rows, cols = out.shape
    begin = pl.program_id(0) * count

    def step(i, carry):
        block = begin + i
        out[i] = jnp.where(flags[block] != 0, back[key[block]], jnp.zeros((), BF16))
        return carry

    lax.fori_loop(0, count, step, 0, unroll=8)


def finish(key, flags, back):
    blocks, rows, cols = back.shape
    steps = 2 if blocks >= 16 else 1
    return pl.pallas_call(
        finish_kernel,
        out_shape=jax.ShapeDtypeStruct(back.shape, BF16),
        grid_spec=pltpu.PrefetchScalarGridSpec(
            num_scalar_prefetch=2,
            grid=(steps,),
            in_specs=[pl.BlockSpec(memory_space=VMEM)],
            out_specs=pl.BlockSpec((blocks // steps, rows, cols), lambda i, *_: (i, 0, 0)),
        ),
        compiler_params=pltpu.CompilerParams(vmem_limit_bytes=6 * MIB),
    )(key, flags, back)


def precond_kernel(*refs):
    pieces, adam, sources, (out, norms) = refs[:8], refs[8], refs[9:15], refs[15:17]
    mixed, held, sems = refs[17], refs[18:24], refs[24]
    width, quarter = out.shape
    half = width // 2
    me = lax.axis_index("grp")
    n = width // quarter
    root, up, up_prev, down_next, up_far, down_far = held
    cuts = [(0, 0, 2), (2, 9, 2), (3, 9, 2), (4, 4, 1), (5, 4, 1)]
    cuts += [(1, 0, 9), (3, 0, 9), (4, 0, 4), (5, 0, 4), (2, 0, 9)]
    copies = []
    for i, (which, first, count) in enumerate(cuts):
        units = pl.ds(first, count)
        source, place = sources[which].at[units], held[which].at[units]
        copies.append(pltpu.make_async_copy(source, place, sems.at[i]))
    for copy in copies:
        copy.start()
    for copy in copies[:5]:
        copy.wait()
    right = jnp.concatenate(
        [
            root[0],
            root[1],
            down_next[9],
            down_next[10],
            up_far[4],
            down_far[4],
            up_prev[9],
            up_prev[10],
        ],
        axis=0,
    )
    for row in range(0, width, quarter):
        parts = [ref[pl.ds(row % half, quarter), :] for ref in pieces[row // half :: 2]]
        value = dot(jnp.concatenate(parts, axis=1), right, ((1,), (0,)))
        mixed[pl.ds(row, quarter), :] = value.astype(BF16)
    for copy in copies[5:]:
        copy.wait()
    square = jnp.zeros((8, quarter), F32)
    for step, (low, first), (high, second) in (
        (0, (up, 0), (up, 5)),
        (1, (down_next, 5), (down_next, 0)),
        (2, (up_far, 0), (down_far, 0)),
        (3, (up_prev, 0), (up_prev, 5)),
    ):
        units = [jnp.concatenate([low[first + c], high[second + c]], axis=0) for c in range(n)]
        value = dot(jnp.concatenate(units, axis=1), mixed[...], ((1,), (0,)))
        base = ((me + step) & (n - 1)) * quarter
        out[pl.ds(pl.multiple_of(base, quarter), quarter), :] = value
        square += jnp.sum((value * value).reshape(quarter // 8, 8, quarter), axis=0)
    norms[...] = jnp.zeros_like(norms)
    norms[0:1, :] = jnp.broadcast_to(jnp.sum(square), (1, 128))
    norms[1:2, :] = jnp.broadcast_to(jnp.sum(adam[...]), (1, 128))


def precondition(pieces, adam, sources):
    rows, quarter = pieces[0].shape
    operands = (*pieces, adam)
    return pl.pallas_call(
        precond_kernel,
        out_shape=(
            jax.ShapeDtypeStruct((2 * rows, quarter), F32),
            jax.ShapeDtypeStruct((8, 128), F32),
        ),
        in_specs=[pl.BlockSpec(memory_space=VMEM)] * len(operands)
        + [pl.BlockSpec(memory_space=pl.ANY)] * len(sources),
        out_specs=(pl.BlockSpec(memory_space=VMEM),) * 2,
        scratch_shapes=[
            VMEM((2 * rows, quarter), BF16),
            *[VMEM(source.shape, BF16) for source in sources],
            pltpu.SemaphoreType.DMA((10,)),
        ],
        compiler_params=pltpu.CompilerParams(vmem_limit_bytes=14 * MIB),
    )(*operands, *map(in_hbm, sources))


def graft_kernel(cells, order, precond, first, second, third, fourth, out):
    sums = first[...] + second[...] + third[...] + fourth[...]
    pre, adam = sums[0:1, :], sums[1:2, :]
    adam = adam * (BIAS_SECOND / (BIAS_FIRST * BIAS_FIRST))
    scale = -jnp.sqrt(adam / cells) / jnp.sqrt(pre / cells + NORM_EPS)
    _, rows, quarter = out.shape
    scale = jnp.concatenate([scale] * (quarter // 128), axis=1)
    for i, place in enumerate(order):
        out[i] = (scale * precond[pl.ds(place * rows, rows), :]).astype(BF16)


def graft(order, precond, norms):
    width, quarter = precond.shape
    shape = (len(order), width // len(order), quarter)
    small = pl.BlockSpec((8, 128), lambda i: (0, 0))
    return pl.pallas_call(
        functools.partial(graft_kernel, float(width * width), order),
        out_shape=pltpu.HBM(shape, BF16),
        grid=(1,),
        in_specs=[pl.BlockSpec((width, quarter), lambda i: (0, 0))] + [small] * 4,
        out_specs=pl.BlockSpec(shape, lambda i: (0, 0, 0)),
        compiler_params=pltpu.CompilerParams(vmem_limit_bytes=8 * MIB),
    )(precond, *norms)


def on_device(
    grad_parts,
    assign,
    block_bounds,
    left_root,
    right_root,
    left_stat,
    right_stat,
    first_moment,
    second_moment,
):
    n_own = lax.axis_size("own")
    n_grp = lax.axis_size("grp")
    grp_index = lax.axis_index("grp")
    total_blocks = assign.shape[0]
    per_owner = total_blocks // n_own
    shard_rows = grad_parts.shape[2]
    width = grad_parts.shape[3]
    quarter = width // n_grp
    half = total_blocks // 2
    starts = [((grp_index + step) & (n_grp - 1)) * quarter for step in range(4)]
    turn = ((n_grp - grp_index) & (n_grp - 1)) * quarter
    grad_parts, starts, turn = lax.optimization_barrier((grad_parts, starts, turn))

    def columns(array, step):
        return slice_at(array, starts[step], quarter, array.ndim - 1)

    part = grad_parts[0]
    order = ORDER if len(ORDER) == n_own else tuple(range(n_own))

    def exchange(array):
        groups = [list(order)]
        return lax.all_to_all(array, "own", 0, 0, axis_index_groups=groups, tiled=True)

    far = columns(part, 2)
    far_low, far_high = lax.optimization_barrier((far[:half], far[half:]))
    far_up = shift(far_low, 1)
    far_down = shift(far_high, -1)
    later, _, _ = lax.optimization_barrier((part, far_low, far_high))
    up, down = columns(later, 1), columns(later, 3)
    up_low, up_high, down_low, down_high = lax.optimization_barrier(
        (up[:half], up[half:], down[:half], down[half:])
    )
    up_direct = shift(up_high, 1)
    down_direct = shift(down_low, -1)
    up_sum, down_sum = add(up_low, far_up, down_high, far_down)
    up_sum, down_sum, left_root, right_root, later = lax.optimization_barrier(
        (up_sum, down_sum, left_root, right_root, part)
    )
    own = columns(later, 0)
    up_sum = shift(up_sum, 1)
    down_sum = shift(down_sum, -1)
    key = places_of(assign, n_own, per_owner, order)
    flags = inside(block_bounds, shard_rows, quarter)
    roots_up, roots_down, root_own = root_pieces(left_root, right_root)
    up_direct, down_direct, key, flags, roots_up, roots_down, root_own = lax.optimization_barrier(
        (up_direct, down_direct, key, flags, roots_up, roots_down, root_own)
    )
    partial, first, second = gather(own, up_direct, down_direct, first_moment, second_moment)

    roots_up, roots_down, up_sum, down_sum, partial = lax.optimization_barrier(
        (roots_up, roots_down, up_sum, down_sum, partial)
    )
    sorted_grad, first_next, second_next = pack(
        key, flags, partial, up_sum, down_sum, first, second
    )
    owned = exchange(sorted_grad)
    roots_prev = shift(roots_up, 1)
    roots_next = shift(roots_down, -1)
    onward = relay(roots_prev, roots_next)
    far_roots = [shift(onward[0], 1), shift(onward[1], -1)]
    roots = [root_own, roots_up, roots_prev, roots_next, *far_roots]

    owned, roots = lax.optimization_barrier((owned, roots))
    low, high, adam = unpack(order, owned, shard_rows)
    prev_low = shift(low, 1)
    next_high = shift(high, -1)
    prev_high = shift(high, 1)
    next_low = shift(low, -1)
    far_low = shift(prev_low, 1)
    far_high = shift(next_high, -1)
    pieces = [low, high, next_low, next_high, far_low, far_high, prev_low, prev_high]
    flat = [piece.reshape(-1, quarter) for piece in pieces]
    precond, norms = precondition(flat, adam, roots)
    norms = [norms] + [shift(norms, step) for step in (1, 2, 3)]
    grafted = graft(order, precond, norms)
    pieces, grafted = lax.optimization_barrier((pieces, grafted))
    back = exchange(grafted)

    whole = jnp.concatenate(
        [jnp.concatenate(pieces[i : i + 2]) for i in (0, 2, 4, 6)], axis=2
    ).reshape(width, width)
    rows = slice_at(whole, starts[0], quarter, 0)
    left_acc = STAT_DECAY * left_stat + dot(rows, whole, ((1,), (1,)))[None]
    cross = dot(whole[:, :quarter], whole, ((0,), (0,)))
    cross = jnp.concatenate([cross, cross], axis=1)
    cross = slice_at(cross, turn, width, 1)
    right_acc = STAT_DECAY * right_stat + cross[None]

    update = finish(key, flags, back)
    return (update, first_next, second_next, left_acc, right_acc)


def solution(mesh):
    placed = (
        P("grp", None, "own", None),
        P(),
        P(),
        P("own", "grp", None),
        P("own", "grp", None),
        P("own", "grp", None),
        P("own", "grp", None),
        P(None, "own", "grp"),
        P(None, "own", "grp"),
    )
    return jax.shard_map(
        on_device,
        mesh=mesh,
        in_specs=placed,
        out_specs=(
            P(None, "own", "grp"),
            P(None, "own", "grp"),
            P(None, "own", "grp"),
            P("own", "grp", None),
            P("own", "grp", None),
        ),
        check_vma=False,
    )
```

```python
import functools

import jax
import jax.numpy as jnp
from jax import lax
from jax.experimental import pallas as pl
from jax.experimental.pallas import tpu as pltpu
from jax.sharding import PartitionSpec as P

BETA_FIRST = 0.9
BETA_SECOND = 0.95
BIAS_FIRST = 1.0 - 0.9**10
BIAS_SECOND = 1.0 - 0.95**10
ADAM_EPS = 1e-08
STAT_DECAY = 0.95
NORM_EPS = 1e-06
F32 = jnp.float32
BF16 = jnp.bfloat16
MIB = 1024 * 1024
VMEM = pltpu.VMEM
LONG = pl.CostEstimate(flops=2 * 10**11, bytes_accessed=10**9, transcendentals=0)


def shift(array, step):
    n = lax.axis_size("grp")
    return lax.ppermute(array, "grp", [(i, (i + step) % n) for i in range(n)])


def in_hbm(array):
    return pltpu.with_memory_space_constraint(array, pltpu.HBM)


def slice_at(array, start, size, axis):
    starts = [start if i == axis else 0 for i in range(array.ndim)]
    sizes = [size if i == axis else n for i, n in enumerate(array.shape)]
    return lax.dynamic_slice(array, starts, sizes, allow_negative_indices=False)


def dot(a, b, dims):
    return lax.dot_general(a, b, (dims, ((), ())), preferred_element_type=F32)


def inside(bounds, rows, cols):
    row, col = lax.axis_index("own") * rows, lax.axis_index("grp") * cols
    ok = (row < bounds[:, 2] - bounds[:, 0]) & (col < bounds[:, 3] - bounds[:, 1])
    return ok.astype(jnp.int32)


def add_kernel(up, far_up, down, far_down, up_out, down_out):
    up_out[...] = (up[...].astype(F32) + far_up[...].astype(F32)).astype(BF16)
    down_out[...] = (down[...].astype(F32) + far_down[...].astype(F32)).astype(BF16)


def add(*arrays):
    shape = jax.ShapeDtypeStruct(arrays[0].shape, BF16)
    return pl.pallas_call(
        add_kernel,
        out_shape=(shape, shape),
        in_specs=[pl.BlockSpec(memory_space=VMEM)] * 4,
        out_specs=(pl.BlockSpec(memory_space=VMEM),) * 2,
        compiler_params=pltpu.CompilerParams(vmem_limit_bytes=4 * MIB),
    )(*arrays)


def roots_kernel(left, right, up, down, own):
    _, units, _, cols = (1, *up.shape)
    rows = up.shape[1]

    def root(half, step):
        col = ((lax.axis_index("grp") + step) & 3) * cols
        col = pl.ds(pl.multiple_of(col, cols), cols)
        return right[0, pl.ds(half * rows, rows), col].astype(BF16)

    for half in range(2):
        own[half] = root(half, 0)
        up[9 + half] = root(half, 1)
        down[9 + half] = root(half, 3)
        for c in range(4):
            unit = left[0, pl.ds(half * rows, rows), pl.ds(c * cols, cols)].astype(BF16)
            up[5 * half + c] = unit
            down[5 - 5 * half + c] = unit
    up[4] = root(0, 2)
    down[4] = root(1, 2)


def root_pieces(left, right):
    _, rows, width = left.shape
    unit = (rows // 2, width // 4)
    return pl.pallas_call(
        roots_kernel,
        out_shape=(
            pltpu.HBM((11, *unit), BF16),
            pltpu.HBM((11, *unit), BF16),
            pltpu.HBM((2, *unit), BF16),
        ),
        grid=(1,),
        in_specs=[pl.BlockSpec(left.shape, lambda i: (0, 0, 0))] * 2,
        out_specs=tuple(pl.BlockSpec((n, *unit), lambda i: (0, 0, 0)) for n in (11, 11, 2)),
        compiler_params=pltpu.CompilerParams(vmem_limit_bytes=8 * MIB),
        cost_estimate=LONG,
    )(in_hbm(left), in_hbm(right))


def gather_kernel(own, up_direct, down_direct, first, second, out, first_out, second_out):
    half = up_direct.shape[0]

    def step(i, carry):
        out[0, i] = own[i].astype(F32) + down_direct[i].astype(F32)
        out[1, i] = own[i + half].astype(F32) + up_direct[i].astype(F32)
        return carry

    lax.fori_loop(0, half, step, 0, unroll=4)
    first_out[...] = BETA_FIRST * first[...]
    second_out[...] = BETA_SECOND * second[...]


def gather(own, up_direct, down_direct, first, second):
    shape = jax.ShapeDtypeStruct((2, *up_direct.shape), F32)
    return pl.pallas_call(
        gather_kernel,
        out_shape=(shape,) * 3,
        in_specs=[pl.BlockSpec(memory_space=VMEM)] * 5,
        out_specs=(pl.BlockSpec(memory_space=VMEM),) * 3,
        compiler_params=pltpu.CompilerParams(vmem_limit_bytes=10 * MIB),
    )(own, up_direct, down_direct, first.reshape(shape.shape), second.reshape(shape.shape))


def pack_kernel(
    key, flags, partial, up_sum, down_sum, first, second, out, squares, first_out, second_out
):
    _, half, rows, cols = partial.shape
    count = first_out.shape[1]
    begin = pl.program_id(0) * count
    lanes = cols // 2

    def one(side, i, value):
        at = begin + i
        block = side * half + at
        keep = flags[block].astype(F32)
        grad = value * keep
        first_next = first[side, at] + (1.0 - BETA_FIRST) * grad
        second_next = second[side, at] + (1.0 - BETA_SECOND) * grad * grad
        first_out[side, i] = first_next
        second_out[side, i] = second_next
        root = second_next * lax.rsqrt(second_next)
        adam = first_next * pl.reciprocal(root + ADAM_EPS * BIAS_SECOND**0.5)
        square = adam * adam
        square = square[:, :lanes] + square[:, lanes:]
        square = (square[: rows // 2] + square[rows // 2 :]) * keep
        place = key[block]
        out[place] = grad.astype(BF16)
        squares[place] = square

    def step(i, carry):
        at = begin + i
        one(0, i, partial[0, at] + up_sum[at].astype(F32))
        one(1, i, partial[1, at] + down_sum[at].astype(F32))
        return carry

    lax.fori_loop(0, count, step, 0, unroll=4)


def pack(key, flags, partial, up_sum, down_sum, first, second):
    _, half, rows, cols = partial.shape
    blocks, lanes = 2 * half, cols // 2
    steps = 2 if half >= 16 else 1
    moment = pl.BlockSpec((2, half // steps, rows, cols), lambda i, *_: (0, i, 0, 0))
    halves = pltpu.HBM((2, half, rows, cols), F32)
    piece, tile = (blocks, rows, cols), (blocks, rows // 2, lanes)
    out, squares, first_next, second_next = pl.pallas_call(
        pack_kernel,
        out_shape=(pltpu.HBM(piece, BF16), pltpu.HBM(tile, F32), halves, halves),
        grid_spec=pltpu.PrefetchScalarGridSpec(
            num_scalar_prefetch=2,
            grid=(steps,),
            in_specs=[pl.BlockSpec(memory_space=VMEM)] * 5,
            out_specs=[
                pl.BlockSpec(piece, lambda i, *_: (0, 0, 0)),
                pl.BlockSpec(tile, lambda i, *_: (0, 0, 0)),
                moment,
                moment,
            ],
        ),
        compiler_params=pltpu.CompilerParams(vmem_limit_bytes=16 * MIB),
    )(key, flags, partial, up_sum, down_sum, first, second)
    shape = (blocks, rows, cols)
    return out, squares, first_next.reshape(shape), second_next.reshape(shape)


def relay_kernel(prev, following, up, down):
    units = up.shape[0]
    up[...] = prev[pl.ds(0, units)]
    down[...] = following[pl.ds(0, units)]


def relay(prev, following):
    shape = jax.ShapeDtypeStruct((5, *prev.shape[1:]), BF16)
    return pl.pallas_call(
        relay_kernel,
        out_shape=(shape, shape),
        in_specs=[pl.BlockSpec(memory_space=VMEM)] * 2,
        out_specs=(pl.BlockSpec(memory_space=VMEM),) * 2,
        compiler_params=pltpu.CompilerParams(vmem_limit_bytes=6 * MIB),
        cost_estimate=LONG,
    )(prev, following)


def finish_kernel(key, flags, back, out):
    count, rows, cols = out.shape
    begin = pl.program_id(0) * count

    def step(i, carry):
        block = begin + i
        out[i] = jnp.where(flags[block] != 0, back[key[block]], jnp.zeros((), BF16))
        return carry

    lax.fori_loop(0, count, step, 0, unroll=8)


def finish(key, flags, back):
    blocks, rows, cols = back.shape
    steps = 2 if blocks >= 16 else 1
    return pl.pallas_call(
        finish_kernel,
        out_shape=jax.ShapeDtypeStruct(back.shape, BF16),
        grid_spec=pltpu.PrefetchScalarGridSpec(
            num_scalar_prefetch=2,
            grid=(steps,),
            in_specs=[pl.BlockSpec(memory_space=VMEM)],
            out_specs=pl.BlockSpec((blocks // steps, rows, cols), lambda i, *_: (i, 0, 0)),
        ),
        compiler_params=pltpu.CompilerParams(vmem_limit_bytes=6 * MIB),
    )(key, flags, back)


def precond_kernel(*refs):
    pieces, sources, (out, norms) = refs[:8], refs[8:14], refs[14:16]
    mixed, held, sems = refs[16], refs[17:23], refs[23]
    width, quarter = out.shape
    half = width // 2
    me = lax.axis_index("grp")
    n = width // quarter
    root, up, up_prev, down_next, up_far, down_far = held
    cuts = [(0, 0, 2), (2, 9, 2), (3, 9, 2), (4, 4, 1), (5, 4, 1)]
    cuts += [(1, 0, 9), (3, 0, 9), (4, 0, 4), (5, 0, 4), (2, 0, 9)]
    copies = []
    for i, (which, first, count) in enumerate(cuts):
        units = pl.ds(first, count)
        source, place = sources[which].at[units], held[which].at[units]
        copies.append(pltpu.make_async_copy(source, place, sems.at[i]))
    for copy in copies:
        copy.start()
    for copy in copies[:5]:
        copy.wait()
    right = jnp.concatenate(
        [
            root[0],
            root[1],
            down_next[9],
            down_next[10],
            up_far[4],
            down_far[4],
            up_prev[9],
            up_prev[10],
        ],
        axis=0,
    )
    for row in range(0, width, quarter):
        parts = [ref[pl.ds(row % half, quarter), :] for ref in pieces[row // half :: 2]]
        value = dot(jnp.concatenate(parts, axis=1), right, ((1,), (0,)))
        mixed[pl.ds(row, quarter), :] = value.astype(BF16)
    for copy in copies[5:]:
        copy.wait()
    square = jnp.zeros((8, quarter), F32)
    for step, (low, first), (high, second) in (
        (0, (up, 0), (up, 5)),
        (1, (down_next, 5), (down_next, 0)),
        (2, (up_far, 0), (down_far, 0)),
        (3, (up_prev, 0), (up_prev, 5)),
    ):
        units = [jnp.concatenate([low[first + c], high[second + c]], axis=0) for c in range(n)]
        value = dot(jnp.concatenate(units, axis=1), mixed[...], ((1,), (0,)))
        base = ((me + step) & (n - 1)) * quarter
        out[pl.ds(pl.multiple_of(base, quarter), quarter), :] = value
        square += jnp.sum((value * value).reshape(quarter // 8, 8, quarter), axis=0)
    norms[...] = jnp.zeros_like(norms)
    norms[0:1, :] = jnp.broadcast_to(jnp.sum(square), (1, 128))


def precondition(pieces, sources):
    rows, quarter = pieces[0].shape
    operands = pieces
    return pl.pallas_call(
        precond_kernel,
        out_shape=(
            jax.ShapeDtypeStruct((2 * rows, quarter), F32),
            jax.ShapeDtypeStruct((8, 128), F32),
        ),
        in_specs=[pl.BlockSpec(memory_space=VMEM)] * len(operands)
        + [pl.BlockSpec(memory_space=pl.ANY)] * len(sources),
        out_specs=(pl.BlockSpec(memory_space=VMEM),) * 2,
        scratch_shapes=[
            VMEM((2 * rows, quarter), BF16),
            *[VMEM(source.shape, BF16) for source in sources],
            pltpu.SemaphoreType.DMA((10,)),
        ],
        compiler_params=pltpu.CompilerParams(vmem_limit_bytes=14 * MIB),
    )(*operands, *map(in_hbm, sources))


def graft_kernel(cells, precond, sums, first, second, third, fourth, out):
    pre = (first[...] + second[...] + third[...] + fourth[...])[0:1, :]
    slot = lax.broadcasted_iota(jnp.int32, sums.shape, 1)
    adam = jnp.sum(jnp.where(slot == lax.axis_index("own"), sums[...], 0.0))
    adam = adam * (BIAS_SECOND / (BIAS_FIRST * BIAS_FIRST))
    scale = -jnp.sqrt(adam / cells) / jnp.sqrt(pre / cells + NORM_EPS)
    pieces, rows, quarter = out.shape
    scale = jnp.concatenate([scale] * (quarter // 128), axis=1)
    for i in range(pieces):
        out[i] = (scale * precond[pl.ds(i * rows, rows), :]).astype(BF16)


def graft(precond, sums, norms):
    width, quarter = precond.shape
    pieces = sums.shape[1]
    shape = (pieces, width // pieces, quarter)
    operands = (precond, sums, *norms)
    return pl.pallas_call(
        functools.partial(graft_kernel, float(width * width)),
        out_shape=pltpu.HBM(shape, BF16),
        grid=(1,),
        in_specs=[pl.BlockSpec(array.shape, lambda i: (0, 0)) for array in operands],
        out_specs=pl.BlockSpec(shape, lambda i: (0, 0, 0)),
        compiler_params=pltpu.CompilerParams(vmem_limit_bytes=8 * MIB),
    )(*operands)


def on_device(
    grad_parts,
    assign,
    block_bounds,
    left_root,
    right_root,
    left_stat,
    right_stat,
    first_moment,
    second_moment,
):
    n_own = lax.axis_size("own")
    n_grp = lax.axis_size("grp")
    grp_index = lax.axis_index("grp")
    total_blocks = assign.shape[0]
    per_owner = total_blocks // n_own
    shard_rows = grad_parts.shape[2]
    width = grad_parts.shape[3]
    quarter = width // n_grp
    half = total_blocks // 2
    starts = [((grp_index + step) & (n_grp - 1)) * quarter for step in range(4)]
    turn = ((n_grp - grp_index) & (n_grp - 1)) * quarter
    grad_parts, starts, turn = lax.optimization_barrier((grad_parts, starts, turn))

    def columns(array, step):
        return slice_at(array, starts[step], quarter, array.ndim - 1)

    part = grad_parts[0]

    def exchange(array):
        return lax.all_to_all(array, "own", split_axis=0, concat_axis=0, tiled=True)

    def summed(array, axis, *steps):
        n = lax.axis_size(axis)
        for step in steps:
            array += lax.ppermute(array, axis, [(i, i ^ step) for i in range(n)])
        return array

    far = columns(part, 2)
    far_low, far_high = lax.optimization_barrier((far[:half], far[half:]))
    far_up = shift(far_low, 1)
    far_down = shift(far_high, -1)
    later, _, _ = lax.optimization_barrier((part, far_low, far_high))
    up, down = columns(later, 1), columns(later, 3)
    up_low, up_high, down_low, down_high = lax.optimization_barrier(
        (up[:half], up[half:], down[:half], down[half:])
    )
    up_direct = shift(up_high, 1)
    down_direct = shift(down_low, -1)
    up_sum, down_sum = add(up_low, far_up, down_high, far_down)
    up_sum, down_sum, left_root, right_root, later = lax.optimization_barrier(
        (up_sum, down_sum, left_root, right_root, part)
    )
    up_sum = shift(up_sum, 1)
    down_sum = shift(down_sum, -1)
    key = (assign % n_own * per_owner + assign // n_own).astype(jnp.int32)
    flags = inside(block_bounds, shard_rows, quarter)
    roots_up, roots_down, root_own = root_pieces(left_root, right_root)
    later, up_direct, down_direct, key, flags, roots_up, roots_down, root_own = (
        lax.optimization_barrier(
            (later, up_direct, down_direct, key, flags, roots_up, roots_down, root_own)
        )
    )
    own = columns(later, 0)
    partial, first, second = gather(own, up_direct, down_direct, first_moment, second_moment)

    roots_up, roots_down, up_sum, down_sum, partial = lax.optimization_barrier(
        (roots_up, roots_down, up_sum, down_sum, partial)
    )
    sorted_grad, squares, first_next, second_next = pack(
        key, flags, partial, up_sum, down_sum, first, second
    )
    owned = exchange(sorted_grad)
    roots_prev = shift(roots_up, 1)
    roots_next = shift(roots_down, -1)
    onward = relay(roots_prev, roots_next)
    far_roots = [shift(onward[0], 1), shift(onward[1], -1)]
    roots = [root_own, roots_up, roots_prev, roots_next, *far_roots]

    adam_sq = jnp.sum(squares, axis=(1, 2))
    bits = [1 << i for i in range(n_own.bit_length() - 1)]
    adam_sq = summed(summed(adam_sq, "grp", 1, 2), "own", *bits[:2])
    owned, roots, adam_sq = lax.optimization_barrier((owned, roots, adam_sq))
    low, high = owned[:half], owned[half:]
    prev_low = shift(low, 1)
    next_high = shift(high, -1)
    prev_high = shift(high, 1)
    next_low = shift(low, -1)
    adam_sq = summed(adam_sq, "own", *bits[2:])
    far_low = shift(prev_low, 1)
    far_high = shift(next_high, -1)
    pieces = [low, high, next_low, next_high, far_low, far_high, prev_low, prev_high]
    flat = [piece.reshape(-1, quarter) for piece in pieces]
    flat, adam_sq = lax.optimization_barrier((flat, adam_sq))
    precond, norms = precondition(flat, roots)
    norms = [norms] + [shift(norms, step) for step in (1, 2, 3)]
    grafted = graft(precond, adam_sq.reshape(1, n_own), norms)
    pieces, grafted = lax.optimization_barrier((pieces, grafted))
    back = exchange(grafted)

    whole = jnp.concatenate(
        [jnp.concatenate(pieces[i : i + 2]) for i in (0, 2, 4, 6)], axis=2
    ).reshape(width, width)
    rows = slice_at(whole, starts[0], quarter, 0)
    left_acc = STAT_DECAY * left_stat + dot(rows, whole, ((1,), (1,)))[None]
    cross = dot(whole[:, :quarter], whole, ((0,), (0,)))
    cross = jnp.concatenate([cross, cross], axis=1)
    cross = slice_at(cross, turn, width, 1)
    right_acc = STAT_DECAY * right_stat + cross[None]

    update = finish(key, flags, back)
    return (update, first_next, second_next, left_acc, right_acc)


def solution(mesh):
    placed = (
        P("grp", None, "own", None),
        P(),
        P(),
        P("own", "grp", None),
        P("own", "grp", None),
        P("own", "grp", None),
        P("own", "grp", None),
        P(None, "own", "grp"),
        P(None, "own", "grp"),
    )
    return jax.shard_map(
        on_device,
        mesh=mesh,
        in_specs=placed,
        out_specs=(
            P(None, "own", "grp"),
            P(None, "own", "grp"),
            P(None, "own", "grp"),
            P("own", "grp", None),
            P("own", "grp", None),
        ),
        check_vma=False,
    )
```

```python
import functools

import jax
import jax.numpy as jnp
from jax import lax
from jax.experimental import pallas as pl
from jax.experimental.pallas import tpu as pltpu
from jax.sharding import PartitionSpec as P

BETA_FIRST = 0.9
BETA_SECOND = 0.95
BIAS_FIRST = 1.0 - 0.9**10
BIAS_SECOND = 1.0 - 0.95**10
ADAM_EPS = 1e-08
STAT_DECAY = 0.95
NORM_EPS = 1e-06
F32 = jnp.float32
BF16 = jnp.bfloat16
ORDER = (
    33, 58, 20, 47, 9, 3, 13, 23, 32, 10, 21, 15, 57, 18, 60, 38,
    49, 11, 52, 31, 40, 34, 61, 55, 0, 27, 53, 46, 24, 2, 28, 54,
    1, 26, 5, 63, 8, 51, 12, 39, 16, 43, 4, 30, 56, 35, 44, 22,
    48, 59, 36, 14, 41, 50, 29, 7, 17, 42, 37, 62, 25, 19, 45, 6,
)
MIB = 1024 * 1024
VMEM = pltpu.VMEM
LONG = pl.CostEstimate(flops=2 * 10**11, bytes_accessed=10**9, transcendentals=0)


def shift(array, step):
    n = lax.axis_size("grp")
    return lax.ppermute(array, "grp", [(i, (i + step) % n) for i in range(n)])


def places_of(assign, n_own, per_owner, order):
    place = [order.index(slot) for slot in range(len(order))]
    key = assign % n_own * per_owner + assign // n_own
    return jnp.asarray(place, jnp.int32)[key]


def in_hbm(array):
    return pltpu.with_memory_space_constraint(array, pltpu.HBM)


def slice_at(array, start, size, axis):
    starts = [start if i == axis else 0 for i in range(array.ndim)]
    sizes = [size if i == axis else n for i, n in enumerate(array.shape)]
    return lax.dynamic_slice(array, starts, sizes, allow_negative_indices=False)


def dot(a, b, dims):
    return lax.dot_general(a, b, (dims, ((), ())), preferred_element_type=F32)


def inside(bounds, rows, cols):
    row, col = lax.axis_index("own") * rows, lax.axis_index("grp") * cols
    ok = (row < bounds[:, 2] - bounds[:, 0]) & (col < bounds[:, 3] - bounds[:, 1])
    return ok.astype(jnp.int32)


def add_kernel(up, far_up, down, far_down, up_out, down_out):
    up_out[...] = (up[...].astype(F32) + far_up[...].astype(F32)).astype(BF16)
    down_out[...] = (down[...].astype(F32) + far_down[...].astype(F32)).astype(BF16)


def add(*arrays):
    shape = jax.ShapeDtypeStruct(arrays[0].shape, BF16)
    return pl.pallas_call(
        add_kernel,
        out_shape=(shape, shape),
        in_specs=[pl.BlockSpec(memory_space=VMEM)] * 4,
        out_specs=(pl.BlockSpec(memory_space=VMEM),) * 2,
        compiler_params=pltpu.CompilerParams(vmem_limit_bytes=4 * MIB),
    )(*arrays)


def roots_kernel(left, right, up, down, own):
    _, units, _, cols = (1, *up.shape)
    rows = up.shape[1]

    def root(half, step):
        col = ((lax.axis_index("grp") + step) & 3) * cols
        col = pl.ds(pl.multiple_of(col, cols), cols)
        return right[0, pl.ds(half * rows, rows), col].astype(BF16)

    for half in range(2):
        own[half] = root(half, 0)
        up[9 + half] = root(half, 1)
        down[9 + half] = root(half, 3)
        for c in range(4):
            unit = left[0, pl.ds(half * rows, rows), pl.ds(c * cols, cols)].astype(BF16)
            up[5 * half + c] = unit
            down[5 - 5 * half + c] = unit
    up[4] = root(0, 2)
    down[4] = root(1, 2)


def root_pieces(left, right):
    _, rows, width = left.shape
    unit = (rows // 2, width // 4)
    return pl.pallas_call(
        roots_kernel,
        out_shape=(
            pltpu.HBM((11, *unit), BF16),
            pltpu.HBM((11, *unit), BF16),
            pltpu.HBM((2, *unit), BF16),
        ),
        grid=(1,),
        in_specs=[pl.BlockSpec(left.shape, lambda i: (0, 0, 0))] * 2,
        out_specs=tuple(pl.BlockSpec((n, *unit), lambda i: (0, 0, 0)) for n in (11, 11, 2)),
        compiler_params=pltpu.CompilerParams(vmem_limit_bytes=8 * MIB),
    )(in_hbm(left), in_hbm(right))


def gather_kernel(own, up_direct, down_direct, first, second, out, first_out, second_out):
    half = up_direct.shape[0]

    def step(i, carry):
        out[0, i] = own[i].astype(F32) + down_direct[i].astype(F32)
        out[1, i] = own[i + half].astype(F32) + up_direct[i].astype(F32)
        return carry

    lax.fori_loop(0, half, step, 0, unroll=4)
    first_out[...] = BETA_FIRST * first[...]
    second_out[...] = BETA_SECOND * second[...]


def gather(own, up_direct, down_direct, first, second):
    shape = jax.ShapeDtypeStruct((2, *up_direct.shape), F32)
    return pl.pallas_call(
        gather_kernel,
        out_shape=(shape,) * 3,
        in_specs=[pl.BlockSpec(memory_space=VMEM)] * 5,
        out_specs=(pl.BlockSpec(memory_space=VMEM),) * 3,
        compiler_params=pltpu.CompilerParams(vmem_limit_bytes=10 * MIB),
        cost_estimate=LONG,
    )(own, up_direct, down_direct, first.reshape(shape.shape), second.reshape(shape.shape))


def pack_kernel(
    key, flags, partial, up_sum, down_sum, first, second, out, first_out, second_out
):
    _, half, rows, cols = partial.shape
    count = first_out.shape[1]
    begin = pl.program_id(0) * count
    lanes = cols // 2

    def one(side, i, value):
        at = begin + i
        block = side * half + at
        keep = flags[block].astype(F32)
        grad = value * keep
        first_next = first[side, at] + (1.0 - BETA_FIRST) * grad
        second_next = second[side, at] + (1.0 - BETA_SECOND) * grad * grad
        first_out[side, i] = first_next
        second_out[side, i] = second_next
        root = second_next * lax.rsqrt(second_next)
        adam = first_next * pl.reciprocal(root + ADAM_EPS * BIAS_SECOND**0.5)
        square = adam * adam
        square = square[:, :lanes] + square[:, lanes:]
        square = (square[: rows // 2] + square[rows // 2 :]) * keep
        piece = jnp.concatenate([grad[:, :lanes], grad[:, lanes:], square], axis=0)
        out[key[block]] = piece.astype(BF16)

    def step(i, carry):
        at = begin + i
        one(0, i, partial[0, at] + up_sum[at].astype(F32))
        one(1, i, partial[1, at] + down_sum[at].astype(F32))
        return carry

    lax.fori_loop(0, count, step, 0, unroll=4)


def pack(key, flags, partial, up_sum, down_sum, first, second):
    _, half, rows, cols = partial.shape
    blocks, lanes = 2 * half, cols // 2
    steps = 2 if half >= 16 else 1
    moment = pl.BlockSpec((2, half // steps, rows, cols), lambda i, *_: (0, i, 0, 0))
    halves = pltpu.HBM((2, half, rows, cols), F32)
    piece = (blocks, 2 * rows + rows // 2, lanes)
    out, first_next, second_next = pl.pallas_call(
        pack_kernel,
        out_shape=(pltpu.HBM(piece, BF16), halves, halves),
        grid_spec=pltpu.PrefetchScalarGridSpec(
            num_scalar_prefetch=2,
            grid=(steps,),
            in_specs=[pl.BlockSpec(memory_space=VMEM)] * 5,
            out_specs=[pl.BlockSpec(piece, lambda i, *_: (0, 0, 0)), moment, moment],
        ),
        compiler_params=pltpu.CompilerParams(vmem_limit_bytes=16 * MIB),
    )(key, flags, partial, up_sum, down_sum, first, second)
    shape = (blocks, rows, cols)
    return out, first_next.reshape(shape), second_next.reshape(shape)


def relay_kernel(prev, following, up, down):
    units = up.shape[0]
    up[...] = prev[pl.ds(0, units)]
    down[...] = following[pl.ds(0, units)]


def relay(prev, following):
    shape = jax.ShapeDtypeStruct((5, *prev.shape[1:]), BF16)
    return pl.pallas_call(
        relay_kernel,
        out_shape=(shape, shape),
        in_specs=[pl.BlockSpec(memory_space=VMEM)] * 2,
        out_specs=(pl.BlockSpec(memory_space=VMEM),) * 2,
        compiler_params=pltpu.CompilerParams(vmem_limit_bytes=6 * MIB),
        cost_estimate=LONG,
    )(prev, following)


def unpack_kernel(order, owned, low, high, adam):
    half, rows, cols = low.shape
    total = jnp.zeros(adam.shape, F32)
    for i, place in enumerate(order):
        piece = owned[i]
        value = jnp.concatenate([piece[:rows], piece[rows : 2 * rows]], axis=1)
        if place < half:
            low[place] = value
        else:
            high[place - half] = value
        total += piece.astype(F32)[2 * rows :]
    adam[...] = total


def unpack(order, owned, rows):
    half = owned.shape[0] // 2
    shape = jax.ShapeDtypeStruct((half, rows, 2 * owned.shape[2]), BF16)
    return pl.pallas_call(
        functools.partial(unpack_kernel, order),
        out_shape=(shape, shape, jax.ShapeDtypeStruct((rows // 2, 128), F32)),
        in_specs=[pl.BlockSpec(memory_space=VMEM)],
        out_specs=(pl.BlockSpec(memory_space=VMEM),) * 3,
        compiler_params=pltpu.CompilerParams(vmem_limit_bytes=6 * MIB),
    )(owned)


def finish_kernel(key, flags, back, out):
    count, rows, cols = out.shape
    begin = pl.program_id(0) * count

    def step(i, carry):
        block = begin + i
        out[i] = jnp.where(flags[block] != 0, back[key[block]], jnp.zeros((), BF16))
        return carry

    lax.fori_loop(0, count, step, 0, unroll=8)


def finish(key, flags, back):
    blocks, rows, cols = back.shape
    steps = 2 if blocks >= 16 else 1
    return pl.pallas_call(
        finish_kernel,
        out_shape=jax.ShapeDtypeStruct(back.shape, BF16),
        grid_spec=pltpu.PrefetchScalarGridSpec(
            num_scalar_prefetch=2,
            grid=(steps,),
            in_specs=[pl.BlockSpec(memory_space=VMEM)],
            out_specs=pl.BlockSpec((blocks // steps, rows, cols), lambda i, *_: (i, 0, 0)),
        ),
        compiler_params=pltpu.CompilerParams(vmem_limit_bytes=6 * MIB),
    )(key, flags, back)


def precond_kernel(*refs):
    pieces, adam, sources, (out, norms) = refs[:8], refs[8], refs[9:15], refs[15:17]
    mixed, held, sems = refs[17], refs[18:24], refs[24]
    width, quarter = out.shape
    half = width // 2
    me = lax.axis_index("grp")
    n = width // quarter
    root, up, up_prev, down_next, up_far, down_far = held
    cuts = [(0, 0, 2), (2, 9, 2), (3, 9, 2), (4, 4, 1), (5, 4, 1)]
    cuts += [(1, 0, 9), (3, 0, 9), (4, 0, 4), (5, 0, 4), (2, 0, 9)]
    copies = []
    for i, (which, first, count) in enumerate(cuts):
        units = pl.ds(first, count)
        source, place = sources[which].at[units], held[which].at[units]
        copies.append(pltpu.make_async_copy(source, place, sems.at[i]))
    for copy in copies:
        copy.start()
    for copy in copies[:5]:
        copy.wait()
    right = jnp.concatenate(
        [
            root[0],
            root[1],
            down_next[9],
            down_next[10],
            up_far[4],
            down_far[4],
            up_prev[9],
            up_prev[10],
        ],
        axis=0,
    )
    for row in range(0, width, quarter):
        parts = [ref[pl.ds(row % half, quarter), :] for ref in pieces[row // half :: 2]]
        value = dot(jnp.concatenate(parts, axis=1), right, ((1,), (0,)))
        mixed[pl.ds(row, quarter), :] = value.astype(BF16)
    for copy in copies[5:]:
        copy.wait()
    square = jnp.zeros((8, quarter), F32)
    for step, (low, first), (high, second) in (
        (0, (up, 0), (up, 5)),
        (1, (down_next, 5), (down_next, 0)),
        (2, (up_far, 0), (down_far, 0)),
        (3, (up_prev, 0), (up_prev, 5)),
    ):
        units = [jnp.concatenate([low[first + c], high[second + c]], axis=0) for c in range(n)]
        value = dot(jnp.concatenate(units, axis=1), mixed[...], ((1,), (0,)))
        base = ((me + step) & (n - 1)) * quarter
        out[pl.ds(pl.multiple_of(base, quarter), quarter), :] = value
        square += jnp.sum((value * value).reshape(quarter // 8, 8, quarter), axis=0)
    norms[...] = jnp.zeros_like(norms)
    norms[0:1, :] = jnp.broadcast_to(jnp.sum(square), (1, 128))
    norms[1:2, :] = jnp.broadcast_to(jnp.sum(adam[...]), (1, 128))


def precondition(pieces, adam, sources):
    rows, quarter = pieces[0].shape
    operands = (*pieces, adam)
    return pl.pallas_call(
        precond_kernel,
        out_shape=(
            jax.ShapeDtypeStruct((2 * rows, quarter), F32),
            jax.ShapeDtypeStruct((8, 128), F32),
        ),
        in_specs=[pl.BlockSpec(memory_space=VMEM)] * len(operands)
        + [pl.BlockSpec(memory_space=pl.ANY)] * len(sources),
        out_specs=(pl.BlockSpec(memory_space=VMEM),) * 2,
        scratch_shapes=[
            VMEM((2 * rows, quarter), BF16),
            *[VMEM(source.shape, BF16) for source in sources],
            pltpu.SemaphoreType.DMA((10,)),
        ],
        compiler_params=pltpu.CompilerParams(vmem_limit_bytes=14 * MIB),
    )(*operands, *map(in_hbm, sources))


def graft_kernel(cells, order, precond, first, second, third, fourth, out):
    sums = first[...] + second[...] + third[...] + fourth[...]
    pre, adam = sums[0:1, :], sums[1:2, :]
    adam = adam * (BIAS_SECOND / (BIAS_FIRST * BIAS_FIRST))
    scale = -jnp.sqrt(adam / cells) / jnp.sqrt(pre / cells + NORM_EPS)
    _, rows, quarter = out.shape
    scale = jnp.concatenate([scale] * (quarter // 128), axis=1)
    for i, place in enumerate(order):
        out[i] = (scale * precond[pl.ds(place * rows, rows), :]).astype(BF16)


def graft(order, precond, norms):
    width, quarter = precond.shape
    shape = (len(order), width // len(order), quarter)
    small = pl.BlockSpec((8, 128), lambda i: (0, 0))
    return pl.pallas_call(
        functools.partial(graft_kernel, float(width * width), order),
        out_shape=pltpu.HBM(shape, BF16),
        grid=(1,),
        in_specs=[pl.BlockSpec((width, quarter), lambda i: (0, 0))] + [small] * 4,
        out_specs=pl.BlockSpec(shape, lambda i: (0, 0, 0)),
        compiler_params=pltpu.CompilerParams(vmem_limit_bytes=8 * MIB),
    )(precond, *norms)


def on_device(
    grad_parts,
    assign,
    block_bounds,
    left_root,
    right_root,
    left_stat,
    right_stat,
    first_moment,
    second_moment,
):
    n_own = lax.axis_size("own")
    n_grp = lax.axis_size("grp")
    grp_index = lax.axis_index("grp")
    total_blocks = assign.shape[0]
    per_owner = total_blocks // n_own
    shard_rows = grad_parts.shape[2]
    width = grad_parts.shape[3]
    quarter = width // n_grp
    half = total_blocks // 2
    starts = [((grp_index + step) & (n_grp - 1)) * quarter for step in range(4)]
    turn = ((n_grp - grp_index) & (n_grp - 1)) * quarter
    grad_parts, starts, turn = lax.optimization_barrier((grad_parts, starts, turn))

    def columns(array, step):
        return slice_at(array, starts[step], quarter, array.ndim - 1)

    part = grad_parts[0]
    order = ORDER if len(ORDER) == n_own else tuple(range(n_own))

    def exchange(array):
        groups = [list(order)]
        return lax.all_to_all(array, "own", 0, 0, axis_index_groups=groups, tiled=True)

    far = columns(part, 2)
    far_low, far_high = lax.optimization_barrier((far[:half], far[half:]))
    far_up = shift(far_low, 1)
    far_down = shift(far_high, -1)
    later, _, _ = lax.optimization_barrier((part, far_low, far_high))
    up, down = columns(later, 1), columns(later, 3)
    up_low, up_high, down_low, down_high = lax.optimization_barrier(
        (up[:half], up[half:], down[:half], down[half:])
    )
    up_direct = shift(up_high, 1)
    down_direct = shift(down_low, -1)
    up_sum, down_sum = add(up_low, far_up, down_high, far_down)
    up_sum, down_sum, left_root, right_root, later = lax.optimization_barrier(
        (up_sum, down_sum, left_root, right_root, part)
    )
    own = columns(later, 0)
    up_sum = shift(up_sum, 1)
    down_sum = shift(down_sum, -1)
    key = places_of(assign, n_own, per_owner, order)
    flags = inside(block_bounds, shard_rows, quarter)
    roots_up, roots_down, root_own = root_pieces(left_root, right_root)
    up_direct, down_direct, key, flags, roots_up, roots_down, root_own = lax.optimization_barrier(
        (up_direct, down_direct, key, flags, roots_up, roots_down, root_own)
    )
    partial, first, second = gather(own, up_direct, down_direct, first_moment, second_moment)

    roots_up, roots_down, up_sum, down_sum, partial = lax.optimization_barrier(
        (roots_up, roots_down, up_sum, down_sum, partial)
    )
    sorted_grad, first_next, second_next = pack(
        key, flags, partial, up_sum, down_sum, first, second
    )
    owned = exchange(sorted_grad)
    roots_prev = shift(roots_up, 1)
    roots_next = shift(roots_down, -1)
    onward = relay(roots_prev, roots_next)
    far_roots = [shift(onward[0], 1), shift(onward[1], -1)]
    roots = [root_own, roots_up, roots_prev, roots_next, *far_roots]

    owned, roots = lax.optimization_barrier((owned, roots))
    low, high, adam = unpack(order, owned, shard_rows)
    prev_low = shift(low, 1)
    next_high = shift(high, -1)
    prev_high = shift(high, 1)
    next_low = shift(low, -1)
    far_low = shift(prev_low, 1)
    far_high = shift(next_high, -1)
    pieces = [low, high, next_low, next_high, far_low, far_high, prev_low, prev_high]
    flat = [piece.reshape(-1, quarter) for piece in pieces]
    precond, norms = precondition(flat, adam, roots)
    norms = [norms] + [shift(norms, step) for step in (1, 2, 3)]
    grafted = graft(order, precond, norms)
    pieces, grafted = lax.optimization_barrier((pieces, grafted))
    back = exchange(grafted)

    whole = jnp.concatenate(
        [jnp.concatenate(pieces[i : i + 2]) for i in (0, 2, 4, 6)], axis=2
    ).reshape(width, width)
    rows = slice_at(whole, starts[0], quarter, 0)
    left_acc = STAT_DECAY * left_stat + dot(rows, whole, ((1,), (1,)))[None]
    cross = dot(whole[:, :quarter], whole, ((0,), (0,)))
    cross = jnp.concatenate([cross, cross], axis=1)
    cross = slice_at(cross, turn, width, 1)
    right_acc = STAT_DECAY * right_stat + cross[None]

    update = finish(key, flags, back)
    return (update, first_next, second_next, left_acc, right_acc)


def solution(mesh):
    placed = (
        P("grp", None, "own", None),
        P(),
        P(),
        P("own", "grp", None),
        P("own", "grp", None),
        P("own", "grp", None),
        P("own", "grp", None),
        P(None, "own", "grp"),
        P(None, "own", "grp"),
    )
    return jax.shard_map(
        on_device,
        mesh=mesh,
        in_specs=placed,
        out_specs=(
            P(None, "own", "grp"),
            P(None, "own", "grp"),
            P(None, "own", "grp"),
            P("own", "grp", None),
            P("own", "grp", None),
        ),
        check_vma=False,
    )
```
